256 devices in a mesh: wide: 64 (over z, x, core), rep: 4 (over y).
Axes of the slice: x: 4, y: 4, z: 8, core: 2. Of those that a mesh axis runs over, the one named last changes fastest.
Arguments:
- factor: float32 [32, 1024, 4096], P(None, 'wide'), may hold values from -0.09375 to 0.09375
- inverses: float32 [4, 1, 1024, 1024], P(None, None, 'wide'), as said below
- right_side: float32 [32, 1024, 512], P(None, 'wide', 'rep'), may hold values from -6 to 6
- obs_cells: int32 [4096], replicated, may hold values from 0 to 8388607
- noise: float32 [1024, 4, 8, 1024], P('wide', None, 'rep'), may hold values from -6 to 6
- spectrum: float32 [1024, 8, 1024], P(None, 'rep', 'wide'), may hold values from 0.25 to 4, as said below
Outputs:
- solved: float32 [32, 1024, 512], P(None, 'wide', 'rep')
- correction: float32 [1024, 4, 8, 1024], P('wide', None, 'rep')
The draws below stay inside these ranges and needn't reach their ends.
Inputs may be any that keep to these rules, and one draw needn't show every extreme that they name: `inverses`: each D_k is lower triangular. spectrum[x, y, z] equals spectrum[(1024 - x) % 1024, y, (1024 - z) % 1024].
All inputs are finite; a program needn't handle non-finite values.
Results may differ from the reference program's by a relative error of at most 0.0001.
Values sent between devices are 32-bit elements; how exact they have to be, the bound alone decides.
No kernel may reach another device: no remote copies, remote signals or barrier semaphores. Data moves between devices by JAX's collectives and lax.ppermute only.
A program may use at most 192 MiB of HBM per device.

```python
import math
import jax
import jax.numpy as jnp
from jax import lax

NB = 4
BS = 1024
S_DEV = 128
NX = 1024
NZ = 1024
YCH = 8
RB_ALL = 1024
PB = 1
NCOL = 4096
BLK_DEV = 32
OBS = 32768
S = 512
FIELDS = 4


def draw_inverses(key, part):
    key = jax.random.fold_in(key, 11)
    key_off, key_diag = jax.random.split(key)
    shape = (NB, PB, RB_ALL, BS)
    rows = (jnp.arange(PB)[:, None] * RB_ALL + jnp.arange(RB_ALL)[None, :])[None, :, :, None]
    cols = jnp.arange(BS)[None, None, None, :]
    off_part = jax.random.normal(key_off, shape, jnp.float32) * (0.7 / math.sqrt(BS))
    diag_part = jax.random.uniform(key_diag, shape, jnp.float32, 0.5, 1.5)
    zeros = jnp.zeros(shape, jnp.float32)
    return jnp.where(cols < rows, off_part, jnp.where(cols == rows, diag_part, zeros)).astype(jnp.float32)


def draw_spectrum(key, part):
    key = jax.random.fold_in(key, 23)
    shape = (NX, YCH, NZ)
    base = jnp.exp(jax.random.uniform(key, shape, jnp.float32, math.log(0.25), math.log(4.0)))
    mirror = jnp.roll(jnp.flip(base, (0, 2)), (1, 1), axis=(0, 2))
    return jnp.sqrt(base * mirror).astype(jnp.float32)


def touch_ends(array, key, low, top_value):
    place = [jax.random.randint(jax.random.fold_in(key, axis), (), 0, length) for axis, length in enumerate(array.shape)]
    main_axis = array.shape.index(max(array.shape))
    beside = place[:main_axis] + [(place[main_axis] + 1) % array.shape[main_axis]] + place[main_axis + 1:]
    return array.at[tuple(place)].set(low).at[tuple(beside)].set(top_value)


def levels(rng, extent, cuts, low, high):
    loudness, own = 1.0, jax.random.fold_in(rng, 6)
    for axis_at, blocks in cuts:
        heights = jnp.exp(jax.random.uniform(jax.random.fold_in(own, axis_at), (blocks,), jnp.float32, low / len(cuts), high / len(cuts)))
        loudness = loudness * jnp.repeat(heights, extent[axis_at] // blocks).reshape([-1 if axis == axis_at else 1 for axis in range(len(extent))])
    return loudness


def centred(stream_key, shape, width, reach, cuts=(), held_as=jnp.bfloat16):
    result = width * jax.random.normal(stream_key, shape, jnp.float32)
    if cuts:
        result = result * levels(stream_key, shape, cuts, -0.22, 0.18)
    return jnp.clip(result, -reach, reach).astype(held_as)


def setup_inputs(seed: int = 0) -> dict:
    keys = jax.random.split(jax.random.key(seed), 7)
    factor = centred(keys[0], (BLK_DEV, RB_ALL, NCOL), NCOL ** -0.5, 0.09375, ((1, 64),), jnp.float32)
    inverses = draw_inverses(jax.random.fold_in(keys[6], 71), 0)
    right_side = centred(keys[2], (BLK_DEV, RB_ALL, S), 1.0, 6.0, ((1, 64), (2, 4)), jnp.float32)
    obs_cells = touch_ends(jax.random.randint(keys[3], (NCOL,), 0, NX * YCH * NZ), jax.random.fold_in(keys[3], 1), 0, (NX * YCH * NZ) - 1).astype(jnp.int32)
    noise = centred(keys[4], (NX, FIELDS, YCH, NZ), 1.0, 6.0, ((0, 64), (2, 4)), jnp.float32)
    spectrum = draw_spectrum(jax.random.fold_in(keys[6], 71), 0)
    return {"factor": factor, "inverses": inverses, "right_side": right_side, "obs_cells": obs_cells, "noise": noise, "spectrum": spectrum}


def reference(factor, inverses, right_side, obs_cells, noise, spectrum):
    precise = lax.Precision.HIGHEST
    lower = factor.reshape(OBS, NCOL)
    work = right_side.reshape(OBS, S)
    blocks = inverses.reshape(NB, BS, BS)
    panels = []
    for panel_index in range(NB):
        top_row = panel_index * BS
        end_row = top_row + BS
        unknowns = jnp.dot(blocks[panel_index], work[top_row:end_row], precision=precise, preferred_element_type=jnp.float32)
        below = work[end_row:] - jnp.dot(lower[end_row:, top_row:end_row], unknowns, precision=precise, preferred_element_type=jnp.float32)
        work = jnp.concatenate([work[:top_row], unknowns, below], axis=0)
        panels.append(unknowns)
    solved = work.reshape(BLK_DEV, RB_ALL, S)
    weights = jnp.concatenate(panels, axis=0)[:, ::S_DEV]
    x_cell = obs_cells // (YCH * NZ)
    y_cell = (obs_cells // NZ) % YCH
    z_cell = obs_cells % NZ
    field = noise.at[x_cell, :, y_cell, z_cell].add(weights)
    spectral = jnp.fft.fftn(field, axes=(0, 3))
    spectral = spectral * spectrum[:, None, :, :]
    correction = jnp.real(jnp.fft.ifftn(spectral, axes=(0, 3))).astype(field.dtype)
    return solved, correction
```

```python
import functools
import math

import jax
import jax.numpy as jnp
import numpy as np
from jax import lax
from jax.experimental import pallas as pl
from jax.experimental.pallas import tpu as pltpu
from jax.sharding import Mesh, PartitionSpec as P

F32 = jnp.float32
BF16 = jnp.bfloat16
WIDE = ("z", "x", "core")
LENGTH = 1024
COLS = 24
NN = (((1,), (0,)), ((), ()))
NT = (((1,), (1,)), ((), ()))
LIMIT = pltpu.CompilerParams(vmem_limit_bytes=56 * 1024 * 1024)


def halves(table):
    high = table.astype(np.float32).astype(jnp.bfloat16)
    low = (table - high.astype(np.float64)).astype(np.float32).astype(jnp.bfloat16)
    return (np.asarray(high), np.asarray(low))


def z_frequencies(owner, xp):
    step = xp.arange(16) % 8
    part = xp.arange(16) // 8
    freq = 16 * owner + step + xp.where(owner >= 32, 1, 0)
    lone = (owner == 0) & (step == 0) & (part == 1)
    return (xp.where(lone, 512, freq), xp.where(lone, 0, 256 * part))


def z_table():
    rows = []
    cells = np.arange(LENGTH)
    for owner in range(64):
        freq, phase = z_frequencies(np.int64(owner), np)
        turn = (freq[:, None] * cells[None, :] + phase[:, None]) % LENGTH
        rows.append(np.cos(2.0 * np.pi * turn / LENGTH))
    return np.concatenate(rows)


def x_table():
    cells = np.arange(LENGTH)
    freq = np.concatenate([np.arange(512), np.arange(512)])
    phase = np.repeat([0, 256], 512)
    freq[512], phase[512] = 512, 0
    turn = (freq[:, None] * cells[None, :] + phase[:, None]) % LENGTH
    return np.cos(2.0 * np.pi * turn / LENGTH)


def split(value):
    high = value.astype(BF16)
    low = (value - high.astype(F32)).astype(BF16)
    return (high, low)


def dot(left, right, dims):
    return lax.dot_general(left, right, dims, preferred_element_type=F32)


def dot_nt(left, right):
    left_high, left_low = split(left)
    right_high, right_low = split(right)
    rows = left.shape[0]
    both = dot(jnp.concatenate([left_high, left_low]), right_high, NT)
    return both[:rows] + both[rows:] + dot(left_high, right_low, NT)


def table_nn(high, low, value):
    value_high, value_low = split(value)
    cols = value.shape[1]
    both = dot(high, jnp.concatenate([value_high, value_low], axis=1), NN)
    return both[:, :cols] + both[:, cols:] + dot(low, value_high, NN)


def swap_groups(value):
    row = lax.broadcasted_iota(jnp.int32, value.shape, 0)
    lane = lax.broadcasted_iota(jnp.int32, value.shape, 1)
    for bit in range(4):
        step = 1 << bit
        row_bit = (row >> bit) & 1
        lane_bit = (lane >> (3 + bit)) & 1
        up = pltpu.roll(pltpu.roll(value, LENGTH - step, 0), 8 * step, 1)
        down = pltpu.roll(pltpu.roll(value, step, 0), 128 - 8 * step, 1)
        value = jnp.where(row_bit == lane_bit, value, jnp.where(lane_bit == 1, up, down))
    return value


def pack_kernel(inverse_ref, noise_ref, high_ref, low_ref, out_ref):
    lane = lax.broadcasted_iota(jnp.int32, (64, 128), 1) // 16
    for r in range(8):
        total = jnp.zeros((64, 128), F32)
        for z in range(8):
            piece = inverse_ref[:, 128 * z : 128 * z + 128]
            piece = pltpu.roll(piece, (16 * (z - r)) % 128, 1) if z != r else piece
            total = jnp.where(lane == z, piece, total)
        for z in range(8):
            out_ref[8 * z + r, 0:64, :] = total
    noise_high, noise_low = split(noise_ref[...])
    both = dot(high_ref[...], jnp.concatenate([noise_high, noise_low]), NT)
    slots = both[:, :128] + both[:, 128:] + dot(low_ref[...], noise_high, NT)
    out_ref[:, 64:80, :] = slots.reshape(64, 16, 128)


def first_kernel(start_ref, inverse_ref, out_ref):
    out_ref[...] = dot_nt(start_ref[0], inverse_ref[...].reshape(LENGTH, 128))


def step_kernel(panel, *refs):
    parts, rest = refs[:4], refs[4:]
    start_ref, inverse_ref = rest[:2]
    factor_refs = rest[2 : 2 + panel]
    older_refs = rest[2 + panel : 1 + 2 * panel]
    out_ref, unknown_ref = rest[1 + 2 * panel :]
    unknown = (parts[0][...] + parts[1][...]) + (parts[2][...] + parts[3][...])
    unknown_ref[...] = unknown
    work = start_ref[0]
    for ref, factor_ref in zip(older_refs, factor_refs):
        work = work - dot_nt(ref[...], factor_ref[...].reshape(128, LENGTH))
    work = work - dot_nt(unknown, factor_refs[-1][...].reshape(128, LENGTH))
    out_ref[...] = dot_nt(work, inverse_ref[...].reshape(LENGTH, 128))


def spectrum_kernel(index_ref, spectrum_ref, extra_ref, even_ref, odd_ref):
    owner = index_ref[0]
    row = lax.broadcasted_iota(jnp.int32, (32, 128), 0)
    lane = lax.broadcasted_iota(jnp.int32, (32, 128), 1)
    lone = (owner == 0) & (lane // 8 == 8)
    same_y = row // 16 == lane % 2
    same_z = row % 16 == (lane // 8) % 8 + jnp.where(owner >= 32, 1, 0)
    pick = jnp.where(same_y & same_z & jnp.logical_not(lone), 1.0, 0.0).astype(BF16)
    extra_pick = jnp.where(lone & (row == lane % 2), 1.0, 0.0)[:8].astype(BF16)

    def exact(value, choose):
        high = value.astype(BF16)
        rest = value - high.astype(F32)
        middle = rest.astype(BF16)
        low = (rest - middle.astype(F32)).astype(BF16)
        return choose(high) + (choose(middle) + choose(low))

    wanted = exact(spectrum_ref[...], lambda part: dot(part, pick, NN))
    wanted = wanted + exact(
        jnp.transpose(extra_ref[...]), lambda part: dot(part, extra_pick, NN)
    )
    at_row = lax.broadcasted_iota(jnp.int32, (512, 512), 0)
    at_col = lax.broadcasted_iota(jnp.int32, (512, 512), 1)
    mirror = jnp.where(at_row + at_col == 512, 1.0, 0.0).astype(BF16)
    plus = wanted[:512]
    upper = wanted[512:]
    minus = exact(upper, lambda part: dot(mirror, part, NN))
    first = lax.broadcasted_iota(jnp.int32, (512, 128), 0) == 0
    minus = jnp.where(first, plus, minus)
    lanes = lax.broadcasted_iota(jnp.int32, (512, 128), 1)
    alone = (owner == 0) & ((lanes // 8) % 8 == 0)
    scale = jnp.where(first, 1.0, 2.0) * jnp.where(alone, 1.0, 2.0) / (LENGTH * LENGTH)
    even = (plus + minus) * (0.5 * scale)
    even_ref[0:512] = even
    even_ref[512:1024] = jnp.where(first, upper * scale, even)
    odd = (plus - minus) * (0.5 * scale)
    odd_ref[...] = jnp.where(lanes < 64, -odd, odd)


def add_weights(pencil, cell_ref, wave_ref, plane_ref, weights):
    doubled = jnp.concatenate(
        [weights[g : g + 1] * plane_ref[y : y + 1] for g in range(4) for y in range(2)]
    )
    waves = (wave_ref[...][:, None, :] * doubled[None]).reshape(128, LENGTH)
    cells = lax.broadcasted_iota(jnp.int32, (LENGTH, LENGTH), 0)
    chosen = jnp.where(cells == cell_ref[...], 1.0, 0.0).astype(BF16)
    high, low = split(waves)
    both = dot(chosen, jnp.concatenate([high, low]), NT)
    return pencil + both[:, :128] + both[:, 128:]


def open_kernel(slab_ref, cell_ref, wave_ref, plane_ref, unknown_ref, out_ref):
    pencil = swap_groups(slab_ref[...].reshape(LENGTH, 128))
    out_ref[...] = add_weights(pencil, cell_ref, wave_ref, plane_ref, unknown_ref[16:20])


def add_kernel(pencil_ref, cell_ref, wave_ref, plane_ref, unknown_ref, out_ref):
    out_ref[...] = add_weights(
        pencil_ref[...], cell_ref, wave_ref, plane_ref, unknown_ref[16:20]
    )


def filter_kernel(
    pencil_ref, cell_ref, wave_ref, plane_ref, a_ref, b_ref, c_ref, d_ref,
    high_ref, low_ref, back_high_ref, back_low_ref, even_ref, odd_ref, out_ref,
):
    weights = (a_ref[16:20] + b_ref[16:20]) + (c_ref[16:20] + d_ref[16:20])
    pencil = add_weights(pencil_ref[...], cell_ref, wave_ref, plane_ref, weights)
    freq = table_nn(high_ref[...], low_ref[...], pencil)
    real, imag = freq[:512], freq[512:]
    odd = odd_ref[...]
    real_out = even_ref[0:512] * real + odd * pltpu.roll(imag, 64, 1)
    imag_out = even_ref[512:1024] * imag - odd * pltpu.roll(real, 64, 1)
    back = table_nn(
        back_high_ref[...], back_low_ref[...], jnp.concatenate([real_out, imag_out])
    )
    out_ref[...] = swap_groups(back).reshape(64, 16, 128)


def close_kernel(slots_ref, high_ref, low_ref, out_ref):
    rows = jnp.transpose(slots_ref[...].reshape(LENGTH, 128))
    rows_high, rows_low = split(rows)
    both = dot(jnp.concatenate([rows_high, rows_low]), high_ref[...], NN)
    out_ref[...] = both[:128] + both[128:] + dot(rows_high, low_ref[...], NN)


def update_kernel(first_panel, index_ref, base_ref, factor_ref, unknown_ref, out_ref):
    block = pl.program_id(0)
    own = index_ref[0] * 16
    row = lax.broadcasted_iota(jnp.int32, (128, LENGTH), 0) + block * 128
    col = lax.broadcasted_iota(jnp.int32, (128, LENGTH), 1)
    base = base_ref[...].reshape(128, 128)
    if first_panel == 0:
        base_row = lax.broadcasted_iota(jnp.int32, (128, 128), 0) + block * 128
        base = jnp.where(base_row < 64, 0.0, base)
    for step in range(2):
        panel = first_panel + step
        rows = factor_ref[:, :, LENGTH * step : LENGTH * (step + 1)].reshape(128, LENGTH)
        mine = (row // 16 == panel) & (col == own + row % 16)
        rows = jnp.where(row < 64, jnp.where(mine, -1.0, 0.0), rows)
        unknown = unknown_ref[:, 16 * step : 16 * step + 16, :].reshape(128, LENGTH)
        base = base - dot_nt(rows, unknown)
    out_ref[...] = base.reshape(8, 16, 128)


def spec(*shape):
    return pl.BlockSpec(shape, lambda *_: (0,) * len(shape))


def block_at(shape, place):
    return pl.BlockSpec(shape, lambda *_: place)


def cost(flops, moved):
    return pl.CostEstimate(flops=flops, bytes_accessed=moved, transcendentals=0)


def shape_of(*shape):
    return jax.ShapeDtypeStruct(shape, F32)


def call(body, name, in_specs, out_specs, out_shape, flops, moved):
    return pl.pallas_call(
        body,
        grid=(1,),
        in_specs=in_specs,
        out_specs=out_specs,
        out_shape=out_shape,
        compiler_params=LIMIT,
        cost_estimate=cost(flops, moved),
        name=name,
    )


def ring(size, step):
    return [(place, (place + step) % size) for place in range(size)]


def share(partial):
    total = partial + lax.ppermute(partial, "core", ring(2, 1))
    return [total] + [lax.ppermute(total, "x", ring(4, step)) for step in (1, 2, 3)]


def update(first_panel, index, base, factor, unknowns):
    return pl.pallas_call(
        functools.partial(update_kernel, first_panel),
        grid=(4,),
        in_specs=[
            pl.BlockSpec(memory_space=pltpu.SMEM),
            pl.BlockSpec((8, 16, 128), lambda i: (i, 0, 0)),
            pl.BlockSpec((8, 16, 2 * LENGTH), lambda i: (i, 0, first_panel // 2)),
            spec(8, 32, LENGTH),
        ],
        out_specs=pl.BlockSpec((8, 16, 128), lambda i: (i, 0, 0)),
        out_shape=shape_of(32, 16, 128),
        compiler_params=LIMIT,
        cost_estimate=cost(3 * 2 * 512 * 2048 * 128, 5_500_000),
        name="update",
    )(index, base, factor, unknowns)


def per_device(factor, inverses, right_side, obs_cells, noise, spectrum):
    z_high, z_low = (jnp.asarray(t) for t in halves(z_table()))
    x_high, x_low = (jnp.asarray(t) for t in halves(x_table()))
    back_high, back_low = (jnp.asarray(t) for t in halves(x_table().T))
    wide = lax.axis_index(WIDE).astype(jnp.int32)
    index = wide.reshape(1)

    lower = jnp.concatenate(
        [
            factor[k, :, LENGTH * j : LENGTH * (j + 1)]
            for k in range(1, 4)
            for j in range(k)
        ]
    )
    lower = lax.all_gather(lower, "z")

    packed = call(
        pack_kernel,
        "pack",
        [spec(64, LENGTH), spec(128, LENGTH)] + [spec(LENGTH, LENGTH)] * 2,
        spec(64, 80, 128),
        shape_of(64, 80, 128),
        3 * 2 * 128 * LENGTH * LENGTH,
        8_000_000,
    )(inverses.reshape(64, LENGTH), noise.reshape(128, LENGTH), z_high, z_low)
    packed = lax.all_to_all(packed, WIDE, 0, 0)

    sides = right_side[:4].reshape(64, 128).T
    weight_side = lax.all_to_all(
        jnp.broadcast_to(sides[None, 0:1], (4, 1, 64)), "y", 0, 0
    ).reshape(4, 64)
    sides = jnp.concatenate(
        [
            sides.reshape(8, 16, 64),
            jnp.broadcast_to(weight_side[None], (8, 4, 64)),
            jnp.zeros((8, 4, 64), F32),
        ],
        axis=1,
    )
    sides = lax.all_to_all(sides, "z", 0, 0)
    sides = sides.reshape(8, COLS, 4, 16).transpose(2, 1, 0, 3).reshape(4, COLS, 128)

    cell_x = (obs_cells // (8 * LENGTH)).reshape(1, 4096)
    plane = obs_cells // LENGTH % 8 - 2 * lax.axis_index("y")
    planes = jnp.stack([plane == 0, plane == 1]).astype(F32)
    freq, phase = z_frequencies(wide, jnp)
    turn = (freq[:, None] * (obs_cells % LENGTH)[None, :] + phase[:, None]) % LENGTH
    waves = jnp.cos(turn.astype(F32) * (2.0 * math.pi / LENGTH))

    extra = lax.ppermute(spectrum[:, :, 0].T, WIDE, [(32, 0)])
    extra = jnp.concatenate([extra, jnp.zeros((6, LENGTH), F32)])
    even, odd = call(
        spectrum_kernel,
        "spectrum",
        [pl.BlockSpec(memory_space=pltpu.SMEM), spec(LENGTH, 32), spec(8, LENGTH)],
        [spec(LENGTH, 128), spec(512, 128)],
        [shape_of(LENGTH, 128), shape_of(512, 128)],
        300_000_000,
        1_500_000,
    )(index, spectrum.reshape(LENGTH, 32), extra)

    obs_specs = lambda k: [
        block_at((1, LENGTH), (0, k)),
        block_at((16, LENGTH), (0, k)),
        block_at((2, LENGTH), (0, k)),
    ]

    partial = call(
        first_kernel,
        "first",
        [spec(1, COLS, 128), spec(64, 16, 128)],
        spec(COLS, LENGTH),
        shape_of(COLS, LENGTH),
        20_000_000,
        700_000,
    )(sides, packed)
    parts = share(partial)
    unknowns = []
    halves_done = []
    pencil = None
    for panel in range(1, 4):
        first_block = panel * (panel - 1) // 2
        partial, unknown = call(
            functools.partial(step_kernel, panel),
            f"step{panel}",
            [spec(COLS, LENGTH)] * 4
            + [
                block_at((1, COLS, 128), (panel, 0, 0)),
                block_at((64, 16, 128), (0, panel, 0)),
            ]
            + [block_at((8, 16, LENGTH), (0, first_block + j, 0)) for j in range(panel)]
            + [spec(COLS, LENGTH)] * (panel - 1),
            [spec(COLS, LENGTH)] * 2,
            [shape_of(COLS, LENGTH)] * 2,
            40_000_000,
            1_500_000,
        )(*parts, sides, packed, *([lower] * panel), *unknowns)
        unknowns.append(unknown)
        parts = share(partial)
        body = open_kernel if panel == 1 else add_kernel
        start = packed if panel == 1 else pencil
        start_spec = block_at((64, 16, 128), (0, 4, 0)) if panel == 1 else spec(LENGTH, 128)
        pencil = call(
            body,
            f"pencil{panel}",
            [start_spec] + obs_specs(panel - 1) + [spec(COLS, LENGTH)],
            spec(LENGTH, 128),
            shape_of(LENGTH, 128),
            2 * 2 * 128 * LENGTH * LENGTH,
            1_500_000,
        )(start, cell_x, waves, planes, unknown)
        if panel == 2:
            gathered = lax.all_gather(
                jnp.concatenate([unknowns[0][:16], unknowns[1][:16]]), "z"
            )
            halves_done = update(0, index, right_side, factor, gathered)

    slots = call(
        filter_kernel,
        "filter",
        [spec(LENGTH, 128)]
        + obs_specs(3)
        + [spec(COLS, LENGTH)] * 4
        + [spec(LENGTH, LENGTH)] * 4
        + [spec(LENGTH, 128), spec(512, 128)],
        spec(64, 16, 128),
        shape_of(64, 16, 128),
        8 * 2 * 128 * LENGTH * LENGTH,
        11_000_000,
    )(pencil, cell_x, waves, planes, *parts, x_high, x_low, back_high, back_low, even, odd)
    slots = lax.all_to_all(slots, WIDE, 0, 0)

    last = (parts[0] + parts[1]) + (parts[2] + parts[3])
    gathered = lax.all_gather(jnp.concatenate([unknowns[2][:16], last[:16]]), "z")
    solved = update(2, index, halves_done, factor, gathered)

    correction = call(
        close_kernel,
        "close",
        [spec(64, 16, 128)] + [spec(LENGTH, LENGTH)] * 2,
        spec(128, LENGTH),
        shape_of(128, LENGTH),
        3 * 2 * 128 * LENGTH * LENGTH,
        5_500_000,
    )(slots, z_high, z_low)
    return (solved, correction.reshape(16, 4, 2, LENGTH))


def solution(mesh):
    grid = Mesh(mesh.devices.reshape(8, 4, 2, 4), ("z", "x", "core", "y"))
    return jax.shard_map(
        per_device,
        mesh=grid,
        in_specs=(
            P(None, WIDE, None),
            P(None, None, WIDE, None),
            P(None, WIDE, "y"),
            P(),
            P(WIDE, None, "y", None),
            P(None, "y", WIDE),
        ),
        out_specs=(P(None, WIDE, "y"), P(WIDE, None, "y", None)),
        check_vma=False,
    )
```

```python
import functools
import math

import jax
import jax.numpy as jnp
import numpy as np
from jax import lax
from jax.experimental import pallas as pl
from jax.experimental.pallas import tpu as pltpu
from jax.sharding import Mesh, PartitionSpec as P

F32 = jnp.float32
BF16 = jnp.bfloat16
WIDE = ("z", "x", "core")
LENGTH = 1024
COLS = 24
NN = (((1,), (0,)), ((), ()))
NT = (((1,), (1,)), ((), ()))
LIMIT = pltpu.CompilerParams(vmem_limit_bytes=56 * 1024 * 1024)


def halves(table):
    high = table.astype(np.float32).astype(jnp.bfloat16)
    low = (table - high.astype(np.float64)).astype(np.float32).astype(jnp.bfloat16)
    return (np.asarray(high), np.asarray(low))


def z_frequencies(owner, xp):
    step = xp.arange(16) % 8
    part = xp.arange(16) // 8
    freq = 16 * owner + step + xp.where(owner >= 32, 1, 0)
    lone = (owner == 0) & (step == 0) & (part == 1)
    return (xp.where(lone, 512, freq), xp.where(lone, 0, 256 * part))


def z_table():
    rows = []
    cells = np.arange(LENGTH)
    for owner in range(64):
        freq, phase = z_frequencies(np.int64(owner), np)
        turn = (freq[:, None] * cells[None, :] + phase[:, None]) % LENGTH
        rows.append(np.cos(2.0 * np.pi * turn / LENGTH))
    return np.concatenate(rows)


def x_table():
    cells = np.arange(LENGTH)
    freq = np.concatenate([np.arange(512), np.arange(512)])
    phase = np.repeat([0, 256], 512)
    freq[512], phase[512] = 512, 0
    turn = (freq[:, None] * cells[None, :] + phase[:, None]) % LENGTH
    return np.cos(2.0 * np.pi * turn / LENGTH)


def split(value):
    high = value.astype(BF16)
    low = (value - high.astype(F32)).astype(BF16)
    return (high, low)


def dot(left, right, dims):
    return lax.dot_general(left, right, dims, preferred_element_type=F32)


def dot_nt(left, right):
    left_high, left_low = split(left)
    right_high, right_low = split(right)
    rows = left.shape[0]
    both = dot(jnp.concatenate([left_high, left_low]), right_high, NT)
    return both[:rows] + both[rows:] + dot(left_high, right_low, NT)


def table_nn(high, low, value):
    value_high, value_low = split(value)
    cols = value.shape[1]
    both = dot(high, jnp.concatenate([value_high, value_low], axis=1), NN)
    return both[:, :cols] + both[:, cols:] + dot(low, value_high, NN)


def swap_groups(value):
    row = lax.broadcasted_iota(jnp.int32, value.shape, 0)
    lane = lax.broadcasted_iota(jnp.int32, value.shape, 1)
    for bit in range(4):
        step = 1 << bit
        row_bit = (row >> bit) & 1
        lane_bit = (lane >> (3 + bit)) & 1
        up = pltpu.roll(pltpu.roll(value, LENGTH - step, 0), 8 * step, 1)
        down = pltpu.roll(pltpu.roll(value, step, 0), 128 - 8 * step, 1)
        value = jnp.where(row_bit == lane_bit, value, jnp.where(lane_bit == 1, up, down))
    return value


def columns_kernel(inverse_ref, right_ref, out_ref, side_ref):
    side_ref[...] = right_ref[...].reshape(64, 128)
    lane = lax.broadcasted_iota(jnp.int32, (64, 128), 1) // 16
    for r in range(8):
        total = jnp.zeros((64, 128), F32)
        for z in range(8):
            piece = inverse_ref[:, 128 * z : 128 * z + 128]
            piece = pltpu.roll(piece, (16 * (z - r)) % 128, 1) if z != r else piece
            total = jnp.where(lane == z, piece, total)
        out_ref[r] = total


def noise_kernel(noise_ref, high_ref, low_ref, out_ref):
    noise_high, noise_low = split(noise_ref[...])
    both = dot(high_ref[...], jnp.concatenate([noise_high, noise_low]), NT)
    slots = both[:, :128] + both[:, 128:] + dot(low_ref[...], noise_high, NT)
    out_ref[...] = slots.reshape(16, 16, 128)


def bundle_kernel(
    index_ref, columns_ref, one_ref, two_ref, three_ref, *refs
):
    side_refs, (near_ref, far_ref) = refs[:4], refs[4:]
    near_ref[:, 0:32, :] = columns_ref[:, 0:32, :]
    far_ref[:, 0:32, :] = columns_ref[:, 32:64, :]
    for t in range(8):
        lanes = lambda j: pl.ds(LENGTH * j + 128 * t, 128)
        near_ref[t, 32:48, :] = one_ref[0, :, lanes(0)]
        near_ref[t, 48:64, :] = two_ref[0, :, lanes(0)]
        far_ref[t, 32:48, :] = two_ref[0, :, lanes(1)]
        for j in range(3):
            far_ref[t, 48 + 16 * j : 64 + 16 * j, :] = three_ref[0, :, lanes(j)]
    near_ref[:, 64:72, :] = side_refs[0][...].reshape(8, 8, 128)
    lane = lax.broadcasted_iota(jnp.int32, (64, 128), 1)
    weights = jnp.zeros((64, 128), F32)
    for step, ref in enumerate(side_refs):
        y = lax.rem(index_ref[1] + 4 - step, 4)
        weights = jnp.where(lane == y, ref[:, 0:1], weights)
    near_ref[:, 72:80, :] = weights.reshape(8, 8, 128)


def source_of(index_ref, step):
    return lax.rem(index_ref[0] // 8 + 8 - step, 8)


def spread(work, index_ref, piece_refs, out_ref):
    high, low = split(work)
    both = jnp.concatenate([high, low])
    for step, ref in enumerate(piece_refs):
        rows_high, rows_low = split(ref[...].reshape(128, 128))
        wide = dot(both, rows_high, NT)
        start = pl.multiple_of(source_of(index_ref, step) * 128, 128)
        out_ref[:, pl.ds(start, 128)] = (
            wide[:COLS] + wide[COLS:] + dot(high, rows_low, NT)
        )


def take_rows(unknown, index_ref, piece_refs, high_ref, low_ref):
    for step, ref in enumerate(piece_refs):
        rows = jnp.concatenate([ref[t] for t in range(8)], axis=1)
        start = pl.multiple_of(source_of(index_ref, step) * 16, 16)
        rows_high, rows_low = split(rows)
        high_ref[pl.ds(start, 16), :] = rows_high
        low_ref[pl.ds(start, 16), :] = rows_low
    high, low = split(unknown)
    wide = dot(jnp.concatenate([high, low]), high_ref[...], NT)
    return wide[:COLS] + wide[COLS:] + dot(high, low_ref[...], NT)


def first_kernel(index_ref, *refs):
    out_ref, side_ref, rows_ref = refs[16:]
    lane = lax.broadcasted_iota(jnp.int32, (64, 128), 1)
    z = index_ref[0] // 8
    for step, ref in enumerate(refs[8:16]):
        own = pltpu.roll(ref[:, 0:8, :].reshape(64, 128), lax.rem(128 - 16 * z, 128), 1)
        weights = pltpu.roll(ref[:, 8:16, :].reshape(64, 128), 16, 1)
        rows = jnp.where(lane < 16, own, jnp.where(lane < 20, weights, 0.0))
        start = pl.multiple_of(source_of(index_ref, step) * 16, 16)
        for k in range(4):
            rows_ref[k, pl.ds(start, 16), :] = rows[16 * k : 16 * k + 16]
    for k in range(4):
        side_ref[k] = jnp.transpose(rows_ref[k])[:COLS]
    spread(side_ref[0], index_ref, refs[:8], out_ref)


def step_kernel(index_ref, start_ref, a_ref, b_ref, c_ref, d_ref, *refs):
    factor_refs, inverse_refs = refs[:8], refs[8:16]
    out_ref, unknown_ref, high_ref, low_ref = refs[16:]
    unknown = (a_ref[...] + b_ref[...]) + (c_ref[...] + d_ref[...])
    unknown_ref[...] = unknown
    work = start_ref[0] - take_rows(unknown, index_ref, factor_refs, high_ref, low_ref)
    spread(work, index_ref, inverse_refs, out_ref)


def spectrum_kernel(index_ref, spectrum_ref, extra_ref, even_ref, odd_ref):
    owner = index_ref[0]
    row = lax.broadcasted_iota(jnp.int32, (32, 128), 0)
    lane = lax.broadcasted_iota(jnp.int32, (32, 128), 1)
    lone = (owner == 0) & (lane // 8 == 8)
    same_y = row // 16 == lane % 2
    same_z = row % 16 == (lane // 8) % 8 + jnp.where(owner >= 32, 1, 0)
    pick = jnp.where(same_y & same_z & jnp.logical_not(lone), 1.0, 0.0).astype(BF16)
    extra_pick = jnp.where(lone & (row == lane % 2), 1.0, 0.0)[:8].astype(BF16)

    def exact(value, choose):
        high = value.astype(BF16)
        rest = value - high.astype(F32)
        middle = rest.astype(BF16)
        low = (rest - middle.astype(F32)).astype(BF16)
        return choose(high) + (choose(middle) + choose(low))

    wanted = exact(spectrum_ref[...], lambda part: dot(part, pick, NN))
    wanted = wanted + exact(
        jnp.transpose(extra_ref[...]), lambda part: dot(part, extra_pick, NN)
    )
    at_row = lax.broadcasted_iota(jnp.int32, (512, 512), 0)
    at_col = lax.broadcasted_iota(jnp.int32, (512, 512), 1)
    mirror = jnp.where(at_row + at_col == 512, 1.0, 0.0).astype(BF16)
    plus = wanted[:512]
    upper = wanted[512:]
    minus = exact(upper, lambda part: dot(mirror, part, NN))
    first = lax.broadcasted_iota(jnp.int32, (512, 128), 0) == 0
    minus = jnp.where(first, plus, minus)
    lanes = lax.broadcasted_iota(jnp.int32, (512, 128), 1)
    alone = (owner == 0) & ((lanes // 8) % 8 == 0)
    scale = jnp.where(first, 1.0, 2.0) * jnp.where(alone, 1.0, 2.0) / (LENGTH * LENGTH)
    even = (plus + minus) * (0.5 * scale)
    even_ref[0:512] = even
    even_ref[512:1024] = jnp.where(first, upper * scale, even)
    odd = (plus - minus) * (0.5 * scale)
    odd_ref[...] = jnp.where(lanes < 64, -odd, odd)


def add_weights(pencil, cell_ref, wave_ref, plane_ref, weights):
    doubled = jnp.concatenate(
        [weights[g : g + 1] * plane_ref[y : y + 1] for g in range(4) for y in range(2)]
    )
    waves = (wave_ref[...][:, None, :] * doubled[None]).reshape(128, LENGTH)
    cells = lax.broadcasted_iota(jnp.int32, (LENGTH, LENGTH), 0)
    chosen = jnp.where(cells == cell_ref[...], 1.0, 0.0).astype(BF16)
    high, low = split(waves)
    both = dot(chosen, jnp.concatenate([high, low]), NT)
    return pencil + both[:, :128] + both[:, 128:]


def wait_kernel(panel, *refs):
    index_ref, source_ref, cell_ref, wave_ref, plane_ref = refs[:5]
    unknown_refs = refs[5 : 5 + panel]
    pencil = source_ref[...].reshape(LENGTH, 128)
    pencil = swap_groups(pencil) if panel == 1 else pencil
    newest = unknown_refs[-1][16:20]
    pencil = add_weights(pencil, cell_ref, wave_ref, plane_ref, newest)
    if panel == 3:
        refs[-1][...] = pencil
        return
    pencil_ref, work_ref, high_ref, low_ref = refs[-4:]
    pencil_ref[...] = pencil
    work = refs[5 + panel][0]
    for j, ref in enumerate(unknown_refs):
        start = 6 + panel + 8 * j
        work = work - take_rows(
            ref[...], index_ref, refs[start : start + 8], high_ref, low_ref
        )
    work_ref[0] = work


def filter_kernel(
    pencil_ref, cell_ref, wave_ref, plane_ref, a_ref, b_ref, c_ref, d_ref,
    high_hbm, low_hbm, back_high_hbm, back_low_hbm, even_ref, odd_ref, out_ref,
    high_ref, low_ref, back_high_ref, back_low_ref, sems,
):
    sources = (high_hbm, low_hbm, back_high_hbm, back_low_hbm)
    places = (high_ref, low_ref, back_high_ref, back_low_ref)
    copies = [
        pltpu.make_async_copy(source, place, sems.at[number])
        for number, (source, place) in enumerate(zip(sources, places))
    ]
    for copy in copies:
        copy.start()
    weights = (a_ref[16:20] + b_ref[16:20]) + (c_ref[16:20] + d_ref[16:20])
    pencil = add_weights(pencil_ref[...], cell_ref, wave_ref, plane_ref, weights)
    copies[0].wait()
    copies[1].wait()
    freq = table_nn(high_ref[...], low_ref[...], pencil)
    real, imag = freq[:512], freq[512:]
    odd = odd_ref[...]
    real_out = even_ref[0:512] * real + odd * pltpu.roll(imag, 64, 1)
    imag_out = even_ref[512:1024] * imag - odd * pltpu.roll(real, 64, 1)
    copies[2].wait()
    copies[3].wait()
    back = table_nn(
        back_high_ref[...], back_low_ref[...], jnp.concatenate([real_out, imag_out])
    )
    out_ref[...] = swap_groups(back).reshape(64, 16, 128)


def close_kernel(slots_ref, high_ref, low_ref, out_ref, rows_ref):
    @pl.when(pl.program_id(0) == 0)
    def _():
        rows = jnp.transpose(slots_ref[...].reshape(LENGTH, 128))
        rows_high, rows_low = split(rows)
        rows_ref[0:128] = rows_high
        rows_ref[128:256] = rows_low

    both = dot(rows_ref[...], high_ref[...], NN)
    total = both[:128] + both[128:] + dot(rows_ref[0:128], low_ref[...], NN)
    out_ref[...] = total.reshape(out_ref.shape)


def update_kernel(first_panel, panels, index_ref, base_ref, factor_ref, *refs):
    out_ref, high_ref, low_ref = refs[8:]
    block = pl.program_id(0)

    @pl.when(block == 0)
    def _():
        for step, ref in enumerate(refs[:8]):
            start = pl.multiple_of(source_of(index_ref, step) * 16, 16)
            for k in range(panels):
                high, low = split(ref[16 * k : 16 * k + 16])
                high_ref[k, pl.ds(start, 16), :] = high
                low_ref[k, pl.ds(start, 16), :] = low

    own = index_ref[0] * 16
    row = lax.broadcasted_iota(jnp.int32, (128, LENGTH), 0) + block * 128
    col = lax.broadcasted_iota(jnp.int32, (128, LENGTH), 1)
    base = base_ref[...].reshape(128, 128)
    if first_panel == 0:
        base_row = lax.broadcasted_iota(jnp.int32, (128, 128), 0) + block * 128
        base = jnp.where(base_row < 64, 0.0, base)
    for step in range(panels):
        panel = first_panel + step
        rows = factor_ref[:, :, LENGTH * step : LENGTH * (step + 1)].reshape(128, LENGTH)
        mine = (row // 16 == panel) & (col == own + row % 16)
        rows = jnp.where(row < 64, jnp.where(mine, -1.0, 0.0), rows)
        rows_high, rows_low = split(rows)
        wide = dot(jnp.concatenate([rows_high, rows_low]), high_ref[step], NT)
        base = base - (wide[:128] + wide[128:] + dot(rows_high, low_ref[step], NT))
    out_ref[...] = base.reshape(8, 16, 128)


def spec(*shape):
    return pl.BlockSpec(shape, lambda *_: (0,) * len(shape))


def block_at(shape, place):
    return pl.BlockSpec(shape, lambda *_: place)


def cost(flops, moved):
    return pl.CostEstimate(flops=flops, bytes_accessed=moved, transcendentals=0)


def shape_of(*shape):
    return jax.ShapeDtypeStruct(shape, F32)


def call(body, name, in_specs, out_specs, out_shape, flops, moved, scratch=(), grid=1):
    return pl.pallas_call(
        body,
        grid=(grid,),
        in_specs=in_specs,
        out_specs=out_specs,
        out_shape=out_shape,
        scratch_shapes=scratch,
        compiler_params=LIMIT,
        cost_estimate=cost(flops, moved),
        name=name,
    )


def ring(size, step):
    return [(place, (place + step) % size) for place in range(size)]


def share(partial):
    total = partial + lax.ppermute(partial, "core", ring(2, 1))
    return [total] + [lax.ppermute(total, "x", ring(4, step)) for step in (1, 2, 3)]


def hop(pieces, step):
    pieces[step] = lax.ppermute(pieces[step - 1], "z", ring(8, 1))
    if step < 4:
        pieces[8 - step] = lax.ppermute(pieces[(9 - step) % 8], "z", ring(8, 7))


def tie(*groups):
    flat = lax.optimization_barrier(tuple(group[at] for group, ats in groups for at in ats))
    flat = list(flat)
    for group, ats in groups:
        for at in ats:
            group[at] = flat.pop(0)


def update(first_panel, panels, index, base, factor, pieces):
    return call(
        functools.partial(update_kernel, first_panel, panels),
        "update",
        [
            SMEM,
            pl.BlockSpec((8, 16, 128), lambda i: (i, 0, 0)),
            pl.BlockSpec((8, 16, panels * LENGTH), lambda i: (i, 0, first_panel // panels)),
        ]
        + [spec(16 * panels, LENGTH)] * 8,
        pl.BlockSpec((8, 16, 128), lambda i: (i, 0, 0)),
        shape_of(32, 16, 128),
        3 * 2 * 512 * panels * LENGTH * 128,
        2_700_000 * panels,
        [pltpu.VMEM((panels, 128, LENGTH), BF16)] * 2,
        grid=4,
    )(index, base, factor, *pieces)


SMEM = pl.BlockSpec(memory_space=pltpu.SMEM)
ANY = pl.BlockSpec(memory_space=pl.ANY)
TABLE = pltpu.VMEM((LENGTH, LENGTH), BF16)


def per_device(factor, inverses, right_side, obs_cells, noise, spectrum):
    z_high, z_low = (jnp.asarray(t) for t in halves(z_table()))
    x_high, x_low = (jnp.asarray(t) for t in halves(x_table()))
    back_high, back_low = (jnp.asarray(t) for t in halves(x_table().T))
    wide = lax.axis_index(WIDE).astype(jnp.int32)
    index = jnp.stack([wide, lax.axis_index("y").astype(jnp.int32)])

    columns, side = call(
        columns_kernel,
        "columns",
        [spec(64, LENGTH), spec(4, 16, 128)],
        [spec(8, 64, 128), spec(64, 128)],
        [shape_of(8, 64, 128), shape_of(64, 128)],
        0,
        500_000,
    )(inverses.reshape(64, LENGTH), right_side)
    box = [columns, side, noise, spectrum]
    tie((box, (0, 1, 2, 3)))
    columns, side, noise, spectrum = box
    columns = lax.all_to_all(columns, ("x", "core"), 0, 0)
    sides = [side] + [lax.ppermute(side, "y", ring(4, step)) for step in (1, 2, 3)]
    extra = lax.ppermute(spectrum[:, :, 0].T, WIDE, [(32, 0)])

    slab = call(
        noise_kernel,
        "noise",
        [spec(128, LENGTH)] + [pl.BlockSpec((256, LENGTH), lambda i: (i, 0))] * 2,
        pl.BlockSpec((16, 16, 128), lambda i: (i, 0, 0)),
        shape_of(64, 16, 128),
        3 * 2 * 128 * LENGTH * LENGTH,
        5_000_000,
        grid=4,
    )(noise.reshape(128, LENGTH), z_high, z_low)
    box = [columns, slab]
    tie((box, (0, 1)))
    columns, slab = box

    near, far = call(
        bundle_kernel,
        "bundle",
        [SMEM, spec(8, 64, 128)]
        + [block_at((1, 16, LENGTH * k), (k, 0, 0)) for k in range(1, 4)]
        + [spec(64, 128)] * 4,
        [spec(8, 80, 128), spec(8, 96, 128)],
        [shape_of(8, 80, 128), shape_of(8, 96, 128)],
        0,
        1_500_000,
    )(index, columns, factor, factor, factor, *sides)
    near, far = [near] * 8, [far] * 8
    hop(near, 1)
    hop(far, 1)

    cell_x = (obs_cells // (8 * LENGTH)).reshape(1, 4096)
    plane = obs_cells // LENGTH % 8 - 2 * lax.axis_index("y")
    planes = jnp.stack([plane == 0, plane == 1]).astype(F32)
    freq, phase = z_frequencies(wide, jnp)
    turn = (freq[:, None] * (obs_cells % LENGTH)[None, :] + phase[:, None]) % LENGTH
    waves = jnp.cos(turn.astype(F32) * (2.0 * math.pi / LENGTH))
    box = [slab, waves, planes, cell_x]
    tie((near, (1, 7)), (box, (0, 1, 2, 3)))
    slab, waves, planes, cell_x = box
    hop(near, 2)
    slab = lax.all_to_all(slab, WIDE, 0, 0)
    tie((near, (2, 6)), (far, (1, 7)))
    hop(near, 3)
    hop(far, 2)
    box = [extra, spectrum]
    tie((near, (3, 5)), (box, (0, 1)))
    extra, spectrum = box
    hop(near, 4)
    extra = jnp.concatenate([extra, jnp.zeros((6, LENGTH), F32)])
    even, odd = call(
        spectrum_kernel,
        "spectrum",
        [SMEM, spec(LENGTH, 32), spec(8, LENGTH)],
        [spec(LENGTH, 128), spec(512, 128)],
        [shape_of(LENGTH, 128), shape_of(512, 128)],
        300_000_000,
        1_500_000,
    )(index, spectrum.reshape(LENGTH, 32), extra)
    box = [even, odd]
    tie((near, (4,)), (far, (2, 6)), (box, (0, 1)))
    even, odd = box

    obs_specs = lambda k: [
        block_at((1, LENGTH), (0, k)),
        block_at((16, LENGTH), (0, k)),
        block_at((2, LENGTH), (0, k)),
    ]
    side_spec = lambda k: block_at((1, COLS, 128), (k, 0, 0))
    piece_specs = lambda at: [block_at((8, 16, 128), (0, at, 0))] * 8
    panel_spec = spec(COLS, LENGTH)
    panel_shape = shape_of(COLS, LENGTH)
    inverse_at = [(near, 0), (near, 1), (far, 0), (far, 1)]
    factor_at = {
        (1, 0): (near, 2),
        (2, 0): (near, 3),
        (2, 1): (far, 2),
        (3, 0): (far, 3),
        (3, 1): (far, 4),
        (3, 2): (far, 5),
    }
    rows_scratch = [pltpu.VMEM((128, LENGTH), BF16)] * 2

    partial, sides = call(
        first_kernel,
        "first",
        [SMEM] + piece_specs(0) + [block_at((8, 16, 128), (0, 4, 0))] * 8,
        [panel_spec, spec(4, COLS, 128)],
        [panel_shape, shape_of(4, COLS, 128)],
        20_000_000,
        1_200_000,
        [pltpu.VMEM((4, 128, 128), F32)],
    )(index, *near, *near)
    parts = share(partial)
    hop(far, 3)
    tie((parts, (0, 1, 2, 3)), (far, (3, 5)))
    unknowns = []
    box = [slab, sides]
    for panel in range(1, 4):
        pencil, work = box
        factor_pieces, factor_place = factor_at[panel, panel - 1]
        inverse_pieces, inverse_place = inverse_at[panel]
        partial, unknown = call(
            step_kernel,
            f"step{panel}",
            [SMEM, side_spec(1 if panel == 1 else 0)]
            + [panel_spec] * 4
            + piece_specs(factor_place)
            + piece_specs(inverse_place),
            [panel_spec] * 2,
            [panel_shape] * 2,
            40_000_000,
            1_500_000,
            rows_scratch,
        )(index, work, *parts, *factor_pieces, *inverse_pieces)
        unknowns.append(unknown)
        parts = share(partial)
        later = panel < 3
        rows = [factor_at[panel + 1, j] for j in range(panel)] if later else []
        box = call(
            functools.partial(wait_kernel, panel),
            f"wait{panel}",
            [SMEM, spec(64, 16, 128) if panel == 1 else spec(LENGTH, 128)]
            + obs_specs(panel - 1)
            + [panel_spec] * panel
            + [side_spec(panel + 1)] * later
            + [one for _, place in rows for one in piece_specs(place)],
            [spec(LENGTH, 128)] + [spec(1, COLS, 128)] * later,
            [shape_of(LENGTH, 128)] + [shape_of(1, COLS, 128)] * later,
            2 * 2 * 128 * LENGTH * LENGTH,
            1_500_000,
            rows_scratch * later,
        )(
            index, pencil, cell_x, waves, planes, *unknowns, *[sides] * later,
            *[one for pieces, _ in rows for one in pieces],
        )
        box = list(box)
        if panel == 1:
            hop(far, 4)
            tie((parts, (0, 1, 2, 3)), (box, (0, 1)), (far, (4,)))
        elif panel == 2:
            early = [jnp.concatenate([u[:16] for u in unknowns])] * 8
            hop(early, 1)
            tie((parts, (0, 1, 2, 3)), (box, (0, 1)), (early, (1, 7)))
        else:
            hop(early, 2)
            tie((parts, (0, 1, 2, 3)), (box, (0,)), (early, (2, 6)))

    slots = call(
        filter_kernel,
        "filter",
        [spec(LENGTH, 128)]
        + obs_specs(3)
        + [panel_spec] * 4
        + [ANY] * 4
        + [spec(LENGTH, 128), spec(512, 128)],
        spec(64, 16, 128),
        shape_of(64, 16, 128),
        8 * 2 * 128 * LENGTH * LENGTH,
        11_000_000,
        [TABLE] * 4 + [pltpu.SemaphoreType.DMA((4,))],
    )(box[0], cell_x, waves, planes, *parts, x_high, x_low, back_high, back_low, even, odd)
    late = (parts[0][:16] + parts[1][:16]) + (parts[2][:16] + parts[3][:16])
    late = [jnp.concatenate([unknowns[2][:16], late])] * 8
    hop(early, 3)
    hop(late, 1)
    box = [slots]
    tie((box, (0,)), (early, (3, 5)), (late, (1, 7)))
    slots = lax.all_to_all(box[0], WIDE, 0, 0)
    hop(early, 4)
    hop(late, 2)
    hop(late, 3)
    solved = update(0, 2, index, right_side, factor, early)
    hop(late, 4)
    solved = update(2, 2, index, solved, factor, late)
    slots, solved = lax.optimization_barrier((slots, solved))
    correction = call(
        close_kernel,
        "close",
        [spec(64, 16, 128)] + [pl.BlockSpec((LENGTH, 256), lambda i: (0, i))] * 2,
        pl.BlockSpec((16, 4, 2, 256), lambda i: (0, 0, 0, i)),
        shape_of(16, 4, 2, LENGTH),
        3 * 2 * 128 * LENGTH * LENGTH,
        5_500_000,
        [pltpu.VMEM((256, LENGTH), BF16)],
        grid=4,
    )(slots, z_high, z_low)
    return (solved, correction)


def solution(mesh):
    grid = Mesh(mesh.devices.reshape(8, 4, 2, 4), ("z", "x", "core", "y"))
    return jax.shard_map(
        per_device,
        mesh=grid,
        in_specs=(
            P(None, WIDE, None),
            P(None, None, WIDE, None),
            P(None, WIDE, "y"),
            P(),
            P(WIDE, None, "y", None),
            P(None, "y", WIDE),
        ),
        out_specs=(P(None, WIDE, "y"), P(WIDE, None, "y", None)),
        check_vma=False,
    )
```

```python
import functools
import math

import jax
import jax.numpy as jnp
import numpy as np
from jax import lax
from jax.experimental import pallas as pl
from jax.experimental.pallas import tpu as pltpu
from jax.sharding import Mesh, PartitionSpec as P

F32 = jnp.float32
BF16 = jnp.bfloat16
WIDE = ("z", "x", "core")
LENGTH = 1024
COLS = 24
NN = (((1,), (0,)), ((), ()))
NT = (((1,), (1,)), ((), ()))
LIMIT = pltpu.CompilerParams(vmem_limit_bytes=56 * 1024 * 1024)


def halves(table):
    high = table.astype(np.float32).astype(jnp.bfloat16)
    low = (table - high.astype(np.float64)).astype(np.float32).astype(jnp.bfloat16)
    return (np.asarray(high), np.asarray(low))


def z_frequencies(owner, xp):
    step = xp.arange(16) % 8
    part = xp.arange(16) // 8
    freq = 16 * owner + step + xp.where(owner >= 32, 1, 0)
    lone = (owner == 0) & (step == 0) & (part == 1)
    return (xp.where(lone, 512, freq), xp.where(lone, 0, 256 * part))


def z_table():
    rows = []
    cells = np.arange(LENGTH)
    for owner in range(64):
        freq, phase = z_frequencies(np.int64(owner), np)
        turn = (freq[:, None] * cells[None, :] + phase[:, None]) % LENGTH
        rows.append(np.cos(2.0 * np.pi * turn / LENGTH))
    return np.concatenate(rows)


def x_table():
    cells = np.arange(LENGTH)
    freq = np.concatenate([np.arange(512), np.arange(512)])
    phase = np.repeat([0, 256], 512)
    freq[512], phase[512] = 512, 0
    turn = (freq[:, None] * cells[None, :] + phase[:, None]) % LENGTH
    return np.cos(2.0 * np.pi * turn / LENGTH)


def split(value):
    high = value.astype(BF16)
    low = (value - high.astype(F32)).astype(BF16)
    return (high, low)


def dot(left, right, dims):
    return lax.dot_general(left, right, dims, preferred_element_type=F32)


def dot_nt(left, right):
    left_high, left_low = split(left)
    right_high, right_low = split(right)
    rows = left.shape[0]
    both = dot(jnp.concatenate([left_high, left_low]), right_high, NT)
    return both[:rows] + both[rows:] + dot(left_high, right_low, NT)


def table_nn(high, low, value):
    value_high, value_low = split(value)
    cols = value.shape[1]
    both = dot(high, jnp.concatenate([value_high, value_low], axis=1), NN)
    return both[:, :cols] + both[:, cols:] + dot(low, value_high, NN)


def swap_groups(value):
    row = lax.broadcasted_iota(jnp.int32, value.shape, 0)
    lane = lax.broadcasted_iota(jnp.int32, value.shape, 1)
    for bit in range(4):
        step = 1 << bit
        row_bit = (row >> bit) & 1
        lane_bit = (lane >> (3 + bit)) & 1
        up = pltpu.roll(pltpu.roll(value, LENGTH - step, 0), 8 * step, 1)
        down = pltpu.roll(pltpu.roll(value, step, 0), 128 - 8 * step, 1)
        value = jnp.where(row_bit == lane_bit, value, jnp.where(lane_bit == 1, up, down))
    return value


def columns_kernel(inverse_ref, right_ref, out_ref, side_ref):
    side_ref[...] = right_ref[...].reshape(64, 128)
    lane = lax.broadcasted_iota(jnp.int32, (64, 128), 1) // 16
    for r in range(8):
        total = jnp.zeros((64, 128), F32)
        for z in range(8):
            piece = inverse_ref[:, 128 * z : 128 * z + 128]
            piece = pltpu.roll(piece, (16 * (z - r)) % 128, 1) if z != r else piece
            total = jnp.where(lane == z, piece, total)
        out_ref[r] = total


def noise_kernel(noise_ref, high_ref, low_ref, out_ref):
    noise_high, noise_low = split(noise_ref[...])
    both = dot(high_ref[...], jnp.concatenate([noise_high, noise_low]), NT)
    slots = both[:, :128] + both[:, 128:] + dot(low_ref[...], noise_high, NT)
    out_ref[...] = slots.reshape(16, 16, 128)


def bundle_kernel(index_ref, columns_ref, one_ref, two_ref, three_ref, *refs):
    side_refs, (start_ref, near_ref, far_ref) = refs[:4], refs[4:]
    start_ref[:, 0:16, :] = columns_ref[:, 0:16, :]
    near_ref[:, 0:32, :] = columns_ref[:, 16:48, :]
    far_ref[:, 0:16, :] = columns_ref[:, 48:64, :]
    for t in range(8):
        lanes = lambda j: pl.ds(LENGTH * j + 128 * t, 128)
        near_ref[t, 32:48, :] = one_ref[0, :, lanes(0)]
        for j in range(2):
            near_ref[t, 48 + 16 * j : 64 + 16 * j, :] = two_ref[0, :, lanes(j)]
        for j in range(3):
            far_ref[t, 16 + 16 * j : 32 + 16 * j, :] = three_ref[0, :, lanes(j)]
    start_ref[:, 16:24, :] = side_refs[0][...].reshape(8, 8, 128)
    lane = lax.broadcasted_iota(jnp.int32, (64, 128), 1)
    weights = jnp.zeros((64, 128), F32)
    for step, ref in enumerate(side_refs):
        y = lax.rem(index_ref[1] + 4 - step, 4)
        weights = jnp.where(lane == y, ref[:, 0:1], weights)
    start_ref[:, 24:32, :] = weights.reshape(8, 8, 128)


def source_of(index_ref, step):
    return lax.rem(index_ref[0] // 8 + 8 - step, 8)


def spread(work, index_ref, piece_refs, out_ref):
    high, low = split(work)
    both = jnp.concatenate([high, low])
    for step, ref in enumerate(piece_refs):
        rows_high, rows_low = split(ref[...].reshape(128, 128))
        wide = dot(both, rows_high, NT)
        start = pl.multiple_of(source_of(index_ref, step) * 128, 128)
        out_ref[:, pl.ds(start, 128)] = (
            wide[:COLS] + wide[COLS:] + dot(high, rows_low, NT)
        )


def take_rows(unknown, index_ref, piece_refs, high_ref, low_ref):
    for step, ref in enumerate(piece_refs):
        rows = jnp.concatenate([ref[t] for t in range(8)], axis=1)
        start = pl.multiple_of(source_of(index_ref, step) * 16, 16)
        rows_high, rows_low = split(rows)
        high_ref[pl.ds(start, 16), :] = rows_high
        low_ref[pl.ds(start, 16), :] = rows_low
    high, low = split(unknown)
    wide = dot(jnp.concatenate([high, low]), high_ref[...], NT)
    return wide[:COLS] + wide[COLS:] + dot(high, low_ref[...], NT)


def first_kernel(index_ref, *refs):
    out_ref, side_ref, rows_ref = refs[16:]
    lane = lax.broadcasted_iota(jnp.int32, (64, 128), 1)
    z = index_ref[0] // 8
    for step, ref in enumerate(refs[8:16]):
        own = pltpu.roll(ref[:, 0:8, :].reshape(64, 128), lax.rem(128 - 16 * z, 128), 1)
        weights = pltpu.roll(ref[:, 8:16, :].reshape(64, 128), 16, 1)
        rows = jnp.where(lane < 16, own, jnp.where(lane < 20, weights, 0.0))
        start = pl.multiple_of(source_of(index_ref, step) * 16, 16)
        for k in range(4):
            rows_ref[k, pl.ds(start, 16), :] = rows[16 * k : 16 * k + 16]
    for k in range(4):
        side_ref[k] = jnp.transpose(rows_ref[k])[:COLS]
    spread(side_ref[0], index_ref, refs[:8], out_ref)


def step_kernel(older, index_ref, start_ref, a_ref, b_ref, c_ref, d_ref, *refs):
    older_refs, refs = refs[:older], refs[older:]
    factor_refs, refs = refs[: 8 * older + 8], refs[8 * older + 8 :]
    inverse_refs = refs[:8]
    out_ref, unknown_ref, high_ref, low_ref = refs[8:]
    unknown = (a_ref[...] + b_ref[...]) + (c_ref[...] + d_ref[...])
    unknown_ref[...] = unknown
    work = start_ref[0]
    for j, one in enumerate([ref[...] for ref in older_refs] + [unknown]):
        work = work - take_rows(
            one, index_ref, factor_refs[8 * j : 8 * j + 8], high_ref.at[j], low_ref.at[j]
        )
    spread(work, index_ref, inverse_refs, out_ref)


def spectrum_kernel(index_ref, spectrum_ref, extra_ref, even_ref, odd_ref):
    owner = index_ref[0]
    row = lax.broadcasted_iota(jnp.int32, (32, 128), 0)
    lane = lax.broadcasted_iota(jnp.int32, (32, 128), 1)
    lone = (owner == 0) & (lane // 8 == 8)
    same_y = row // 16 == lane % 2
    same_z = row % 16 == (lane // 8) % 8 + jnp.where(owner >= 32, 1, 0)
    pick = jnp.where(same_y & same_z & jnp.logical_not(lone), 1.0, 0.0).astype(BF16)
    extra_pick = jnp.where(lone & (row == lane % 2), 1.0, 0.0)[:8].astype(BF16)

    def exact(value, choose):
        high = value.astype(BF16)
        rest = value - high.astype(F32)
        middle = rest.astype(BF16)
        low = (rest - middle.astype(F32)).astype(BF16)
        return choose(high) + (choose(middle) + choose(low))

    wanted = exact(spectrum_ref[...], lambda part: dot(part, pick, NN))
    wanted = wanted + exact(
        jnp.transpose(extra_ref[...]), lambda part: dot(part, extra_pick, NN)
    )
    at_row = lax.broadcasted_iota(jnp.int32, (512, 512), 0)
    at_col = lax.broadcasted_iota(jnp.int32, (512, 512), 1)
    mirror = jnp.where(at_row + at_col == 512, 1.0, 0.0).astype(BF16)
    plus = wanted[:512]
    upper = wanted[512:]
    minus = exact(upper, lambda part: dot(mirror, part, NN))
    first = lax.broadcasted_iota(jnp.int32, (512, 128), 0) == 0
    minus = jnp.where(first, plus, minus)
    lanes = lax.broadcasted_iota(jnp.int32, (512, 128), 1)
    alone = (owner == 0) & ((lanes // 8) % 8 == 0)
    scale = jnp.where(first, 1.0, 2.0) * jnp.where(alone, 1.0, 2.0) / (LENGTH * LENGTH)
    even = (plus + minus) * (0.5 * scale)
    even_ref[0:512] = even
    even_ref[512:1024] = jnp.where(first, upper * scale, even)
    odd = (plus - minus) * (0.5 * scale)
    odd_ref[...] = jnp.where(lanes < 64, -odd, odd)


def add_weights(pencil, cell_ref, wave_ref, plane_ref, weights):
    doubled = jnp.concatenate(
        [weights[g : g + 1] * plane_ref[y : y + 1] for g in range(4) for y in range(2)]
    )
    waves = (wave_ref[...][:, None, :] * doubled[None]).reshape(128, LENGTH)
    cells = lax.broadcasted_iota(jnp.int32, (LENGTH, LENGTH), 0)
    chosen = jnp.where(cells == cell_ref[...], 1.0, 0.0).astype(BF16)
    high, low = split(waves)
    both = dot(chosen, jnp.concatenate([high, low]), NT)
    return pencil + both[:, :128] + both[:, 128:]


def wait_kernel(panel, *refs):
    index_ref, cell_ref, wave_ref, plane_ref, unknown_ref = refs[:5]
    weights = unknown_ref[16:20]
    if panel == 1:
        side_ref, piece_refs = refs[5], refs[6:14]
        pencil_ref, work_ref, high_ref, low_ref = refs[14:]
        pencil = add_weights(0.0, cell_ref, wave_ref, plane_ref, weights)
        pencil_ref[...] = pencil
        work_ref[0] = side_ref[0] - take_rows(
            unknown_ref[...], index_ref, piece_refs, high_ref, low_ref
        )
        return
    pencil = refs[5][...]
    if panel == 2:
        pencil = pencil + swap_groups(refs[6][...].reshape(LENGTH, 128))
    refs[-1][...] = add_weights(pencil, cell_ref, wave_ref, plane_ref, weights)


def filter_kernel(
    pencil_ref, cell_ref, wave_ref, plane_ref, a_ref, b_ref, c_ref, d_ref,
    high_hbm, low_hbm, back_high_hbm, back_low_hbm, even_ref, odd_ref, out_ref,
    high_ref, low_ref, back_high_ref, back_low_ref, sems,
):
    sources = (high_hbm, low_hbm, back_high_hbm, back_low_hbm)
    places = (high_ref, low_ref, back_high_ref, back_low_ref)
    copies = [
        pltpu.make_async_copy(source, place, sems.at[number])
        for number, (source, place) in enumerate(zip(sources, places))
    ]
    for copy in copies:
        copy.start()
    weights = (a_ref[16:20] + b_ref[16:20]) + (c_ref[16:20] + d_ref[16:20])
    pencil = add_weights(pencil_ref[...], cell_ref, wave_ref, plane_ref, weights)
    copies[0].wait()
    copies[1].wait()
    freq = table_nn(high_ref[...], low_ref[...], pencil)
    real, imag = freq[:512], freq[512:]
    odd = odd_ref[...]
    real_out = even_ref[0:512] * real + odd * pltpu.roll(imag, 64, 1)
    imag_out = even_ref[512:1024] * imag - odd * pltpu.roll(real, 64, 1)
    copies[2].wait()
    copies[3].wait()
    back = table_nn(
        back_high_ref[...], back_low_ref[...], jnp.concatenate([real_out, imag_out])
    )
    out_ref[...] = swap_groups(back).reshape(64, 16, 128)


def close_kernel(slots_ref, high_ref, low_ref, out_ref, rows_ref):
    @pl.when(pl.program_id(0) == 0)
    def _():
        rows = jnp.transpose(slots_ref[...].reshape(LENGTH, 128))
        rows_high, rows_low = split(rows)
        rows_ref[0:128] = rows_high
        rows_ref[128:256] = rows_low

    both = dot(rows_ref[...], high_ref[...], NN)
    total = both[:128] + both[128:] + dot(rows_ref[0:128], low_ref[...], NN)
    out_ref[...] = total.reshape(out_ref.shape)


def update_kernel(first_panel, panels, index_ref, base_ref, factor_ref, *refs):
    out_ref, high_ref, low_ref = refs[8:]
    block = pl.program_id(0)

    @pl.when(block == 0)
    def _():
        for step, ref in enumerate(refs[:8]):
            start = pl.multiple_of(source_of(index_ref, step) * 16, 16)
            for k in range(panels):
                high, low = split(ref[16 * k : 16 * k + 16])
                high_ref[k, pl.ds(start, 16), :] = high
                low_ref[k, pl.ds(start, 16), :] = low

    own = index_ref[0] * 16
    row = lax.broadcasted_iota(jnp.int32, (128, LENGTH), 0) + block * 128
    col = lax.broadcasted_iota(jnp.int32, (128, LENGTH), 1)
    base = base_ref[...].reshape(128, 128)
    if first_panel == 0:
        base_row = lax.broadcasted_iota(jnp.int32, (128, 128), 0) + block * 128
        base = jnp.where(base_row < 64, 0.0, base)
    for step in range(panels):
        panel = first_panel + step
        rows = factor_ref[:, :, LENGTH * step : LENGTH * (step + 1)].reshape(128, LENGTH)
        mine = (row // 16 == panel) & (col == own + row % 16)
        rows = jnp.where(row < 64, jnp.where(mine, -1.0, 0.0), rows)
        rows_high, rows_low = split(rows)
        wide = dot(jnp.concatenate([rows_high, rows_low]), high_ref[step], NT)
        base = base - (wide[:128] + wide[128:] + dot(rows_high, low_ref[step], NT))
    out_ref[...] = base.reshape(8, 16, 128)


def spec(*shape):
    return pl.BlockSpec(shape, lambda *_: (0,) * len(shape))


def block_at(shape, place):
    return pl.BlockSpec(shape, lambda *_: place)


def cost(flops, moved):
    return pl.CostEstimate(flops=flops, bytes_accessed=moved, transcendentals=0)


def shape_of(*shape):
    return jax.ShapeDtypeStruct(shape, F32)


def call(body, name, in_specs, out_specs, out_shape, flops, moved, scratch=(), grid=1):
    return pl.pallas_call(
        body,
        grid=(grid,),
        in_specs=in_specs,
        out_specs=out_specs,
        out_shape=out_shape,
        scratch_shapes=scratch,
        compiler_params=LIMIT,
        cost_estimate=cost(flops, moved),
        name=name,
    )


def ring(size, step):
    return [(place, (place + step) % size) for place in range(size)]


def share(partial):
    total = partial + lax.ppermute(partial, "core", ring(2, 1))
    return [total] + [lax.ppermute(total, "x", ring(4, step)) for step in (1, 2, 3)]


def hop(pieces, step):
    pieces[step] = lax.ppermute(pieces[step - 1], "z", ring(8, 1))
    if step < 4:
        pieces[8 - step] = lax.ppermute(pieces[(9 - step) % 8], "z", ring(8, 7))


def tie(*groups):
    flat = lax.optimization_barrier(tuple(group[at] for group, ats in groups for at in ats))
    flat = list(flat)
    for group, ats in groups:
        for at in ats:
            group[at] = flat.pop(0)


def update(first_panel, panels, index, base, factor, pieces):
    return call(
        functools.partial(update_kernel, first_panel, panels),
        "update",
        [
            SMEM,
            pl.BlockSpec((8, 16, 128), lambda i: (i, 0, 0)),
            pl.BlockSpec((8, 16, panels * LENGTH), lambda i: (i, 0, first_panel // panels)),
        ]
        + [spec(16 * panels, LENGTH)] * 8,
        pl.BlockSpec((8, 16, 128), lambda i: (i, 0, 0)),
        shape_of(32, 16, 128),
        3 * 2 * 512 * panels * LENGTH * 128,
        2_700_000 * panels,
        [pltpu.VMEM((panels, 128, LENGTH), BF16)] * 2,
        grid=4,
    )(index, base, factor, *pieces)


SMEM = pl.BlockSpec(memory_space=pltpu.SMEM)
ANY = pl.BlockSpec(memory_space=pl.ANY)
TABLE = pltpu.VMEM((LENGTH, LENGTH), BF16)


def per_device(factor, inverses, right_side, obs_cells, noise, spectrum):
    z_high, z_low = (jnp.asarray(t) for t in halves(z_table()))
    x_high, x_low = (jnp.asarray(t) for t in halves(x_table()))
    back_high, back_low = (jnp.asarray(t) for t in halves(x_table().T))
    wide = lax.axis_index(WIDE).astype(jnp.int32)
    index = jnp.stack([wide, lax.axis_index("y").astype(jnp.int32)])

    columns, side = call(
        columns_kernel,
        "columns",
        [spec(64, LENGTH), spec(4, 16, 128)],
        [spec(8, 64, 128), spec(64, 128)],
        [shape_of(8, 64, 128), shape_of(64, 128)],
        0,
        500_000,
    )(inverses.reshape(64, LENGTH), right_side)
    box = [columns, side, noise, spectrum]
    tie((box, (0, 1, 2, 3)))
    columns, side, noise, spectrum = box
    columns = lax.all_to_all(columns, ("x", "core"), 0, 0)
    sides = [side] + [lax.ppermute(side, "y", ring(4, step)) for step in (1, 2, 3)]
    extra = lax.ppermute(spectrum[:, :, 0].T, WIDE, [(32, 0)])
    head, near, far = call(
        bundle_kernel,
        "bundle",
        [SMEM, spec(8, 64, 128)]
        + [block_at((1, 16, LENGTH * k), (k, 0, 0)) for k in range(1, 4)]
        + [spec(64, 128)] * 4,
        [spec(8, 32, 128), spec(8, 80, 128), spec(8, 64, 128)],
        [shape_of(8, 32, 128), shape_of(8, 80, 128), shape_of(8, 64, 128)],
        0,
        1_500_000,
    )(index, columns, factor, factor, factor, *sides)
    head, near, far = [head] * 8, [near] * 8, [far] * 8
    hop(head, 1)
    hop(near, 1)
    box = [noise]
    tie((head, (1, 7)), (box, (0,)))

    hop(head, 2)
    slab = call(
        noise_kernel,
        "noise",
        [spec(128, LENGTH)] + [pl.BlockSpec((256, LENGTH), lambda i: (i, 0))] * 2,
        pl.BlockSpec((16, 16, 128), lambda i: (i, 0, 0)),
        shape_of(64, 16, 128),
        3 * 2 * 128 * LENGTH * LENGTH,
        5_000_000,
        grid=4,
    )(box[0].reshape(128, LENGTH), z_high, z_low)
    box = [slab, extra, spectrum]
    tie((head, (2, 6)), (near, (1, 7)), (box, (0, 1, 2)))
    slab, extra, spectrum = box

    hop(head, 3)
    hop(near, 2)
    extra = jnp.concatenate([extra, jnp.zeros((6, LENGTH), F32)])
    even, odd = call(
        spectrum_kernel,
        "spectrum",
        [SMEM, spec(LENGTH, 32), spec(8, LENGTH)],
        [spec(LENGTH, 128), spec(512, 128)],
        [shape_of(LENGTH, 128), shape_of(512, 128)],
        300_000_000,
        1_500_000,
    )(index, spectrum.reshape(LENGTH, 32), extra)
    box = [even, odd]
    tie((head, (3, 5)), (near, (2, 6)), (box, (0, 1)))
    even, odd = box
    hop(head, 4)
    hop(near, 3)

    obs_specs = lambda k: [
        block_at((1, LENGTH), (0, k)),
        block_at((16, LENGTH), (0, k)),
        block_at((2, LENGTH), (0, k)),
    ]
    side_spec = lambda k: block_at((1, COLS, 128), (k, 0, 0))
    piece_specs = lambda at: [block_at((8, 16, 128), (0, at, 0))] * 8
    panel_spec = spec(COLS, LENGTH)
    panel_shape = shape_of(COLS, LENGTH)
    rows_scratch = pltpu.VMEM((128, LENGTH), BF16)

    partial, sides = call(
        first_kernel,
        "first",
        [SMEM] + piece_specs(0) + [block_at((8, 16, 128), (0, 1, 0))] * 8,
        [panel_spec, spec(4, COLS, 128)],
        [panel_shape, shape_of(4, COLS, 128)],
        20_000_000,
        1_200_000,
        [pltpu.VMEM((4, 128, 128), F32)],
    )(index, *head, *head)
    total = partial + lax.ppermute(partial, "core", ring(2, 1))
    box = [total, obs_cells]
    tie((near, (3, 5)), (far, (0,)), (box, (0, 1)))
    total, obs_cells = box
    parts = [total] + [lax.ppermute(total, "x", ring(4, step)) for step in (1, 2, 3)]
    hop(near, 4)
    far = [far[0]] * 8
    hop(far, 1)

    cell_x = (obs_cells // (8 * LENGTH)).reshape(1, 4096)
    plane = obs_cells // LENGTH % 8 - 2 * lax.axis_index("y")
    planes = jnp.stack([plane == 0, plane == 1]).astype(F32)
    freq, phase = z_frequencies(wide, jnp)
    turn = (freq[:, None] * (obs_cells % LENGTH)[None, :] + phase[:, None]) % LENGTH
    waves = jnp.cos(turn.astype(F32) * (2.0 * math.pi / LENGTH))
    box = [slab, waves, planes, cell_x]
    tie((box, (0, 1, 2, 3)))
    slab, waves, planes, cell_x = box
    slab = lax.all_to_all(slab, WIDE, 0, 0)
    tie((parts, (0, 1, 2, 3)), (near, (4,)), (far, (1, 7)))

    def step(panel, work, work_at, inverse, factors, older):
        return call(
            functools.partial(step_kernel, len(older)),
            f"step{panel}",
            [SMEM, side_spec(work_at)]
            + [panel_spec] * (4 + len(older))
            + [one for _, place in factors for one in piece_specs(place)]
            + piece_specs(inverse[1]),
            [panel_spec] * 2,
            [panel_shape] * 2,
            40_000_000,
            1_500_000,
            [pltpu.VMEM((len(older) + 1, 128, LENGTH), BF16)] * 2,
        )(index, work, *parts, *older, *[p for ps, _ in factors for p in ps], *inverse[0])

    def wait(panel, unknown, *rest, specs, outs=1, scratch=()):
        return call(
            functools.partial(wait_kernel, panel),
            f"wait{panel}",
            [SMEM] + obs_specs(panel - 1) + [panel_spec] + specs,
            [spec(LENGTH, 128), spec(1, COLS, 128)][:outs],
            [shape_of(LENGTH, 128), shape_of(1, COLS, 128)][:outs],
            2 * 2 * 128 * LENGTH * LENGTH,
            1_500_000,
            scratch,
        )(index, cell_x, waves, planes, unknown, *rest)

    partial, first = step(1, sides, 1, (near, 0), [(near, 2)], [])
    parts = share(partial)
    hop(far, 2)
    hop(far, 3)
    box = list(
        wait(
            1, first, sides, *near,
            specs=[side_spec(2)] + piece_specs(3), outs=2, scratch=[rows_scratch] * 2,
        )
    )
    tie((parts, (0, 1, 2, 3)), (box, (0, 1)), (far, (3, 5)))

    partial, second = step(2, box[1], 0, (near, 1), [(near, 4)], [])
    parts = share(partial)
    hop(far, 4)
    early = [jnp.concatenate([first[:16], second[:16]])] * 8
    hop(early, 1)
    box = list(
        wait(2, second, box[0], slab, specs=[spec(LENGTH, 128), spec(64, 16, 128)])
    )
    tie((parts, (0, 1, 2, 3)), (box, (0,)), (early, (1, 7)), (far, (4,)))

    partial, third = step(
        3, sides, 3, (far, 0), [(far, 1), (far, 2), (far, 3)], [first, second]
    )
    parts = share(partial)
    hop(early, 2)
    box = list(wait(3, third, box[0], specs=[spec(LENGTH, 128)]))
    tie((parts, (0, 1, 2, 3)), (box, (0,)), (early, (2, 6)))

    slots = call(
        filter_kernel,
        "filter",
        [spec(LENGTH, 128)]
        + obs_specs(3)
        + [panel_spec] * 4
        + [ANY] * 4
        + [spec(LENGTH, 128), spec(512, 128)],
        spec(64, 16, 128),
        shape_of(64, 16, 128),
        8 * 2 * 128 * LENGTH * LENGTH,
        11_000_000,
        [TABLE] * 4 + [pltpu.SemaphoreType.DMA((4,))],
    )(box[0], cell_x, waves, planes, *parts, x_high, x_low, back_high, back_low, even, odd)
    late = (parts[0][:16] + parts[1][:16]) + (parts[2][:16] + parts[3][:16])
    late = [jnp.concatenate([third[:16], late])] * 8
    hop(early, 3)
    hop(late, 1)
    box = [slots]
    tie((box, (0,)), (early, (3, 5)), (late, (1, 7)))
    slots = lax.all_to_all(box[0], WIDE, 0, 0)
    hop(early, 4)
    hop(late, 2)
    solved = update(0, 2, index, right_side, factor, early)
    hop(late, 3)
    hop(late, 4)
    slots, solved = lax.optimization_barrier((slots, solved))
    correction = call(
        close_kernel,
        "close",
        [spec(64, 16, 128)] + [pl.BlockSpec((LENGTH, 256), lambda i: (0, i))] * 2,
        pl.BlockSpec((16, 4, 2, 256), lambda i: (0, 0, 0, i)),
        shape_of(16, 4, 2, LENGTH),
        3 * 2 * 128 * LENGTH * LENGTH,
        5_500_000,
        [pltpu.VMEM((256, LENGTH), BF16)],
        grid=4,
    )(slots, z_high, z_low)
    solved, correction = lax.optimization_barrier((solved, correction))
    solved = update(2, 2, index, solved, factor, late)
    return (solved, correction)


def solution(mesh):
    grid = Mesh(mesh.devices.reshape(8, 4, 2, 4), ("z", "x", "core", "y"))
    return jax.shard_map(
        per_device,
        mesh=grid,
        in_specs=(
            P(None, WIDE, None),
            P(None, None, WIDE, None),
            P(None, WIDE, "y"),
            P(),
            P(WIDE, None, "y", None),
            P(None, "y", WIDE),
        ),
        out_specs=(P(None, WIDE, "y"), P(WIDE, None, "y", None)),
        check_vma=False,
    )
```

```python
import functools
import math

import jax
import jax.numpy as jnp
import numpy as np
from jax import lax
from jax.experimental import pallas as pl
from jax.experimental.pallas import tpu as pltpu
from jax.sharding import Mesh, PartitionSpec as P

F32 = jnp.float32
BF16 = jnp.bfloat16
WIDE = ("z", "x", "core")
LENGTH = 1024
COLS = 24
NN = (((1,), (0,)), ((), ()))
NT = (((1,), (1,)), ((), ()))
LIMIT = pltpu.CompilerParams(vmem_limit_bytes=56 * 1024 * 1024)


def halves(table):
    high = table.astype(np.float32).astype(jnp.bfloat16)
    low = (table - high.astype(np.float64)).astype(np.float32).astype(jnp.bfloat16)
    return (np.asarray(high), np.asarray(low))


def z_frequencies(owner, xp):
    step = xp.arange(16) % 8
    part = xp.arange(16) // 8
    freq = 16 * owner + step + xp.where(owner >= 32, 1, 0)
    lone = (owner == 0) & (step == 0) & (part == 1)
    return (xp.where(lone, 512, freq), xp.where(lone, 0, 256 * part))


def z_table():
    rows = []
    cells = np.arange(LENGTH)
    for owner in range(64):
        freq, phase = z_frequencies(np.int64(owner), np)
        turn = (freq[:, None] * cells[None, :] + phase[:, None]) % LENGTH
        rows.append(np.cos(2.0 * np.pi * turn / LENGTH))
    return np.concatenate(rows)


def x_table():
    cells = np.arange(LENGTH)
    freq = np.concatenate([np.arange(512), np.arange(512)])
    phase = np.repeat([0, 256], 512)
    freq[512], phase[512] = 512, 0
    turn = (freq[:, None] * cells[None, :] + phase[:, None]) % LENGTH
    return np.cos(2.0 * np.pi * turn / LENGTH)


def split(value):
    high = value.astype(BF16)
    low = (value - high.astype(F32)).astype(BF16)
    return (high, low)


def dot(left, right, dims):
    return lax.dot_general(left, right, dims, preferred_element_type=F32)


def dot_nt(left, right):
    left_high, left_low = split(left)
    right_high, right_low = split(right)
    rows = left.shape[0]
    both = dot(jnp.concatenate([left_high, left_low]), right_high, NT)
    return both[:rows] + both[rows:] + dot(left_high, right_low, NT)


def table_nn(high, low, value):
    value_high, value_low = split(value)
    cols = value.shape[1]
    both = dot(high, jnp.concatenate([value_high, value_low], axis=1), NN)
    return both[:, :cols] + both[:, cols:] + dot(low, value_high, NN)


def swap_groups(value):
    row = lax.broadcasted_iota(jnp.int32, value.shape, 0)
    lane = lax.broadcasted_iota(jnp.int32, value.shape, 1)
    for bit in range(4):
        step = 1 << bit
        row_bit = (row >> bit) & 1
        lane_bit = (lane >> (3 + bit)) & 1
        up = pltpu.roll(pltpu.roll(value, LENGTH - step, 0), 8 * step, 1)
        down = pltpu.roll(pltpu.roll(value, step, 0), 128 - 8 * step, 1)
        value = jnp.where(row_bit == lane_bit, value, jnp.where(lane_bit == 1, up, down))
    return value


def columns_kernel(inverse_ref, right_ref, out_ref, side_ref):
    side_ref[...] = right_ref[...].reshape(64, 128)
    lane = lax.broadcasted_iota(jnp.int32, (64, 128), 1) // 16
    for r in range(8):
        total = jnp.zeros((64, 128), F32)
        for z in range(8):
            piece = inverse_ref[:, 128 * z : 128 * z + 128]
            piece = pltpu.roll(piece, (16 * (z - r)) % 128, 1) if z != r else piece
            total = jnp.where(lane == z, piece, total)
        out_ref[r] = total


def noise_kernel(noise_ref, high_ref, low_ref, out_ref):
    noise_high, noise_low = split(noise_ref[...])
    both = dot(high_ref[...], jnp.concatenate([noise_high, noise_low]), NT)
    slots = both[:, :128] + both[:, 128:] + dot(low_ref[...], noise_high, NT)
    out_ref[...] = slots.reshape(16, 16, 128)


def lower_kernel(one_ref, two_ref, three_ref, out_ref):
    place = 0
    for k, ref in enumerate((one_ref, two_ref, three_ref)):
        for j in range(k + 1):
            out_ref[16 * place : 16 * place + 16] = ref[0, :, LENGTH * j : LENGTH * (j + 1)]
            place += 1


def bundle_kernel(index_ref, columns_ref, *refs):
    side_refs, (near_ref, far_ref) = refs[:4], refs[4:]
    lane = lax.broadcasted_iota(jnp.int32, (64, 128), 1)
    weights = jnp.zeros((64, 128), F32)
    for step, ref in enumerate(side_refs):
        y = lax.rem(index_ref[1] + 4 - step, 4)
        weights = jnp.where(lane == y + 16, ref[:, 0:1], weights)
    side = side_refs[0][...]
    inverses = [columns_ref[:, 16 * k : 16 * k + 16, :].reshape(128, 128) for k in range(4)]
    for z in range(8):
        own = pltpu.roll(side, (128 - 16 * z) % 128, 1) if z else side
        rows = jnp.where(lane < 16, own, weights)
        for k in range(2):
            near_ref[z, 128 * k : 128 * k + 128] = inverses[k]
            far_ref[z, 128 * k : 128 * k + 128] = inverses[2 + k]
        near_ref[z, 256:288] = jnp.transpose(jnp.concatenate([rows, rows]))[:32]


def spread(work, inverse_ref, out_ref):
    high, low = split(work)
    rows_high, rows_low = split(inverse_ref[...].reshape(LENGTH, 128))
    wide = dot(jnp.concatenate([high, low]), rows_high, NT)
    out_ref[...] = wide[:COLS] + wide[COLS:] + dot(high, rows_low, NT)


def first_kernel(near_ref, side_near_ref, out_ref, side_ref):
    lane = lax.broadcasted_iota(jnp.int32, (COLS, 128), 1) // 16
    for k in range(4):
        rows = jnp.zeros((COLS, 128), F32)
        for z in range(8):
            piece = side_near_ref[z, 0:COLS]
            turn = (16 * (z - k)) % 128
            piece = pltpu.roll(piece, turn, 1) if turn else piece
            rows = jnp.where(lane == z, piece, rows)
        side_ref[k] = rows
    spread(side_ref[0], near_ref, out_ref)


def step_kernel(start_ref, a_ref, b_ref, c_ref, d_ref, factor_ref, inverse_ref, out_ref, unknown_ref):
    unknown = (a_ref[...] + b_ref[...]) + (c_ref[...] + d_ref[...])
    unknown_ref[...] = unknown
    work = start_ref[0] - dot_nt(unknown, factor_ref[...].reshape(128, LENGTH))
    spread(work, inverse_ref, out_ref)


def spectrum_kernel(index_ref, spectrum_ref, extra_ref, even_ref, odd_ref):
    owner = index_ref[0]
    row = lax.broadcasted_iota(jnp.int32, (32, 128), 0)
    lane = lax.broadcasted_iota(jnp.int32, (32, 128), 1)
    lone = (owner == 0) & (lane // 8 == 8)
    same_y = row // 16 == lane % 2
    same_z = row % 16 == (lane // 8) % 8 + jnp.where(owner >= 32, 1, 0)
    pick = jnp.where(same_y & same_z & jnp.logical_not(lone), 1.0, 0.0).astype(BF16)
    extra_pick = jnp.where(lone & (row == lane % 2), 1.0, 0.0)[:8].astype(BF16)

    def exact(value, choose):
        high = value.astype(BF16)
        rest = value - high.astype(F32)
        middle = rest.astype(BF16)
        low = (rest - middle.astype(F32)).astype(BF16)
        return choose(high) + (choose(middle) + choose(low))

    wanted = exact(spectrum_ref[...], lambda part: dot(part, pick, NN))
    wanted = wanted + exact(
        jnp.transpose(extra_ref[...]), lambda part: dot(part, extra_pick, NN)
    )
    at_row = lax.broadcasted_iota(jnp.int32, (512, 512), 0)
    at_col = lax.broadcasted_iota(jnp.int32, (512, 512), 1)
    mirror = jnp.where(at_row + at_col == 512, 1.0, 0.0).astype(BF16)
    plus = wanted[:512]
    upper = wanted[512:]
    minus = exact(upper, lambda part: dot(mirror, part, NN))
    first = lax.broadcasted_iota(jnp.int32, (512, 128), 0) == 0
    minus = jnp.where(first, plus, minus)
    lanes = lax.broadcasted_iota(jnp.int32, (512, 128), 1)
    alone = (owner == 0) & ((lanes // 8) % 8 == 0)
    scale = jnp.where(first, 1.0, 2.0) * jnp.where(alone, 1.0, 2.0) / (LENGTH * LENGTH)
    even = (plus + minus) * (0.5 * scale)
    even_ref[0:512] = even
    even_ref[512:1024] = jnp.where(first, upper * scale, even)
    odd = (plus - minus) * (0.5 * scale)
    odd_ref[...] = jnp.where(lanes < 64, -odd, odd)


def add_weights(pencil, cell_ref, wave_ref, plane_ref, weights):
    doubled = jnp.concatenate(
        [weights[g : g + 1] * plane_ref[y : y + 1] for g in range(4) for y in range(2)]
    )
    waves = (wave_ref[...][:, None, :] * doubled[None]).reshape(128, LENGTH)
    cells = lax.broadcasted_iota(jnp.int32, (LENGTH, LENGTH), 0)
    chosen = jnp.where(cells == cell_ref[...], 1.0, 0.0).astype(BF16)
    high, low = split(waves)
    both = dot(chosen, jnp.concatenate([high, low]), NT)
    return pencil + both[:, :128] + both[:, 128:]


def wait_kernel(panel, *refs):
    cell_ref, wave_ref, plane_ref, pencil_ref = refs[:4]
    unknown_refs, refs = refs[4 : 4 + panel], refs[4 + panel :]
    weights = unknown_refs[-1][16:20]
    pencil = 0.0 if panel == 1 else pencil_ref[...]
    if panel == 3:
        pencil = pencil + swap_groups(refs[0][...].reshape(LENGTH, 128))
        refs[1][...] = add_weights(pencil, cell_ref, wave_ref, plane_ref, weights)
        return
    side_ref, factor_refs, (out_ref, work_ref) = refs[0], refs[1:-2], refs[-2:]
    out_ref[...] = add_weights(pencil, cell_ref, wave_ref, plane_ref, weights)
    work = side_ref[0]
    for ref, factor_ref in zip(unknown_refs, factor_refs):
        work = work - dot_nt(ref[...], factor_ref[...].reshape(128, LENGTH))
    work_ref[0] = work


def filter_kernel(
    pencil_ref, cell_ref, wave_ref, plane_ref, a_ref, b_ref, c_ref, d_ref,
    high_hbm, low_hbm, back_high_hbm, back_low_hbm, even_ref, odd_ref, out_ref,
    high_ref, low_ref, back_high_ref, back_low_ref, sems,
):
    sources = (high_hbm, low_hbm, back_high_hbm, back_low_hbm)
    places = (high_ref, low_ref, back_high_ref, back_low_ref)
    copies = [
        pltpu.make_async_copy(source, place, sems.at[number])
        for number, (source, place) in enumerate(zip(sources, places))
    ]
    for copy in copies:
        copy.start()
    weights = (a_ref[16:20] + b_ref[16:20]) + (c_ref[16:20] + d_ref[16:20])
    pencil = add_weights(pencil_ref[...], cell_ref, wave_ref, plane_ref, weights)
    copies[0].wait()
    copies[1].wait()
    freq = table_nn(high_ref[...], low_ref[...], pencil)
    real, imag = freq[:512], freq[512:]
    odd = odd_ref[...]
    real_out = even_ref[0:512] * real + odd * pltpu.roll(imag, 64, 1)
    imag_out = even_ref[512:1024] * imag - odd * pltpu.roll(real, 64, 1)
    copies[2].wait()
    copies[3].wait()
    back = table_nn(
        back_high_ref[...], back_low_ref[...], jnp.concatenate([real_out, imag_out])
    )
    out_ref[...] = swap_groups(back).reshape(64, 16, 128)


def close_kernel(slots_ref, high_ref, low_ref, out_ref, rows_ref):
    @pl.when(pl.program_id(0) == 0)
    def _():
        rows = jnp.transpose(slots_ref[...].reshape(LENGTH, 128))
        rows_high, rows_low = split(rows)
        rows_ref[0:128] = rows_high
        rows_ref[128:256] = rows_low

    both = dot(rows_ref[...], high_ref[...], NN)
    total = both[:128] + both[128:] + dot(rows_ref[0:128], low_ref[...], NN)
    out_ref[...] = total.reshape(out_ref.shape)


def update_kernel(
    first_panel, panels, index_ref, base_ref, factor_ref, unknown_ref, out_ref, high_ref, low_ref
):
    block = pl.program_id(0)

    @pl.when(block == 0)
    def _():
        for k in range(panels):
            high, low = split(unknown_ref[:, 16 * k : 16 * k + 16, :].reshape(128, LENGTH))
            high_ref[k] = high
            low_ref[k] = low

    own = index_ref[0] * 16
    row = lax.broadcasted_iota(jnp.int32, (128, LENGTH), 0) + block * 128
    col = lax.broadcasted_iota(jnp.int32, (128, LENGTH), 1)
    base = base_ref[...].reshape(128, 128)
    if first_panel == 0:
        base_row = lax.broadcasted_iota(jnp.int32, (128, 128), 0) + block * 128
        base = jnp.where(base_row < 64, 0.0, base)
    for step in range(panels):
        panel = first_panel + step
        rows = factor_ref[:, :, LENGTH * step : LENGTH * (step + 1)].reshape(128, LENGTH)
        mine = (row // 16 == panel) & (col == own + row % 16)
        rows = jnp.where(row < 64, jnp.where(mine, -1.0, 0.0), rows)
        rows_high, rows_low = split(rows)
        wide = dot(jnp.concatenate([rows_high, rows_low]), high_ref[step], NT)
        base = base - (wide[:128] + wide[128:] + dot(rows_high, low_ref[step], NT))
    out_ref[...] = base.reshape(8, 16, 128)


def spec(*shape):
    return pl.BlockSpec(shape, lambda *_: (0,) * len(shape))


def block_at(shape, place):
    return pl.BlockSpec(shape, lambda *_: place)


def cost(flops, moved):
    return pl.CostEstimate(flops=flops, bytes_accessed=moved, transcendentals=0)


def shape_of(*shape):
    return jax.ShapeDtypeStruct(shape, F32)


def call(body, name, in_specs, out_specs, out_shape, flops, moved, scratch=(), grid=1):
    return pl.pallas_call(
        body,
        grid=(grid,),
        in_specs=in_specs,
        out_specs=out_specs,
        out_shape=out_shape,
        scratch_shapes=scratch,
        compiler_params=LIMIT,
        cost_estimate=cost(flops, moved),
        name=name,
    )


def ring(size, step):
    return [(place, (place + step) % size) for place in range(size)]


def share(partial):
    total = partial + lax.ppermute(partial, "core", ring(2, 1))
    return [total] + [lax.ppermute(total, "x", ring(4, step)) for step in (1, 2, 3)]


def tie(*groups):
    flat = lax.optimization_barrier(tuple(group[at] for group, ats in groups for at in ats))
    flat = list(flat)
    for group, ats in groups:
        for at in ats:
            group[at] = flat.pop(0)


def update(first_panel, panels, index, base, factor, unknowns):
    return call(
        functools.partial(update_kernel, first_panel, panels),
        "update",
        [
            SMEM,
            pl.BlockSpec((8, 16, 128), lambda i: (i, 0, 0)),
            pl.BlockSpec((8, 16, panels * LENGTH), lambda i: (i, 0, first_panel // panels)),
        ]
        + [spec(8, 16 * panels, LENGTH)],
        pl.BlockSpec((8, 16, 128), lambda i: (i, 0, 0)),
        shape_of(32, 16, 128),
        3 * 2 * 512 * panels * LENGTH * 128,
        2_700_000 * panels,
        [pltpu.VMEM((panels, 128, LENGTH), BF16)] * 2,
        grid=4,
    )(index, base, factor, unknowns)


SMEM = pl.BlockSpec(memory_space=pltpu.SMEM)
ANY = pl.BlockSpec(memory_space=pl.ANY)
TABLE = pltpu.VMEM((LENGTH, LENGTH), BF16)


def per_device(factor, inverses, right_side, obs_cells, noise, spectrum):
    z_high, z_low = (jnp.asarray(t) for t in halves(z_table()))
    x_high, x_low = (jnp.asarray(t) for t in halves(x_table()))
    back_high, back_low = (jnp.asarray(t) for t in halves(x_table().T))
    wide = lax.axis_index(WIDE).astype(jnp.int32)
    index = jnp.stack([wide, lax.axis_index("y").astype(jnp.int32)])

    columns, side = call(
        columns_kernel,
        "columns",
        [spec(64, LENGTH), spec(4, 16, 128)],
        [spec(8, 64, 128), spec(64, 128)],
        [shape_of(8, 64, 128), shape_of(64, 128)],
        0,
        500_000,
    )(inverses.reshape(64, LENGTH), right_side)
    box = [columns, side, spectrum, factor]
    tie((box, (0, 1, 2, 3)))
    columns, side, spectrum, factor = box
    columns = lax.all_to_all(columns, ("x", "core"), 0, 0)

    lower = call(
        lower_kernel,
        "lower",
        [block_at((1, 16, LENGTH * k), (k, 0, 0)) for k in range(1, 4)],
        spec(96, LENGTH),
        shape_of(96, LENGTH),
        0,
        800_000,
    )(factor, factor, factor)
    lower = lax.all_gather(lower, "z")

    sides = [side] + [lax.ppermute(side, "y", ring(4, step)) for step in (1, 2, 3)]
    near, far = call(
        bundle_kernel,
        "bundle",
        [SMEM, spec(8, 64, 128)] + [spec(64, 128)] * 4,
        [spec(8, 288, 128), spec(8, 256, 128)],
        [shape_of(8, 288, 128), shape_of(8, 256, 128)],
        0,
        2_500_000,
    )(index, columns, *sides)
    box = [near, far, noise, spectrum, obs_cells]
    tie((box, (0, 1, 2, 3, 4)))
    near, far, noise, spectrum, obs_cells = box
    near = lax.all_to_all(near, "z", 0, 0)
    extra = lax.ppermute(spectrum[:, :, 0].T, WIDE, [(32, 0)])

    slab = call(
        noise_kernel,
        "noise",
        [spec(128, LENGTH)] + [pl.BlockSpec((256, LENGTH), lambda i: (i, 0))] * 2,
        pl.BlockSpec((16, 16, 128), lambda i: (i, 0, 0)),
        shape_of(64, 16, 128),
        3 * 2 * 128 * LENGTH * LENGTH,
        5_000_000,
        grid=4,
    )(noise.reshape(128, LENGTH), z_high, z_low)

    extra = jnp.concatenate([extra, jnp.zeros((6, LENGTH), F32)])
    even, odd = call(
        spectrum_kernel,
        "spectrum",
        [SMEM, spec(LENGTH, 32), spec(8, LENGTH)],
        [spec(LENGTH, 128), spec(512, 128)],
        [shape_of(LENGTH, 128), shape_of(512, 128)],
        300_000_000,
        1_500_000,
    )(index, spectrum.reshape(LENGTH, 32), extra)

    cell_x = (obs_cells // (8 * LENGTH)).reshape(1, 4096)
    plane = obs_cells // LENGTH % 8 - 2 * lax.axis_index("y")
    planes = jnp.stack([plane == 0, plane == 1]).astype(F32)
    freq, phase = z_frequencies(wide, jnp)
    turn = (freq[:, None] * (obs_cells % LENGTH)[None, :] + phase[:, None]) % LENGTH
    waves = jnp.cos(turn.astype(F32) * (2.0 * math.pi / LENGTH))
    box = [near, slab, even, odd, cell_x, planes, waves]
    tie((box, tuple(range(7))))
    near, slab, even, odd, cell_x, planes, waves = box

    obs_specs = lambda k: [
        block_at((1, LENGTH), (0, k)),
        block_at((16, LENGTH), (0, k)),
        block_at((2, LENGTH), (0, k)),
    ]
    side_spec = lambda k: block_at((1, COLS, 128), (k, 0, 0))
    factor_spec = lambda k, j: block_at((8, 16, LENGTH), (0, k * (k - 1) // 2 + j, 0))
    inverse_spec = lambda k: block_at((8, 128, 128), (0, k % 2, 0))
    panel_spec = spec(COLS, LENGTH)
    panel_shape = shape_of(COLS, LENGTH)
    pencil_spec = spec(LENGTH, 128)

    partial, sides = call(
        first_kernel,
        "first",
        [inverse_spec(0), block_at((8, 32, 128), (0, 8, 0))],
        [panel_spec, spec(4, COLS, 128)],
        [panel_shape, shape_of(4, COLS, 128)],
        20_000_000,
        1_200_000,
    )(near, near)
    parts = share(partial)
    box = [far]
    tie((parts, (1,)), (box, (0,)))
    far = lax.all_to_all(box[0], "z", 0, 0)
    unknowns = []
    work = sides
    pencil = waves
    for panel in range(1, 4):
        partial, unknown = call(
            step_kernel,
            f"step{panel}",
            [side_spec(1 if panel == 1 else 0)]
            + [panel_spec] * 4
            + [factor_spec(panel, panel - 1), inverse_spec(panel)],
            [panel_spec] * 2,
            [panel_shape] * 2,
            40_000_000,
            1_500_000,
        )(work, *parts, lower, near if panel == 1 else far)
        unknowns.append(unknown)
        parts = share(partial)
        if panel == 1:
            box = [slab]
            tie((parts, (1,)), (box, (0,)))
            slab = lax.all_to_all(box[0], WIDE, 0, 0)
        if panel == 2:
            early = lax.all_gather(jnp.concatenate([u[:16] for u in unknowns]), "z")
        later = panel < 3
        box = list(
            call(
                functools.partial(wait_kernel, panel),
                f"wait{panel}",
                obs_specs(panel - 1)
                + [spec(16, 128) if panel == 1 else pencil_spec]
                + [panel_spec] * panel
                + ([side_spec(panel + 1)] if later else [spec(64, 16, 128)])
                + [factor_spec(panel + 1, j) for j in range(panel)] * later,
                [pencil_spec] + [spec(1, COLS, 128)] * later,
                [shape_of(LENGTH, 128)] + [shape_of(1, COLS, 128)] * later,
                2 * 2 * 128 * LENGTH * LENGTH,
                1_500_000,
            )(
                cell_x, waves, planes, pencil, *unknowns, sides if later else slab,
                *[lower] * (panel * later),
            )
        )
        tie((parts, (0, 1, 2, 3)), (box, (0, 1) if later else (0,)))
        pencil, work = box[0], box[-1]

    slots = call(
        filter_kernel,
        "filter",
        [spec(LENGTH, 128)]
        + obs_specs(3)
        + [panel_spec] * 4
        + [ANY] * 4
        + [spec(LENGTH, 128), spec(512, 128)],
        spec(64, 16, 128),
        shape_of(64, 16, 128),
        8 * 2 * 128 * LENGTH * LENGTH,
        11_000_000,
        [TABLE] * 4 + [pltpu.SemaphoreType.DMA((4,))],
    )(pencil, cell_x, waves, planes, *parts, x_high, x_low, back_high, back_low, even, odd)
    late = (parts[0][:16] + parts[1][:16]) + (parts[2][:16] + parts[3][:16])
    late = lax.all_gather(jnp.concatenate([unknowns[2][:16], late]), "z")
    slots = lax.all_to_all(slots, WIDE, 0, 0)
    solved = update(0, 2, index, right_side, factor, early)
    slots, solved = lax.optimization_barrier((slots, solved))
    correction = call(
        close_kernel,
        "close",
        [spec(64, 16, 128)] + [pl.BlockSpec((LENGTH, 256), lambda i: (0, i))] * 2,
        pl.BlockSpec((16, 4, 2, 256), lambda i: (0, 0, 0, i)),
        shape_of(16, 4, 2, LENGTH),
        3 * 2 * 128 * LENGTH * LENGTH,
        5_500_000,
        [pltpu.VMEM((256, LENGTH), BF16)],
        grid=4,
    )(slots, z_high, z_low)
    solved, correction = lax.optimization_barrier((solved, correction))
    solved = update(2, 2, index, solved, factor, late)
    return (solved, correction)


def solution(mesh):
    grid = Mesh(mesh.devices.reshape(8, 4, 2, 4), ("z", "x", "core", "y"))
    return jax.shard_map(
        per_device,
        mesh=grid,
        in_specs=(
            P(None, WIDE, None),
            P(None, None, WIDE, None),
            P(None, WIDE, "y"),
            P(),
            P(WIDE, None, "y", None),
            P(None, "y", WIDE),
        ),
        out_specs=(P(None, WIDE, "y"), P(WIDE, None, "y", None)),
        check_vma=False,
    )
```

```python
import functools
import math

import jax
import jax.numpy as jnp
import numpy as np
from jax import lax
from jax.experimental import pallas as pl
from jax.experimental.pallas import tpu as pltpu
from jax.sharding import Mesh, PartitionSpec as P

F32 = jnp.float32
BF16 = jnp.bfloat16
WIDE = ("z", "x", "core")
LENGTH = 1024
COLS = 24
NN = (((1,), (0,)), ((), ()))
NT = (((1,), (1,)), ((), ()))
LIMIT = pltpu.CompilerParams(vmem_limit_bytes=56 * 1024 * 1024)


def halves(table):
    high = table.astype(np.float32).astype(jnp.bfloat16)
    low = (table - high.astype(np.float64)).astype(np.float32).astype(jnp.bfloat16)
    return (np.asarray(high), np.asarray(low))


def z_frequencies(owner, xp):
    step = xp.arange(16) % 8
    part = xp.arange(16) // 8
    freq = 16 * owner + step + xp.where(owner >= 32, 1, 0)
    lone = (owner == 0) & (step == 0) & (part == 1)
    return (xp.where(lone, 512, freq), xp.where(lone, 0, 256 * part))


def z_table():
    rows = []
    cells = np.arange(LENGTH)
    for owner in range(64):
        freq, phase = z_frequencies(np.int64(owner), np)
        turn = (freq[:, None] * cells[None, :] + phase[:, None]) % LENGTH
        rows.append(np.cos(2.0 * np.pi * turn / LENGTH))
    return np.concatenate(rows)


def x_table():
    cells = np.arange(LENGTH)
    freq = np.concatenate([np.arange(512), np.arange(512)])
    phase = np.repeat([0, 256], 512)
    freq[512], phase[512] = 512, 0
    turn = (freq[:, None] * cells[None, :] + phase[:, None]) % LENGTH
    return np.cos(2.0 * np.pi * turn / LENGTH)


def split(value):
    high = value.astype(BF16)
    low = (value - high.astype(F32)).astype(BF16)
    return (high, low)


def dot(left, right, dims):
    return lax.dot_general(left, right, dims, preferred_element_type=F32)


def dot_nt(left, right):
    left_high, left_low = split(left)
    right_high, right_low = split(right)
    rows = left.shape[0]
    both = dot(jnp.concatenate([left_high, left_low]), right_high, NT)
    return both[:rows] + both[rows:] + dot(left_high, right_low, NT)


def table_nn(high, low, value):
    value_high, value_low = split(value)
    cols = value.shape[1]
    both = dot(high, jnp.concatenate([value_high, value_low], axis=1), NN)
    return both[:, :cols] + both[:, cols:] + dot(low, value_high, NN)


def swap_groups(value):
    row = lax.broadcasted_iota(jnp.int32, value.shape, 0)
    lane = lax.broadcasted_iota(jnp.int32, value.shape, 1)
    for bit in range(4):
        step = 1 << bit
        row_bit = (row >> bit) & 1
        lane_bit = (lane >> (3 + bit)) & 1
        up = pltpu.roll(pltpu.roll(value, LENGTH - step, 0), 8 * step, 1)
        down = pltpu.roll(pltpu.roll(value, step, 0), 128 - 8 * step, 1)
        value = jnp.where(row_bit == lane_bit, value, jnp.where(lane_bit == 1, up, down))
    return value


def columns_kernel(inverse_ref, right_ref, out_ref, side_ref):
    side_ref[...] = right_ref[...].reshape(64, 128)
    lane = lax.broadcasted_iota(jnp.int32, (64, 128), 1) // 16
    for r in range(8):
        total = jnp.zeros((64, 128), F32)
        for z in range(8):
            piece = inverse_ref[:, 128 * z : 128 * z + 128]
            piece = pltpu.roll(piece, (16 * (z - r)) % 128, 1) if z != r else piece
            total = jnp.where(lane == z, piece, total)
        out_ref[r] = total


def noise_kernel(noise_ref, high_ref, low_ref, out_ref):
    noise_high, noise_low = split(noise_ref[...])
    both = dot(high_ref[...], jnp.concatenate([noise_high, noise_low]), NT)
    slots = both[:, :128] + both[:, 128:] + dot(low_ref[...], noise_high, NT)
    out_ref[...] = slots.reshape(16, 16, 128)


def lower_kernel(one_ref, two_ref, three_ref, out_ref):
    place = 0
    for k, ref in enumerate((one_ref, two_ref, three_ref)):
        for j in range(k + 1):
            out_ref[16 * place : 16 * place + 16] = ref[0, :, LENGTH * j : LENGTH * (j + 1)]
            place += 1


def bundle_kernel(index_ref, columns_ref, *refs):
    side_refs, out_ref = refs[:4], refs[4]
    lane = lax.broadcasted_iota(jnp.int32, (64, 128), 1)
    weights = jnp.zeros((64, 128), F32)
    for step, ref in enumerate(side_refs):
        y = lax.rem(index_ref[1] + 4 - step, 4)
        weights = jnp.where(lane == y + 16, ref[:, 0:1], weights)
    side = side_refs[0][...]
    quarter = columns_ref[pl.ds(2 * index_ref[1], 2)]
    quarter = [quarter[:, 32 * h : 32 * h + 32].reshape(64, 128) for h in range(2)]
    for z in range(8):
        own = pltpu.roll(side, (128 - 16 * z) % 128, 1) if z else side
        rows = jnp.where(lane < 16, own, weights)
        out_ref[z, 0:64] = quarter[0]
        out_ref[z, 64:128] = quarter[1]
        out_ref[z, 128:160] = jnp.transpose(jnp.concatenate([rows, rows]))[:32]


def spread(work, index_ref, inverse_refs, out_ref, high_ref, low_ref):
    for number, ref in enumerate(inverse_refs):
        y = lax.rem(index_ref[1] + 4 - number // 2, 4)
        start = pl.multiple_of(32 * y + 16 * (number % 2), 16)
        rows_high, rows_low = split(ref[...])
        high_ref[:, pl.ds(start, 16), :] = rows_high
        low_ref[:, pl.ds(start, 16), :] = rows_low
    high, low = split(work)
    rows_high = high_ref[...].reshape(LENGTH, 128)
    wide = dot(jnp.concatenate([high, low]), rows_high, NT)
    rows_low = low_ref[...].reshape(LENGTH, 128)
    out_ref[...] = wide[:COLS] + wide[COLS:] + dot(high, rows_low, NT)


def first_kernel(index_ref, slab_ref, *refs):
    inverse_refs, (out_ref, side_ref, high_ref, low_ref) = refs[:8], refs[8:]
    lane = lax.broadcasted_iota(jnp.int32, (COLS, 128), 1) // 16
    for k in range(4):
        rows = jnp.zeros((COLS, 128), F32)
        for z in range(8):
            piece = slab_ref[z, 0:COLS]
            turn = (16 * (z - k)) % 128
            piece = pltpu.roll(piece, turn, 1) if turn else piece
            rows = jnp.where(lane == z, piece, rows)
        side_ref[k] = rows
    spread(side_ref[0], index_ref, inverse_refs, out_ref, high_ref, low_ref)


def step_kernel(index_ref, start_ref, a_ref, b_ref, c_ref, d_ref, factor_ref, *refs):
    inverse_refs, (out_ref, unknown_ref, high_ref, low_ref) = refs[:8], refs[8:]
    unknown = (a_ref[...] + b_ref[...]) + (c_ref[...] + d_ref[...])
    unknown_ref[...] = unknown
    work = start_ref[0] - dot_nt(unknown, factor_ref[...].reshape(128, LENGTH))
    spread(work, index_ref, inverse_refs, out_ref, high_ref, low_ref)


def spectrum_kernel(index_ref, spectrum_ref, extra_ref, even_ref, odd_ref):
    owner = index_ref[0]
    row = lax.broadcasted_iota(jnp.int32, (32, 128), 0)
    lane = lax.broadcasted_iota(jnp.int32, (32, 128), 1)
    lone = (owner == 0) & (lane // 8 == 8)
    same_y = row // 16 == lane % 2
    same_z = row % 16 == (lane // 8) % 8 + jnp.where(owner >= 32, 1, 0)
    pick = jnp.where(same_y & same_z & jnp.logical_not(lone), 1.0, 0.0).astype(BF16)
    extra_pick = jnp.where(lone & (row == lane % 2), 1.0, 0.0)[:8].astype(BF16)

    def exact(value, choose):
        high = value.astype(BF16)
        rest = value - high.astype(F32)
        middle = rest.astype(BF16)
        low = (rest - middle.astype(F32)).astype(BF16)
        return choose(high) + (choose(middle) + choose(low))

    wanted = exact(spectrum_ref[...], lambda part: dot(part, pick, NN))
    wanted = wanted + exact(
        jnp.transpose(extra_ref[...]), lambda part: dot(part, extra_pick, NN)
    )
    at_row = lax.broadcasted_iota(jnp.int32, (512, 512), 0)
    at_col = lax.broadcasted_iota(jnp.int32, (512, 512), 1)
    mirror = jnp.where(at_row + at_col == 512, 1.0, 0.0).astype(BF16)
    plus = wanted[:512]
    upper = wanted[512:]
    minus = exact(upper, lambda part: dot(mirror, part, NN))
    first = lax.broadcasted_iota(jnp.int32, (512, 128), 0) == 0
    minus = jnp.where(first, plus, minus)
    lanes = lax.broadcasted_iota(jnp.int32, (512, 128), 1)
    alone = (owner == 0) & ((lanes // 8) % 8 == 0)
    scale = jnp.where(first, 1.0, 2.0) * jnp.where(alone, 1.0, 2.0) / (LENGTH * LENGTH)
    even = (plus + minus) * (0.5 * scale)
    even_ref[0:512] = even
    even_ref[512:1024] = jnp.where(first, upper * scale, even)
    odd = (plus - minus) * (0.5 * scale)
    odd_ref[...] = jnp.where(lanes < 64, -odd, odd)


def add_weights(pencil, cell_ref, wave_ref, plane_ref, weights):
    doubled = jnp.concatenate(
        [weights[g : g + 1] * plane_ref[y : y + 1] for g in range(4) for y in range(2)]
    )
    waves = (wave_ref[...][:, None, :] * doubled[None]).reshape(128, LENGTH)
    cells = lax.broadcasted_iota(jnp.int32, (LENGTH, LENGTH), 0)
    chosen = jnp.where(cells == cell_ref[...], 1.0, 0.0).astype(BF16)
    high, low = split(waves)
    both = dot(chosen, jnp.concatenate([high, low]), NT)
    return pencil + both[:, :128] + both[:, 128:]


def wait_kernel(panel, *refs):
    cell_ref, wave_ref, plane_ref, pencil_ref = refs[:4]
    unknown_refs, refs = refs[4 : 4 + panel], refs[4 + panel :]
    weights = unknown_refs[-1][16:20]
    pencil = 0.0 if panel == 1 else pencil_ref[...]
    if panel == 3:
        pencil = pencil + swap_groups(refs[0][...].reshape(LENGTH, 128))
        refs[1][...] = add_weights(pencil, cell_ref, wave_ref, plane_ref, weights)
        return
    side_ref, factor_refs, (out_ref, work_ref) = refs[0], refs[1:-2], refs[-2:]
    out_ref[...] = add_weights(pencil, cell_ref, wave_ref, plane_ref, weights)
    work = side_ref[0]
    for ref, factor_ref in zip(unknown_refs, factor_refs):
        work = work - dot_nt(ref[...], factor_ref[...].reshape(128, LENGTH))
    work_ref[0] = work


def filter_kernel(
    pencil_ref, cell_ref, wave_ref, plane_ref, a_ref, b_ref, c_ref, d_ref,
    high_hbm, low_hbm, back_high_hbm, back_low_hbm, even_ref, odd_ref, out_ref,
    high_ref, low_ref, back_high_ref, back_low_ref, sems,
):
    sources = (high_hbm, low_hbm, back_high_hbm, back_low_hbm)
    places = (high_ref, low_ref, back_high_ref, back_low_ref)
    copies = [
        pltpu.make_async_copy(source, place, sems.at[number])
        for number, (source, place) in enumerate(zip(sources, places))
    ]
    for copy in copies:
        copy.start()
    weights = (a_ref[16:20] + b_ref[16:20]) + (c_ref[16:20] + d_ref[16:20])
    pencil = add_weights(pencil_ref[...], cell_ref, wave_ref, plane_ref, weights)
    copies[0].wait()
    copies[1].wait()
    freq = table_nn(high_ref[...], low_ref[...], pencil)
    real, imag = freq[:512], freq[512:]
    odd = odd_ref[...]
    real_out = even_ref[0:512] * real + odd * pltpu.roll(imag, 64, 1)
    imag_out = even_ref[512:1024] * imag - odd * pltpu.roll(real, 64, 1)
    copies[2].wait()
    copies[3].wait()
    back = table_nn(
        back_high_ref[...], back_low_ref[...], jnp.concatenate([real_out, imag_out])
    )
    out_ref[...] = swap_groups(back).reshape(64, 16, 128)


def close_kernel(slots_ref, high_ref, low_ref, out_ref, rows_ref):
    @pl.when(pl.program_id(0) == 0)
    def _():
        rows = jnp.transpose(slots_ref[...].reshape(LENGTH, 128))
        rows_high, rows_low = split(rows)
        rows_ref[0:128] = rows_high
        rows_ref[128:256] = rows_low

    both = dot(rows_ref[...], high_ref[...], NN)
    total = both[:128] + both[128:] + dot(rows_ref[0:128], low_ref[...], NN)
    out_ref[...] = total.reshape(out_ref.shape)


def update_kernel(
    first_panel, panels, index_ref, base_ref, factor_ref, unknown_ref, out_ref, high_ref, low_ref
):
    block = pl.program_id(0)

    @pl.when(block == 0)
    def _():
        for k in range(panels):
            high, low = split(unknown_ref[:, 16 * k : 16 * k + 16, :].reshape(128, LENGTH))
            high_ref[k] = high
            low_ref[k] = low

    own = index_ref[0] * 16
    row = lax.broadcasted_iota(jnp.int32, (128, LENGTH), 0) + block * 128
    col = lax.broadcasted_iota(jnp.int32, (128, LENGTH), 1)
    base = base_ref[...].reshape(128, 128)
    if first_panel == 0:
        base_row = lax.broadcasted_iota(jnp.int32, (128, 128), 0) + block * 128
        base = jnp.where(base_row < 64, 0.0, base)
    for step in range(panels):
        panel = first_panel + step
        rows = factor_ref[:, :, LENGTH * step : LENGTH * (step + 1)].reshape(128, LENGTH)
        mine = (row // 16 == panel) & (col == own + row % 16)
        rows = jnp.where(row < 64, jnp.where(mine, -1.0, 0.0), rows)
        rows_high, rows_low = split(rows)
        wide = dot(jnp.concatenate([rows_high, rows_low]), high_ref[step], NT)
        base = base - (wide[:128] + wide[128:] + dot(rows_high, low_ref[step], NT))
    out_ref[...] = base.reshape(8, 16, 128)


def spec(*shape):
    return pl.BlockSpec(shape, lambda *_: (0,) * len(shape))


def block_at(shape, place):
    return pl.BlockSpec(shape, lambda *_: place)


def cost(flops, moved):
    return pl.CostEstimate(flops=flops, bytes_accessed=moved, transcendentals=0)


def shape_of(*shape):
    return jax.ShapeDtypeStruct(shape, F32)


def call(body, name, in_specs, out_specs, out_shape, flops, moved, scratch=(), grid=1):
    return pl.pallas_call(
        body,
        grid=(grid,),
        in_specs=in_specs,
        out_specs=out_specs,
        out_shape=out_shape,
        scratch_shapes=scratch,
        compiler_params=LIMIT,
        cost_estimate=cost(flops, moved),
        name=name,
    )


def ring(size, step):
    return [(place, (place + step) % size) for place in range(size)]


def share(partial):
    total = partial + lax.ppermute(partial, "core", ring(2, 1))
    return [total] + [lax.ppermute(total, "x", ring(4, step)) for step in (1, 2, 3)]


def tie(*groups):
    flat = lax.optimization_barrier(tuple(group[at] for group, ats in groups for at in ats))
    flat = list(flat)
    for group, ats in groups:
        for at in ats:
            group[at] = flat.pop(0)


def update(first_panel, panels, index, base, factor, unknowns):
    return call(
        functools.partial(update_kernel, first_panel, panels),
        "update",
        [
            SMEM,
            pl.BlockSpec((8, 16, 128), lambda i: (i, 0, 0)),
            pl.BlockSpec((8, 16, panels * LENGTH), lambda i: (i, 0, first_panel // panels)),
        ]
        + [spec(8, 16 * panels, LENGTH)],
        pl.BlockSpec((8, 16, 128), lambda i: (i, 0, 0)),
        shape_of(32, 16, 128),
        3 * 2 * 512 * panels * LENGTH * 128,
        2_700_000 * panels,
        [pltpu.VMEM((panels, 128, LENGTH), BF16)] * 2,
        grid=4,
    )(index, base, factor, unknowns)


SMEM = pl.BlockSpec(memory_space=pltpu.SMEM)
ANY = pl.BlockSpec(memory_space=pl.ANY)
TABLE = pltpu.VMEM((LENGTH, LENGTH), BF16)


def per_device(factor, inverses, right_side, obs_cells, noise, spectrum):
    z_high, z_low = (jnp.asarray(t) for t in halves(z_table()))
    x_high, x_low = (jnp.asarray(t) for t in halves(x_table()))
    back_high, back_low = (jnp.asarray(t) for t in halves(x_table().T))
    wide = lax.axis_index(WIDE).astype(jnp.int32)
    index = jnp.stack([wide, lax.axis_index("y").astype(jnp.int32)])

    columns, side = call(
        columns_kernel,
        "columns",
        [spec(64, LENGTH), spec(4, 16, 128)],
        [spec(8, 64, 128), spec(64, 128)],
        [shape_of(8, 64, 128), shape_of(64, 128)],
        0,
        500_000,
    )(inverses.reshape(64, LENGTH), right_side)
    box = [columns, side, factor]
    tie((box, (0, 1, 2)))
    columns, side, factor = box
    columns = lax.all_to_all(columns, ("x", "core"), 0, 0)
    extra = lax.ppermute(spectrum[:, :, 0].T, WIDE, [(32, 0)])
    box = [columns, extra]
    tie((box, (0, 1)))
    columns, extra = box

    lower = call(
        lower_kernel,
        "lower",
        [block_at((1, 16, LENGTH * k), (k, 0, 0)) for k in range(1, 4)],
        spec(96, LENGTH),
        shape_of(96, LENGTH),
        0,
        800_000,
    )(factor, factor, factor)
    lower = lax.all_gather(lower, "z")

    sides = [side] + [lax.ppermute(side, "y", ring(4, step)) for step in (1, 2, 3)]
    quarter = call(
        bundle_kernel,
        "bundle",
        [SMEM, spec(8, 64, 128)] + [spec(64, 128)] * 4,
        spec(8, 160, 128),
        shape_of(8, 160, 128),
        0,
        1_500_000,
    )(index, columns, *sides)
    box = [quarter, noise, spectrum, obs_cells]
    tie((box, (0, 1, 2, 3)))
    quarter, noise, spectrum, obs_cells = box
    quarter = lax.all_to_all(quarter, "z", 0, 0)

    slab = call(
        noise_kernel,
        "noise",
        [spec(128, LENGTH)] + [pl.BlockSpec((256, LENGTH), lambda i: (i, 0))] * 2,
        pl.BlockSpec((16, 16, 128), lambda i: (i, 0, 0)),
        shape_of(64, 16, 128),
        3 * 2 * 128 * LENGTH * LENGTH,
        5_000_000,
        grid=4,
    )(noise.reshape(128, LENGTH), z_high, z_low)

    extra = jnp.concatenate([extra, jnp.zeros((6, LENGTH), F32)])
    even, odd = call(
        spectrum_kernel,
        "spectrum",
        [SMEM, spec(LENGTH, 32), spec(8, LENGTH)],
        [spec(LENGTH, 128), spec(512, 128)],
        [shape_of(LENGTH, 128), shape_of(512, 128)],
        300_000_000,
        1_500_000,
    )(index, spectrum.reshape(LENGTH, 32), extra)

    cell_x = (obs_cells // (8 * LENGTH)).reshape(1, 4096)
    plane = obs_cells // LENGTH % 8 - 2 * lax.axis_index("y")
    planes = jnp.stack([plane == 0, plane == 1]).astype(F32)
    freq, phase = z_frequencies(wide, jnp)
    turn = (freq[:, None] * (obs_cells % LENGTH)[None, :] + phase[:, None]) % LENGTH
    waves = jnp.cos(turn.astype(F32) * (2.0 * math.pi / LENGTH))
    box = [quarter, slab, even, odd, cell_x, planes, waves]
    tie((box, tuple(range(7))))
    quarter, slab, even, odd, cell_x, planes, waves = box
    own = [quarter[:, 0:64], quarter[:, 64:128]]
    own = [[one] + [lax.ppermute(one, "y", ring(4, step)) for step in (1, 2, 3)] for one in own]
    slab = lax.all_to_all(slab, WIDE, 0, 0)

    obs_specs = lambda k: [
        block_at((1, LENGTH), (0, k)),
        block_at((16, LENGTH), (0, k)),
        block_at((2, LENGTH), (0, k)),
    ]
    side_spec = lambda k: block_at((1, COLS, 128), (k, 0, 0))
    factor_spec = lambda k, j: block_at((8, 16, LENGTH), (0, k * (k - 1) // 2 + j, 0))
    inverse_specs = lambda k: [block_at((8, 16, 128), (0, k % 2 + a, 0)) for a in (0, 2)] * 4
    inverses = [[one for one in own[k // 2] for _ in range(2)] for k in range(4)]
    inverse_scratch = [pltpu.VMEM((8, 128, 128), BF16)] * 2
    panel_spec = spec(COLS, LENGTH)
    panel_shape = shape_of(COLS, LENGTH)
    pencil_spec = spec(LENGTH, 128)

    partial, sides = call(
        first_kernel,
        "first",
        [SMEM, block_at((8, 32, 128), (0, 4, 0))] + inverse_specs(0),
        [panel_spec, spec(4, COLS, 128)],
        [panel_shape, shape_of(4, COLS, 128)],
        20_000_000,
        1_200_000,
        inverse_scratch,
    )(index, quarter, *inverses[0])
    parts = share(partial)
    unknowns = []
    work = sides
    pencil = waves
    for panel in range(1, 4):
        partial, unknown = call(
            step_kernel,
            f"step{panel}",
            [SMEM, side_spec(1 if panel == 1 else 0)]
            + [panel_spec] * 4
            + [factor_spec(panel, panel - 1)]
            + inverse_specs(panel),
            [panel_spec] * 2,
            [panel_shape] * 2,
            40_000_000,
            1_500_000,
            inverse_scratch,
        )(index, work, *parts, lower, *inverses[panel])
        unknowns.append(unknown)
        parts = share(partial)
        if panel == 3:
            early = lax.all_gather(jnp.concatenate([u[:16] for u in unknowns]), "z")
        later = panel < 3
        box = list(
            call(
                functools.partial(wait_kernel, panel),
                f"wait{panel}",
                obs_specs(panel - 1)
                + [spec(16, 128) if panel == 1 else pencil_spec]
                + [panel_spec] * panel
                + ([side_spec(panel + 1)] if later else [spec(64, 16, 128)])
                + [factor_spec(panel + 1, j) for j in range(panel)] * later,
                [pencil_spec] + [spec(1, COLS, 128)] * later,
                [shape_of(LENGTH, 128)] + [shape_of(1, COLS, 128)] * later,
                2 * 2 * 128 * LENGTH * LENGTH,
                1_500_000,
            )(
                cell_x, waves, planes, pencil, *unknowns, sides if later else slab,
                *[lower] * (panel * later),
            )
        )
        tie((parts, (0, 1, 2, 3)), (box, (0, 1) if later else (0,)))
        pencil, work = box[0], box[-1]

    slots = call(
        filter_kernel,
        "filter",
        [spec(LENGTH, 128)]
        + obs_specs(3)
        + [panel_spec] * 4
        + [ANY] * 4
        + [spec(LENGTH, 128), spec(512, 128)],
        spec(64, 16, 128),
        shape_of(64, 16, 128),
        8 * 2 * 128 * LENGTH * LENGTH,
        11_000_000,
        [TABLE] * 4 + [pltpu.SemaphoreType.DMA((4,))],
    )(pencil, cell_x, waves, planes, *parts, x_high, x_low, back_high, back_low, even, odd)
    late = (parts[0][:16] + parts[1][:16]) + (parts[2][:16] + parts[3][:16])
    late = lax.all_gather(jnp.concatenate([late, jnp.zeros((16, LENGTH), F32)]), "z")
    slots = lax.all_to_all(slots, WIDE, 0, 0)
    solved = update(0, 3, index, right_side, factor, early)
    slots, solved = lax.optimization_barrier((slots, solved))
    correction = call(
        close_kernel,
        "close",
        [spec(64, 16, 128)] + [pl.BlockSpec((LENGTH, 256), lambda i: (0, i))] * 2,
        pl.BlockSpec((16, 4, 2, 256), lambda i: (0, 0, 0, i)),
        shape_of(16, 4, 2, LENGTH),
        3 * 2 * 128 * LENGTH * LENGTH,
        5_500_000,
        [pltpu.VMEM((256, LENGTH), BF16)],
        grid=4,
    )(slots, z_high, z_low)
    solved, correction = lax.optimization_barrier((solved, correction))
    solved = update(3, 1, index, solved, factor, late)
    return (solved, correction)


def solution(mesh):
    grid = Mesh(mesh.devices.reshape(8, 4, 2, 4), ("z", "x", "core", "y"))
    return jax.shard_map(
        per_device,
        mesh=grid,
        in_specs=(
            P(None, WIDE, None),
            P(None, None, WIDE, None),
            P(None, WIDE, "y"),
            P(),
            P(WIDE, None, "y", None),
            P(None, "y", WIDE),
        ),
        out_specs=(P(None, WIDE, "y"), P(WIDE, None, "y", None)),
        check_vma=False,
    )
```

```python
import functools
import math

import jax
import jax.numpy as jnp
import numpy as np
from jax import lax
from jax.experimental import pallas as pl
from jax.experimental.pallas import tpu as pltpu
from jax.sharding import Mesh, PartitionSpec as P

F32 = jnp.float32
BF16 = jnp.bfloat16
WIDE = ("z", "x", "core")
LENGTH = 1024
COLS = 24
NN = (((1,), (0,)), ((), ()))
NT = (((1,), (1,)), ((), ()))
LIMIT = pltpu.CompilerParams(vmem_limit_bytes=56 * 1024 * 1024)


def halves(table):
    high = table.astype(np.float32).astype(jnp.bfloat16)
    low = (table - high.astype(np.float64)).astype(np.float32).astype(jnp.bfloat16)
    return (np.asarray(high), np.asarray(low))


def z_frequencies(owner, xp):
    step = xp.arange(16) % 8
    part = xp.arange(16) // 8
    freq = 16 * owner + step + xp.where(owner >= 32, 1, 0)
    lone = (owner == 0) & (step == 0) & (part == 1)
    return (xp.where(lone, 512, freq), xp.where(lone, 0, 256 * part))


def z_table():
    rows = []
    cells = np.arange(LENGTH)
    for owner in range(64):
        freq, phase = z_frequencies(np.int64(owner), np)
        turn = (freq[:, None] * cells[None, :] + phase[:, None]) % LENGTH
        rows.append(np.cos(2.0 * np.pi * turn / LENGTH))
    return np.concatenate(rows)


def x_table():
    cells = np.arange(LENGTH)
    freq = np.concatenate([np.arange(512), np.arange(512)])
    phase = np.repeat([0, 256], 512)
    freq[512], phase[512] = 512, 0
    turn = (freq[:, None] * cells[None, :] + phase[:, None]) % LENGTH
    return np.cos(2.0 * np.pi * turn / LENGTH)


def split(value):
    high = value.astype(BF16)
    low = (value - high.astype(F32)).astype(BF16)
    return (high, low)


def dot(left, right, dims):
    return lax.dot_general(left, right, dims, preferred_element_type=F32)


def dot_nt(left, right):
    left_high, left_low = split(left)
    right_high, right_low = split(right)
    rows = left.shape[0]
    both = dot(jnp.concatenate([left_high, left_low]), right_high, NT)
    return both[:rows] + both[rows:] + dot(left_high, right_low, NT)


def table_nn(high, low, value):
    value_high, value_low = split(value)
    cols = value.shape[1]
    both = dot(high, jnp.concatenate([value_high, value_low], axis=1), NN)
    return both[:, :cols] + both[:, cols:] + dot(low, value_high, NN)


def swap_groups(value):
    row = lax.broadcasted_iota(jnp.int32, value.shape, 0)
    lane = lax.broadcasted_iota(jnp.int32, value.shape, 1)
    for bit in range(4):
        step = 1 << bit
        row_bit = (row >> bit) & 1
        lane_bit = (lane >> (3 + bit)) & 1
        up = pltpu.roll(pltpu.roll(value, LENGTH - step, 0), 8 * step, 1)
        down = pltpu.roll(pltpu.roll(value, step, 0), 128 - 8 * step, 1)
        value = jnp.where(row_bit == lane_bit, value, jnp.where(lane_bit == 1, up, down))
    return value


def columns_kernel(inverse_ref, right_ref, out_ref, side_ref):
    side_ref[...] = right_ref[...].reshape(64, 128)
    lane = lax.broadcasted_iota(jnp.int32, (64, 128), 1) // 16
    for r in range(8):
        total = jnp.zeros((64, 128), F32)
        for z in range(8):
            piece = inverse_ref[:, 128 * z : 128 * z + 128]
            piece = pltpu.roll(piece, (16 * (z - r)) % 128, 1) if z != r else piece
            total = jnp.where(lane == z, piece, total)
        out_ref[r] = total


def noise_kernel(noise_ref, high_ref, low_ref, out_ref):
    noise_high, noise_low = split(noise_ref[...])
    both = dot(high_ref[...], jnp.concatenate([noise_high, noise_low]), NT)
    slots = both[:, :128] + both[:, 128:] + dot(low_ref[...], noise_high, NT)
    out_ref[...] = slots.reshape(16, 16, 128)


def lower_kernel(one_ref, two_ref, three_ref, out_ref):
    place = 0
    for k, ref in enumerate((one_ref, two_ref, three_ref)):
        for j in range(k + 1):
            out_ref[16 * place : 16 * place + 16] = ref[0, :, LENGTH * j : LENGTH * (j + 1)]
            place += 1


def bundle_kernel(index_ref, columns_ref, *refs):
    side_refs, extra_ref, out_ref = refs[:4], refs[4], refs[5]
    lane = lax.broadcasted_iota(jnp.int32, (64, 128), 1)
    weights = jnp.zeros((64, 128), F32)
    for step, ref in enumerate(side_refs):
        y = lax.rem(index_ref[1] + 4 - step, 4)
        weights = jnp.where(lane == y + 16, ref[:, 0:1], weights)
    side = side_refs[0][...]
    quarter = columns_ref[pl.ds(2 * index_ref[1], 2)]
    quarter = [quarter[:, 32 * h : 32 * h + 32].reshape(64, 128) for h in range(2)]
    for z in range(8):
        own = pltpu.roll(side, (128 - 16 * z) % 128, 1) if z else side
        rows = jnp.where(lane < 16, own, weights)
        out_ref[z, 0:64] = quarter[0]
        out_ref[z, 64:128] = quarter[1]
        out_ref[z, 128:160] = jnp.transpose(jnp.concatenate([rows, rows]))[:32]
        out_ref[z, 160:176] = extra_ref[...]


def spread(work, index_ref, inverse_refs, out_ref, high_ref, low_ref):
    for number, ref in enumerate(inverse_refs):
        y = lax.rem(index_ref[1] + 4 - number // 2, 4)
        start = pl.multiple_of(32 * y + 16 * (number % 2), 16)
        rows_high, rows_low = split(ref[...])
        high_ref[:, pl.ds(start, 16), :] = rows_high
        low_ref[:, pl.ds(start, 16), :] = rows_low
    high, low = split(work)
    rows_high = high_ref[...].reshape(LENGTH, 128)
    wide = dot(jnp.concatenate([high, low]), rows_high, NT)
    rows_low = low_ref[...].reshape(LENGTH, 128)
    out_ref[...] = wide[:COLS] + wide[COLS:] + dot(high, rows_low, NT)


def first_kernel(index_ref, slab_ref, *refs):
    inverse_refs, (out_ref, side_ref, high_ref, low_ref) = refs[:8], refs[8:]
    lane = lax.broadcasted_iota(jnp.int32, (COLS, 128), 1) // 16
    for k in range(4):
        rows = jnp.zeros((COLS, 128), F32)
        for z in range(8):
            piece = slab_ref[z, 0:COLS]
            turn = (16 * (z - k)) % 128
            piece = pltpu.roll(piece, turn, 1) if turn else piece
            rows = jnp.where(lane == z, piece, rows)
        side_ref[k] = rows
    spread(side_ref[0], index_ref, inverse_refs, out_ref, high_ref, low_ref)


def step_kernel(panel, index_ref, start_ref, a_ref, b_ref, c_ref, d_ref, factor_ref, *refs):
    inverse_refs, refs = refs[:8], refs[8:]
    unknown = (a_ref[...] + b_ref[...]) + (c_ref[...] + d_ref[...])
    if panel == 2:
        older_ref, refs = refs[0], refs[1:]
        refs[2][0:16] = older_ref[0:16]
        refs[2][16:32] = unknown[0:16]
    out_ref, unknown_ref, high_ref, low_ref = refs[0], refs[1], refs[-2], refs[-1]
    unknown_ref[...] = unknown
    work = start_ref[0] - dot_nt(unknown, factor_ref[...].reshape(128, LENGTH))
    spread(work, index_ref, inverse_refs, out_ref, high_ref, low_ref)


def spectrum_kernel(index_ref, spectrum_ref, extra_ref, even_ref, odd_ref):
    owner = index_ref[0]
    row = lax.broadcasted_iota(jnp.int32, (32, 128), 0)
    lane = lax.broadcasted_iota(jnp.int32, (32, 128), 1)
    lone = (owner == 0) & (lane // 8 == 8)
    same_y = row // 16 == lane % 2
    same_z = row % 16 == (lane // 8) % 8 + jnp.where(owner >= 32, 1, 0)
    pick = jnp.where(same_y & same_z & jnp.logical_not(lone), 1.0, 0.0).astype(BF16)
    extra_pick = jnp.where(lone & (row == lane % 2), 1.0, 0.0)[:8].astype(BF16)

    def exact(value, choose):
        high = value.astype(BF16)
        rest = value - high.astype(F32)
        middle = rest.astype(BF16)
        low = (rest - middle.astype(F32)).astype(BF16)
        return choose(high) + (choose(middle) + choose(low))

    wanted = exact(spectrum_ref[...], lambda part: dot(part, pick, NN))
    extra = [
        jnp.concatenate([extra_ref[0, 8 * y + t : 8 * y + t + 1] for t in range(8)], axis=1)
        for y in range(2)
    ]
    extra = jnp.concatenate(extra + [jnp.zeros((6, LENGTH), F32)])
    wanted = wanted + exact(jnp.transpose(extra), lambda part: dot(part, extra_pick, NN))
    at_row = lax.broadcasted_iota(jnp.int32, (512, 512), 0)
    at_col = lax.broadcasted_iota(jnp.int32, (512, 512), 1)
    mirror = jnp.where(at_row + at_col == 512, 1.0, 0.0).astype(BF16)
    plus = wanted[:512]
    upper = wanted[512:]
    minus = exact(upper, lambda part: dot(mirror, part, NN))
    first = lax.broadcasted_iota(jnp.int32, (512, 128), 0) == 0
    minus = jnp.where(first, plus, minus)
    lanes = lax.broadcasted_iota(jnp.int32, (512, 128), 1)
    alone = (owner == 0) & ((lanes // 8) % 8 == 0)
    scale = jnp.where(first, 1.0, 2.0) * jnp.where(alone, 1.0, 2.0) / (LENGTH * LENGTH)
    even = (plus + minus) * (0.5 * scale)
    even_ref[0:512] = even
    even_ref[512:1024] = jnp.where(first, upper * scale, even)
    odd = (plus - minus) * (0.5 * scale)
    odd_ref[...] = jnp.where(lanes < 64, -odd, odd)


def add_weights(pencil, cell_ref, wave_ref, plane_ref, weights):
    doubled = jnp.concatenate(
        [weights[g : g + 1] * plane_ref[y : y + 1] for g in range(4) for y in range(2)]
    )
    waves = (wave_ref[...][:, None, :] * doubled[None]).reshape(128, LENGTH)
    cells = lax.broadcasted_iota(jnp.int32, (LENGTH, LENGTH), 0)
    chosen = jnp.where(cells == cell_ref[...], 1.0, 0.0).astype(BF16)
    high, low = split(waves)
    both = dot(chosen, jnp.concatenate([high, low]), NT)
    return pencil + both[:, :128] + both[:, 128:]


def wait_kernel(panel, *refs):
    cell_ref, wave_ref, plane_ref, pencil_ref = refs[:4]
    unknown_refs, refs = refs[4 : 4 + panel], refs[4 + panel :]
    weights = unknown_refs[-1][16:20]
    pencil = pencil_ref[...].reshape(LENGTH, 128)
    pencil = swap_groups(pencil) if panel == 1 else pencil
    pencil = add_weights(pencil, cell_ref, wave_ref, plane_ref, weights)
    if panel == 3:
        refs[0][...] = pencil
        return
    side_ref, factor_refs, (out_ref, work_ref) = refs[0], refs[1:-2], refs[-2:]
    out_ref[...] = pencil
    work = side_ref[0]
    for ref, factor_ref in zip(unknown_refs, factor_refs):
        work = work - dot_nt(ref[...], factor_ref[...].reshape(128, LENGTH))
    work_ref[0] = work


def filter_kernel(
    pencil_ref, cell_ref, wave_ref, plane_ref, a_ref, b_ref, c_ref, d_ref,
    high_hbm, low_hbm, back_high_hbm, back_low_hbm, even_ref, odd_ref, out_ref,
    high_ref, low_ref, back_high_ref, back_low_ref, sems,
):
    sources = (high_hbm, low_hbm, back_high_hbm, back_low_hbm)
    places = (high_ref, low_ref, back_high_ref, back_low_ref)
    copies = [
        pltpu.make_async_copy(source, place, sems.at[number])
        for number, (source, place) in enumerate(zip(sources, places))
    ]
    for copy in copies:
        copy.start()
    weights = (a_ref[16:20] + b_ref[16:20]) + (c_ref[16:20] + d_ref[16:20])
    pencil = add_weights(pencil_ref[...], cell_ref, wave_ref, plane_ref, weights)
    copies[0].wait()
    copies[1].wait()
    freq = table_nn(high_ref[...], low_ref[...], pencil)
    real, imag = freq[:512], freq[512:]
    odd = odd_ref[...]
    real_out = even_ref[0:512] * real + odd * pltpu.roll(imag, 64, 1)
    imag_out = even_ref[512:1024] * imag - odd * pltpu.roll(real, 64, 1)
    copies[2].wait()
    copies[3].wait()
    back = table_nn(
        back_high_ref[...], back_low_ref[...], jnp.concatenate([real_out, imag_out])
    )
    out_ref[...] = swap_groups(back).reshape(64, 16, 128)


def close_kernel(slots_ref, high_ref, low_ref, out_ref, rows_ref):
    @pl.when(pl.program_id(0) == 0)
    def _():
        rows = jnp.transpose(slots_ref[...].reshape(LENGTH, 128))
        rows_high, rows_low = split(rows)
        rows_ref[0:128] = rows_high
        rows_ref[128:256] = rows_low

    both = dot(rows_ref[...], high_ref[...], NN)
    total = both[:128] + both[128:] + dot(rows_ref[0:128], low_ref[...], NN)
    out_ref[...] = total.reshape(out_ref.shape)


def update_kernel(
    first_panel, panels, index_ref, base_ref, factor_ref, unknown_ref, out_ref, high_ref, low_ref
):
    block = pl.program_id(0)

    @pl.when(block == 0)
    def _():
        for k in range(panels):
            high, low = split(unknown_ref[:, 16 * k : 16 * k + 16, :].reshape(128, LENGTH))
            high_ref[k] = high
            low_ref[k] = low

    own = index_ref[0] * 16
    row = lax.broadcasted_iota(jnp.int32, (128, LENGTH), 0) + block * 128
    col = lax.broadcasted_iota(jnp.int32, (128, LENGTH), 1)
    base = base_ref[...].reshape(128, 128)
    if first_panel == 0:
        base_row = lax.broadcasted_iota(jnp.int32, (128, 128), 0) + block * 128
        base = jnp.where(base_row < 64, 0.0, base)
    for step in range(panels):
        panel = first_panel + step
        rows = factor_ref[:, :, LENGTH * step : LENGTH * (step + 1)].reshape(128, LENGTH)
        mine = (row // 16 == panel) & (col == own + row % 16)
        rows = jnp.where(row < 64, jnp.where(mine, -1.0, 0.0), rows)
        rows_high, rows_low = split(rows)
        wide = dot(jnp.concatenate([rows_high, rows_low]), high_ref[step], NT)
        base = base - (wide[:128] + wide[128:] + dot(rows_high, low_ref[step], NT))
    out_ref[...] = base.reshape(8, 16, 128)


def spec(*shape):
    return pl.BlockSpec(shape, lambda *_: (0,) * len(shape))


def block_at(shape, place):
    return pl.BlockSpec(shape, lambda *_: place)


def cost(flops, moved):
    return pl.CostEstimate(flops=flops, bytes_accessed=moved, transcendentals=0)


def shape_of(*shape):
    return jax.ShapeDtypeStruct(shape, F32)


def call(body, name, in_specs, out_specs, out_shape, flops, moved, scratch=(), grid=1):
    return pl.pallas_call(
        body,
        grid=(grid,),
        in_specs=in_specs,
        out_specs=out_specs,
        out_shape=out_shape,
        scratch_shapes=scratch,
        compiler_params=LIMIT,
        cost_estimate=cost(flops, moved),
        name=name,
    )


def ring(size, step):
    return [(place, (place + step) % size) for place in range(size)]


def share(partial):
    total = partial + lax.ppermute(partial, "core", ring(2, 1))
    return [total] + [lax.ppermute(total, "x", ring(4, step)) for step in (1, 2, 3)]


def tie(*groups):
    flat = lax.optimization_barrier(tuple(group[at] for group, ats in groups for at in ats))
    flat = list(flat)
    for group, ats in groups:
        for at in ats:
            group[at] = flat.pop(0)


def update(first_panel, panels, index, base, factor, unknowns):
    return call(
        functools.partial(update_kernel, first_panel, panels),
        "update",
        [
            SMEM,
            pl.BlockSpec((8, 16, 128), lambda i: (i, 0, 0)),
            pl.BlockSpec((8, 16, panels * LENGTH), lambda i: (i, 0, first_panel // panels)),
        ]
        + [spec(8, 16 * panels, LENGTH)],
        pl.BlockSpec((8, 16, 128), lambda i: (i, 0, 0)),
        shape_of(32, 16, 128),
        3 * 2 * 512 * panels * LENGTH * 128,
        2_700_000 * panels,
        [pltpu.VMEM((panels, 128, LENGTH), BF16)] * 2,
        grid=4,
    )(index, base, factor, unknowns)


SMEM = pl.BlockSpec(memory_space=pltpu.SMEM)
ANY = pl.BlockSpec(memory_space=pl.ANY)
TABLE = pltpu.VMEM((LENGTH, LENGTH), BF16)


def per_device(factor, inverses, right_side, obs_cells, noise, spectrum):
    z_high, z_low = (jnp.asarray(t) for t in halves(z_table()))
    x_high, x_low = (jnp.asarray(t) for t in halves(x_table()))
    back_high, back_low = (jnp.asarray(t) for t in halves(x_table().T))
    wide = lax.axis_index(WIDE).astype(jnp.int32)
    index = jnp.stack([wide, lax.axis_index("y").astype(jnp.int32)])

    columns, side = call(
        columns_kernel,
        "columns",
        [spec(64, LENGTH), spec(4, 16, 128)],
        [spec(8, 64, 128), spec(64, 128)],
        [shape_of(8, 64, 128), shape_of(64, 128)],
        0,
        500_000,
    )(inverses.reshape(64, LENGTH), right_side)
    box = [columns, side, factor]
    tie((box, (0, 1, 2)))
    columns, side, factor = box
    columns = lax.all_to_all(columns, ("x", "core"), 0, 0)
    extra = spectrum[:, :, 0].T.reshape(16, 128)

    lower = call(
        lower_kernel,
        "lower",
        [block_at((1, 16, LENGTH * k), (k, 0, 0)) for k in range(1, 4)],
        spec(96, LENGTH),
        shape_of(96, LENGTH),
        0,
        800_000,
    )(factor, factor, factor)
    lower = lax.all_gather(lower, "z")

    sides = [side] + [lax.ppermute(side, "y", ring(4, step)) for step in (1, 2, 3)]
    quarter = call(
        bundle_kernel,
        "bundle",
        [SMEM, spec(8, 64, 128)] + [spec(64, 128)] * 4 + [spec(16, 128)],
        spec(8, 176, 128),
        shape_of(8, 176, 128),
        0,
        1_500_000,
    )(index, columns, *sides, extra)
    box = [quarter, noise, spectrum, obs_cells]
    tie((box, (0, 1, 2, 3)))
    quarter, noise, spectrum, obs_cells = box
    quarter = lax.all_to_all(quarter, "z", 0, 0)

    slab = call(
        noise_kernel,
        "noise",
        [spec(128, LENGTH)] + [pl.BlockSpec((256, LENGTH), lambda i: (i, 0))] * 2,
        pl.BlockSpec((16, 16, 128), lambda i: (i, 0, 0)),
        shape_of(64, 16, 128),
        3 * 2 * 128 * LENGTH * LENGTH,
        5_000_000,
        grid=4,
    )(noise.reshape(128, LENGTH), z_high, z_low)

    cell_x = (obs_cells // (8 * LENGTH)).reshape(1, 4096)
    plane = obs_cells // LENGTH % 8 - 2 * lax.axis_index("y")
    planes = jnp.stack([plane == 0, plane == 1]).astype(F32)
    freq, phase = z_frequencies(wide, jnp)
    turn = (freq[:, None] * (obs_cells % LENGTH)[None, :] + phase[:, None]) % LENGTH
    waves = jnp.cos(turn.astype(F32) * (2.0 * math.pi / LENGTH))
    box = [quarter, slab, spectrum, cell_x, planes, waves]
    tie((box, tuple(range(6))))
    quarter, slab, spectrum, cell_x, planes, waves = box
    own = [quarter[:, 0:64], quarter[:, 64:128]]
    own = [[one] + [lax.ppermute(one, "y", ring(4, step)) for step in (1, 2, 3)] for one in own]
    slab = lax.all_to_all(slab, WIDE, 0, 0)

    obs_specs = lambda k: [
        block_at((1, LENGTH), (0, k)),
        block_at((16, LENGTH), (0, k)),
        block_at((2, LENGTH), (0, k)),
    ]
    side_spec = lambda k: block_at((1, COLS, 128), (k, 0, 0))
    factor_spec = lambda k, j: block_at((8, 16, LENGTH), (0, k * (k - 1) // 2 + j, 0))
    inverse_specs = lambda k: [block_at((8, 16, 128), (0, k % 2 + a, 0)) for a in (0, 2)] * 4
    inverses = lambda k: [one for one in own[k // 2] for _ in range(2)]
    inverse_scratch = [pltpu.VMEM((8, 128, 128), BF16)] * 2
    panel_spec = spec(COLS, LENGTH)
    panel_shape = shape_of(COLS, LENGTH)
    pencil_spec = spec(LENGTH, 128)

    partial, sides = call(
        first_kernel,
        "first",
        [SMEM, block_at((8, 32, 128), (0, 4, 0))] + inverse_specs(0),
        [panel_spec, spec(4, COLS, 128)],
        [panel_shape, shape_of(4, COLS, 128)],
        20_000_000,
        1_200_000,
        inverse_scratch,
    )(index, quarter, *inverses(0))
    box = [partial, spectrum]
    tie((box, (0, 1)))
    partial, spectrum = box
    parts = share(partial)
    even, odd = call(
        spectrum_kernel,
        "spectrum",
        [SMEM, spec(LENGTH, 32), block_at((1, 16, 128), (4, 10, 0))],
        [spec(LENGTH, 128), spec(512, 128)],
        [shape_of(LENGTH, 128), shape_of(512, 128)],
        300_000_000,
        1_500_000,
    )(index, spectrum.reshape(LENGTH, 32), quarter)
    box = [even, odd]
    tie((parts, (0, 1, 2, 3)), (own[1], (1, 2, 3)), (box, (0, 1)))
    even, odd = box
    unknowns = []
    work = sides
    pencil = slab
    for panel in range(1, 4):
        partial, unknown, *pair = call(
            functools.partial(step_kernel, panel),
            f"step{panel}",
            [SMEM, side_spec(1 if panel == 1 else 0)]
            + [panel_spec] * 4
            + [factor_spec(panel, panel - 1)]
            + inverse_specs(panel)
            + [panel_spec] * (panel == 2),
            [panel_spec] * 2 + [spec(32, LENGTH)] * (panel == 2),
            [panel_shape] * 2 + [shape_of(32, LENGTH)] * (panel == 2),
            40_000_000,
            1_500_000,
            inverse_scratch,
        )(index, work, *parts, lower, *inverses(panel), *unknowns[:1] * (panel == 2))
        unknowns.append(unknown)
        parts = share(partial)
        if panel == 2:
            early = lax.all_gather(pair[0], "z")
        later = panel < 3
        box = list(
            call(
                functools.partial(wait_kernel, panel),
                f"wait{panel}",
                obs_specs(panel - 1)
                + [spec(64, 16, 128) if panel == 1 else pencil_spec]
                + [panel_spec] * panel
                + [side_spec(panel + 1)] * later
                + [factor_spec(panel + 1, j) for j in range(panel)] * later,
                [pencil_spec] + [spec(1, COLS, 128)] * later,
                [shape_of(LENGTH, 128)] + [shape_of(1, COLS, 128)] * later,
                2 * 2 * 128 * LENGTH * LENGTH,
                1_500_000,
            )(
                cell_x, waves, planes, pencil, *unknowns, *[sides] * later,
                *[lower] * (panel * later),
            )
        )
        tie((parts, (0, 1, 2, 3)), (box, (0, 1) if later else (0,)))
        pencil, work = box[0], box[-1]

    slots = call(
        filter_kernel,
        "filter",
        [spec(LENGTH, 128)]
        + obs_specs(3)
        + [panel_spec] * 4
        + [ANY] * 4
        + [spec(LENGTH, 128), spec(512, 128)],
        spec(64, 16, 128),
        shape_of(64, 16, 128),
        8 * 2 * 128 * LENGTH * LENGTH,
        11_000_000,
        [TABLE] * 4 + [pltpu.SemaphoreType.DMA((4,))],
    )(pencil, cell_x, waves, planes, *parts, x_high, x_low, back_high, back_low, even, odd)
    late = (parts[0][:16] + parts[1][:16]) + (parts[2][:16] + parts[3][:16])
    late = lax.all_gather(jnp.concatenate([unknowns[2][:16], late]), "z")
    slots = lax.all_to_all(slots, WIDE, 0, 0)
    solved = update(0, 2, index, right_side, factor, early)
    slots, solved = lax.optimization_barrier((slots, solved))
    correction = call(
        close_kernel,
        "close",
        [spec(64, 16, 128)] + [pl.BlockSpec((LENGTH, 256), lambda i: (0, i))] * 2,
        pl.BlockSpec((16, 4, 2, 256), lambda i: (0, 0, 0, i)),
        shape_of(16, 4, 2, LENGTH),
        3 * 2 * 128 * LENGTH * LENGTH,
        5_500_000,
        [pltpu.VMEM((256, LENGTH), BF16)],
        grid=4,
    )(slots, z_high, z_low)
    solved, correction = lax.optimization_barrier((solved, correction))
    solved = update(2, 2, index, solved, factor, late)
    return (solved, correction)


def solution(mesh):
    grid = Mesh(mesh.devices.reshape(8, 4, 2, 4), ("z", "x", "core", "y"))
    return jax.shard_map(
        per_device,
        mesh=grid,
        in_specs=(
            P(None, WIDE, None),
            P(None, None, WIDE, None),
            P(None, WIDE, "y"),
            P(),
            P(WIDE, None, "y", None),
            P(None, "y", WIDE),
        ),
        out_specs=(P(None, WIDE, "y"), P(WIDE, None, "y", None)),
        check_vma=False,
    )
```

```python
import functools
import math

import jax
import jax.numpy as jnp
import numpy as np
from jax import lax
from jax.experimental import pallas as pl
from jax.experimental.pallas import tpu as pltpu
from jax.sharding import Mesh, PartitionSpec as P

F32 = jnp.float32
BF16 = jnp.bfloat16
WIDE = ("z", "x", "core")
LENGTH = 1024
COLS = 24
NN = (((1,), (0,)), ((), ()))
NT = (((1,), (1,)), ((), ()))
LIMIT = pltpu.CompilerParams(vmem_limit_bytes=56 * 1024 * 1024)


def halves(table):
    high = table.astype(np.float32).astype(jnp.bfloat16)
    low = (table - high.astype(np.float64)).astype(np.float32).astype(jnp.bfloat16)
    return (np.asarray(high), np.asarray(low))


def z_frequencies(owner, xp):
    step = xp.arange(16) % 8
    part = xp.arange(16) // 8
    freq = 16 * owner + step + xp.where(owner >= 32, 1, 0)
    lone = (owner == 0) & (step == 0) & (part == 1)
    return (xp.where(lone, 512, freq), xp.where(lone, 0, 256 * part))


def z_table():
    rows = []
    cells = np.arange(LENGTH)
    for owner in range(64):
        freq, phase = z_frequencies(np.int64(owner), np)
        turn = (freq[:, None] * cells[None, :] + phase[:, None]) % LENGTH
        rows.append(np.cos(2.0 * np.pi * turn / LENGTH))
    return np.concatenate(rows)


def x_table():
    cells = np.arange(LENGTH)
    freq = np.concatenate([np.arange(512), np.arange(512)])
    phase = np.repeat([0, 256], 512)
    freq[512], phase[512] = 512, 0
    turn = (freq[:, None] * cells[None, :] + phase[:, None]) % LENGTH
    return np.cos(2.0 * np.pi * turn / LENGTH)


def split(value):
    high = value.astype(BF16)
    low = (value - high.astype(F32)).astype(BF16)
    return (high, low)


def dot(left, right, dims):
    return lax.dot_general(left, right, dims, preferred_element_type=F32)


def dot_nt(left, right):
    left_high, left_low = split(left)
    right_high, right_low = split(right)
    rows = left.shape[0]
    both = dot(jnp.concatenate([left_high, left_low]), right_high, NT)
    return both[:rows] + both[rows:] + dot(left_high, right_low, NT)


def table_nn(high, low, value):
    value_high, value_low = split(value)
    cols = value.shape[1]
    both = dot(high, jnp.concatenate([value_high, value_low], axis=1), NN)
    return both[:, :cols] + both[:, cols:] + dot(low, value_high, NN)


def swap_groups(value):
    row = lax.broadcasted_iota(jnp.int32, value.shape, 0)
    lane = lax.broadcasted_iota(jnp.int32, value.shape, 1)
    for bit in range(4):
        step = 1 << bit
        row_bit = (row >> bit) & 1
        lane_bit = (lane >> (3 + bit)) & 1
        up = pltpu.roll(pltpu.roll(value, LENGTH - step, 0), 8 * step, 1)
        down = pltpu.roll(pltpu.roll(value, step, 0), 128 - 8 * step, 1)
        value = jnp.where(row_bit == lane_bit, value, jnp.where(lane_bit == 1, up, down))
    return value


def columns_kernel(inverse_ref, right_ref, out_ref, side_ref):
    side_ref[...] = right_ref[...].reshape(64, 128)
    lane = lax.broadcasted_iota(jnp.int32, (64, 128), 1) // 16
    for r in range(8):
        total = jnp.zeros((64, 128), F32)
        for z in range(8):
            piece = inverse_ref[:, 128 * z : 128 * z + 128]
            piece = pltpu.roll(piece, (16 * (z - r)) % 128, 1) if z != r else piece
            total = jnp.where(lane == z, piece, total)
        out_ref[r] = total


def noise_kernel(noise_ref, high_ref, low_ref, out_ref):
    noise_high, noise_low = split(noise_ref[...])
    both = dot(high_ref[...], jnp.concatenate([noise_high, noise_low]), NT)
    slots = both[:, :128] + both[:, 128:] + dot(low_ref[...], noise_high, NT)
    out_ref[...] = slots.reshape(16, 16, 128)


def lower_kernel(one_ref, two_ref, three_ref, near_ref, far_ref):
    near_ref[0:16] = one_ref[0]
    for j in range(2):
        near_ref[16 * j + 16 : 16 * j + 32] = two_ref[0, :, LENGTH * j : LENGTH * (j + 1)]
    for j in range(3):
        far_ref[16 * j : 16 * j + 16] = three_ref[0, :, LENGTH * j : LENGTH * (j + 1)]


def bundle_kernel(index_ref, columns_ref, *refs):
    side_refs, extra_ref, out_ref = refs[:4], refs[4], refs[5]
    lane = lax.broadcasted_iota(jnp.int32, (64, 128), 1)
    weights = jnp.zeros((64, 128), F32)
    for step, ref in enumerate(side_refs):
        y = lax.rem(index_ref[1] + 4 - step, 4)
        weights = jnp.where(lane == y + 16, ref[:, 0:1], weights)
    side = side_refs[0][...]
    quarter = columns_ref[pl.ds(2 * index_ref[1], 2)]
    second = quarter[:, 16:32].reshape(32, 128)
    others = quarter[:, 32:64].reshape(64, 128)
    whole = columns_ref[:, 0:16, :].reshape(128, 128)
    for z in range(8):
        own = pltpu.roll(side, (128 - 16 * z) % 128, 1) if z else side
        rows = jnp.where(lane < 16, own, weights)
        out_ref[z, 0:128] = whole
        out_ref[z, 128:160] = second
        out_ref[z, 160:224] = others
        out_ref[z, 224:256] = jnp.transpose(jnp.concatenate([rows, rows]))[:32]
        out_ref[z, 256:272] = extra_ref[...]


def product(work, rows_high, rows_low):
    high, low = split(work)
    wide = dot(jnp.concatenate([high, low]), rows_high, NT)
    return wide[:COLS] + wide[COLS:] + dot(high, rows_low, NT)


def spread(work, index_ref, inverse_refs, out_ref, high_ref, low_ref):
    for number, ref in enumerate(inverse_refs):
        y = lax.rem(index_ref[1] + 4 - number // 2, 4)
        start = pl.multiple_of(32 * y + 16 * (number % 2), 16)
        rows_high, rows_low = split(ref[...])
        high_ref[:, pl.ds(start, 16), :] = rows_high
        low_ref[:, pl.ds(start, 16), :] = rows_low
    rows_high = high_ref[...].reshape(LENGTH, 128)
    out_ref[...] = product(work, rows_high, low_ref[...].reshape(LENGTH, 128))


def first_kernel(slab_ref, inverse_ref, out_ref, side_ref):
    lane = lax.broadcasted_iota(jnp.int32, (COLS, 128), 1) // 16
    for k in range(4):
        rows = jnp.zeros((COLS, 128), F32)
        for z in range(8):
            piece = slab_ref[z, 0:COLS]
            turn = (16 * (z - k)) % 128
            piece = pltpu.roll(piece, turn, 1) if turn else piece
            rows = jnp.where(lane == z, piece, rows)
        side_ref[k] = rows
    out_ref[...] = product(side_ref[0], *split(inverse_ref[...].reshape(LENGTH, 128)))


def step_kernel(panel, index_ref, start_ref, a_ref, b_ref, c_ref, d_ref, factor_ref, *refs):
    inverse_refs, refs = refs[:8], refs[8:]
    unknown = (a_ref[...] + b_ref[...]) + (c_ref[...] + d_ref[...])
    if panel == 1:
        refs[2][0:16] = unknown[0:16]
        refs[2][16:32] = jnp.zeros((16, LENGTH), F32)
    if panel == 3:
        older_ref, refs = refs[0], refs[1:]
        refs[2][0:16] = older_ref[0:16]
        refs[2][16:32] = unknown[0:16]
    out_ref, unknown_ref, high_ref, low_ref = refs[0], refs[1], refs[-2], refs[-1]
    unknown_ref[...] = unknown
    work = start_ref[0] - dot_nt(unknown, factor_ref[...].reshape(128, LENGTH))
    spread(work, index_ref, inverse_refs, out_ref, high_ref, low_ref)


def spectrum_kernel(index_ref, spectrum_ref, extra_ref, even_ref, odd_ref):
    owner = index_ref[0]
    row = lax.broadcasted_iota(jnp.int32, (32, 128), 0)
    lane = lax.broadcasted_iota(jnp.int32, (32, 128), 1)
    lone = (owner == 0) & (lane // 8 == 8)
    same_y = row // 16 == lane % 2
    same_z = row % 16 == (lane // 8) % 8 + jnp.where(owner >= 32, 1, 0)
    pick = jnp.where(same_y & same_z & jnp.logical_not(lone), 1.0, 0.0).astype(BF16)
    extra_pick = jnp.where(lone & (row == lane % 2), 1.0, 0.0)[:8].astype(BF16)

    def exact(value, choose):
        high = value.astype(BF16)
        rest = value - high.astype(F32)
        middle = rest.astype(BF16)
        low = (rest - middle.astype(F32)).astype(BF16)
        return choose(high) + (choose(middle) + choose(low))

    wanted = exact(spectrum_ref[...], lambda part: dot(part, pick, NN))
    extra = [
        jnp.concatenate([extra_ref[0, 8 * y + t : 8 * y + t + 1] for t in range(8)], axis=1)
        for y in range(2)
    ]
    extra = jnp.concatenate(extra + [jnp.zeros((6, LENGTH), F32)])
    wanted = wanted + exact(jnp.transpose(extra), lambda part: dot(part, extra_pick, NN))
    at_row = lax.broadcasted_iota(jnp.int32, (512, 512), 0)
    at_col = lax.broadcasted_iota(jnp.int32, (512, 512), 1)
    mirror = jnp.where(at_row + at_col == 512, 1.0, 0.0).astype(BF16)
    plus = wanted[:512]
    upper = wanted[512:]
    minus = exact(upper, lambda part: dot(mirror, part, NN))
    first = lax.broadcasted_iota(jnp.int32, (512, 128), 0) == 0
    minus = jnp.where(first, plus, minus)
    lanes = lax.broadcasted_iota(jnp.int32, (512, 128), 1)
    alone = (owner == 0) & ((lanes // 8) % 8 == 0)
    scale = jnp.where(first, 1.0, 2.0) * jnp.where(alone, 1.0, 2.0) / (LENGTH * LENGTH)
    even = (plus + minus) * (0.5 * scale)
    even_ref[0:512] = even
    even_ref[512:1024] = jnp.where(first, upper * scale, even)
    odd = (plus - minus) * (0.5 * scale)
    odd_ref[...] = jnp.where(lanes < 64, -odd, odd)


def add_weights(pencil, cell_ref, wave_ref, plane_ref, weights):
    doubled = jnp.concatenate(
        [weights[g : g + 1] * plane_ref[y : y + 1] for g in range(4) for y in range(2)]
    )
    waves = (wave_ref[...][:, None, :] * doubled[None]).reshape(128, LENGTH)
    cells = lax.broadcasted_iota(jnp.int32, (LENGTH, LENGTH), 0)
    chosen = jnp.where(cells == cell_ref[...], 1.0, 0.0).astype(BF16)
    high, low = split(waves)
    both = dot(chosen, jnp.concatenate([high, low]), NT)
    return pencil + both[:, :128] + both[:, 128:]


def wait_kernel(panel, *refs):
    cell_ref, wave_ref, plane_ref, pencil_ref = refs[:4]
    unknown_refs, refs = refs[4 : 4 + panel], refs[4 + panel :]
    weights = unknown_refs[-1][16:20]
    pencil = pencil_ref[...].reshape(LENGTH, 128)
    pencil = swap_groups(pencil) if panel == 1 else pencil
    pencil = add_weights(pencil, cell_ref, wave_ref, plane_ref, weights)
    if panel == 3:
        refs[0][...] = pencil
        return
    side_ref, factor_refs, (out_ref, work_ref) = refs[0], refs[1:-2], refs[-2:]
    out_ref[...] = pencil
    work = side_ref[0]
    for ref, factor_ref in zip(unknown_refs, factor_refs):
        work = work - dot_nt(ref[...], factor_ref[...].reshape(128, LENGTH))
    work_ref[0] = work


def filter_kernel(
    pencil_ref, cell_ref, wave_ref, plane_ref, a_ref, b_ref, c_ref, d_ref,
    high_hbm, low_hbm, back_high_hbm, back_low_hbm, even_ref, odd_ref, out_ref,
    high_ref, low_ref, back_high_ref, back_low_ref, sems,
):
    sources = (high_hbm, low_hbm, back_high_hbm, back_low_hbm)
    places = (high_ref, low_ref, back_high_ref, back_low_ref)
    copies = [
        pltpu.make_async_copy(source, place, sems.at[number])
        for number, (source, place) in enumerate(zip(sources, places))
    ]
    for copy in copies:
        copy.start()
    weights = (a_ref[16:20] + b_ref[16:20]) + (c_ref[16:20] + d_ref[16:20])
    pencil = add_weights(pencil_ref[...], cell_ref, wave_ref, plane_ref, weights)
    copies[0].wait()
    copies[1].wait()
    freq = table_nn(high_ref[...], low_ref[...], pencil)
    real, imag = freq[:512], freq[512:]
    odd = odd_ref[...]
    real_out = even_ref[0:512] * real + odd * pltpu.roll(imag, 64, 1)
    imag_out = even_ref[512:1024] * imag - odd * pltpu.roll(real, 64, 1)
    copies[2].wait()
    copies[3].wait()
    back = table_nn(
        back_high_ref[...], back_low_ref[...], jnp.concatenate([real_out, imag_out])
    )
    out_ref[...] = swap_groups(back).reshape(64, 16, 128)


def close_kernel(slots_ref, high_ref, low_ref, out_ref, rows_ref):
    @pl.when(pl.program_id(0) == 0)
    def _():
        rows = jnp.transpose(slots_ref[...].reshape(LENGTH, 128))
        rows_high, rows_low = split(rows)
        rows_ref[0:128] = rows_high
        rows_ref[128:256] = rows_low

    both = dot(rows_ref[...], high_ref[...], NN)
    total = both[:128] + both[128:] + dot(rows_ref[0:128], low_ref[...], NN)
    out_ref[...] = total.reshape(out_ref.shape)


def update_kernel(
    first_panel, panels, index_ref, base_ref, unknown_ref, *refs
):
    factor_refs, (out_ref, high_ref, low_ref) = refs[:panels], refs[panels:]
    block = pl.program_id(0)

    @pl.when(block == 0)
    def _():
        for k in range(panels):
            high, low = split(unknown_ref[:, 16 * k : 16 * k + 16, :].reshape(128, LENGTH))
            high_ref[k] = high
            low_ref[k] = low

    own = index_ref[0] * 16
    row = lax.broadcasted_iota(jnp.int32, (128, LENGTH), 0) + block * 128
    col = lax.broadcasted_iota(jnp.int32, (128, LENGTH), 1)
    base = base_ref[...].reshape(128, 128)
    if first_panel == 0:
        base_row = lax.broadcasted_iota(jnp.int32, (128, 128), 0) + block * 128
        base = jnp.where(base_row < 64, 0.0, base)
    for step in range(panels):
        panel = first_panel + step
        rows = factor_refs[step][...].reshape(128, LENGTH)
        mine = (row // 16 == panel) & (col == own + row % 16)
        rows = jnp.where(row < 64, jnp.where(mine, -1.0, 0.0), rows)
        rows_high, rows_low = split(rows)
        wide = dot(jnp.concatenate([rows_high, rows_low]), high_ref[step], NT)
        base = base - (wide[:128] + wide[128:] + dot(rows_high, low_ref[step], NT))
    out_ref[...] = base.reshape(8, 16, 128)


def spec(*shape):
    return pl.BlockSpec(shape, lambda *_: (0,) * len(shape))


def block_at(shape, place):
    return pl.BlockSpec(shape, lambda *_: place)


def cost(flops, moved):
    return pl.CostEstimate(flops=flops, bytes_accessed=moved, transcendentals=0)


def shape_of(*shape):
    return jax.ShapeDtypeStruct(shape, F32)


def call(body, name, in_specs, out_specs, out_shape, flops, moved, scratch=(), grid=1):
    return pl.pallas_call(
        body,
        grid=(grid,),
        in_specs=in_specs,
        out_specs=out_specs,
        out_shape=out_shape,
        scratch_shapes=scratch,
        compiler_params=LIMIT,
        cost_estimate=cost(flops, moved),
        name=name,
    )


def ring(size, step):
    return [(place, (place + step) % size) for place in range(size)]


def share(partial):
    total = partial + lax.ppermute(partial, "core", ring(2, 1))
    return [total] + [lax.ppermute(total, "x", ring(4, step)) for step in (1, 2, 3)]


def tie(*groups):
    flat = lax.optimization_barrier(tuple(group[at] for group, ats in groups for at in ats))
    flat = list(flat)
    for group, ats in groups:
        for at in ats:
            group[at] = flat.pop(0)


def update(first_panel, panels, index, base, factor, unknowns):
    return call(
        functools.partial(update_kernel, first_panel, panels),
        "update",
        [
            SMEM,
            pl.BlockSpec((8, 16, 128), lambda i: (i, 0, 0)),
            spec(8, 16 * panels, LENGTH),
        ]
        + [
            pl.BlockSpec((8, 16, LENGTH), lambda i, place=first_panel + k: (i, 0, place))
            for k in range(panels)
        ],
        pl.BlockSpec((8, 16, 128), lambda i: (i, 0, 0)),
        shape_of(32, 16, 128),
        3 * 2 * 512 * panels * LENGTH * 128,
        2_700_000 * panels,
        [pltpu.VMEM((panels, 128, LENGTH), BF16)] * 2,
        grid=4,
    )(index, base, unknowns, *[factor] * panels)


SMEM = pl.BlockSpec(memory_space=pltpu.SMEM)
ANY = pl.BlockSpec(memory_space=pl.ANY)
TABLE = pltpu.VMEM((LENGTH, LENGTH), BF16)


def per_device(factor, inverses, right_side, obs_cells, noise, spectrum):
    z_high, z_low = (jnp.asarray(t) for t in halves(z_table()))
    x_high, x_low = (jnp.asarray(t) for t in halves(x_table()))
    back_high, back_low = (jnp.asarray(t) for t in halves(x_table().T))
    wide = lax.axis_index(WIDE).astype(jnp.int32)
    index = jnp.stack([wide, lax.axis_index("y").astype(jnp.int32)])

    columns, side = call(
        columns_kernel,
        "columns",
        [spec(64, LENGTH), spec(4, 16, 128)],
        [spec(8, 64, 128), spec(64, 128)],
        [shape_of(8, 64, 128), shape_of(64, 128)],
        0,
        500_000,
    )(inverses.reshape(64, LENGTH), right_side)
    box = [columns, side, factor]
    tie((box, (0, 1, 2)))
    columns, side, factor = box
    columns = lax.all_to_all(columns, ("x", "core"), 0, 0)
    extra = spectrum[:, :, 0].T.reshape(16, 128)

    lower, lower_far = call(
        lower_kernel,
        "lower",
        [block_at((1, 16, LENGTH * k), (k, 0, 0)) for k in range(1, 4)],
        [spec(48, LENGTH)] * 2,
        [shape_of(48, LENGTH)] * 2,
        0,
        800_000,
    )(factor, factor, factor)
    lower = lax.all_gather(lower, "z")

    sides = [side] + [lax.ppermute(side, "y", ring(4, step)) for step in (1, 2, 3)]
    quarter = call(
        bundle_kernel,
        "bundle",
        [SMEM, spec(8, 64, 128)] + [spec(64, 128)] * 4 + [spec(16, 128)],
        spec(8, 272, 128),
        shape_of(8, 272, 128),
        0,
        1_500_000,
    )(index, columns, *sides, extra)
    box = [quarter, noise, spectrum, obs_cells, lower_far]
    tie((box, (0, 1, 2, 3, 4)))
    quarter, noise, spectrum, obs_cells, lower_far = box
    lower_far = lax.all_gather(lower_far, "z")
    quarter = lax.all_to_all(quarter, "z", 0, 0)

    slab = call(
        noise_kernel,
        "noise",
        [spec(128, LENGTH)] + [pl.BlockSpec((256, LENGTH), lambda i: (i, 0))] * 2,
        pl.BlockSpec((16, 16, 128), lambda i: (i, 0, 0)),
        shape_of(64, 16, 128),
        3 * 2 * 128 * LENGTH * LENGTH,
        5_000_000,
        grid=4,
    )(noise.reshape(128, LENGTH), z_high, z_low)

    cell_x = (obs_cells // (8 * LENGTH)).reshape(1, 4096)
    plane = obs_cells // LENGTH % 8 - 2 * lax.axis_index("y")
    planes = jnp.stack([plane == 0, plane == 1]).astype(F32)
    freq, phase = z_frequencies(wide, jnp)
    turn = (freq[:, None] * (obs_cells % LENGTH)[None, :] + phase[:, None]) % LENGTH
    waves = jnp.cos(turn.astype(F32) * (2.0 * math.pi / LENGTH))
    box = [quarter, slab, spectrum, cell_x, planes, waves]
    tie((box, tuple(range(6))))
    quarter, slab, spectrum, cell_x, planes, waves = box
    own = quarter[:, 128:224]
    own = [own] + [lax.ppermute(own, "y", ring(4, step)) for step in (1, 2, 3)]
    slab = lax.all_to_all(slab, WIDE, 0, 0)

    obs_specs = lambda k: [
        block_at((1, LENGTH), (0, k)),
        block_at((16, LENGTH), (0, k)),
        block_at((2, LENGTH), (0, k)),
    ]
    side_spec = lambda k: block_at((1, COLS, 128), (k, 0, 0))
    factor_spec = lambda k, j: block_at((8, 16, LENGTH), (0, j + (k == 2), 0))
    factor_rows = lambda k: lower_far if k == 3 else lower
    inverse_specs = lambda k: [
        block_at((8, 16, 128), (0, a if k == 1 else k + 2 * a, 0)) for a in range(2)
    ] * 4
    inverses = [one for one in range(4) for _ in range(2)]
    inverse_scratch = [pltpu.VMEM((8, 128, 128), BF16)] * 2
    panel_spec = spec(COLS, LENGTH)
    panel_shape = shape_of(COLS, LENGTH)
    pencil_spec = spec(LENGTH, 128)

    partial, sides = call(
        first_kernel,
        "first",
        [block_at((8, 32, 128), (0, 7, 0)), block_at((8, 128, 128), (0, 0, 0))],
        [panel_spec, spec(4, COLS, 128)],
        [panel_shape, shape_of(4, COLS, 128)],
        20_000_000,
        1_200_000,
    )(quarter, quarter)
    box = [partial, spectrum]
    tie((box, (0, 1)))
    partial, spectrum = box
    parts = share(partial)
    even, odd = call(
        spectrum_kernel,
        "spectrum",
        [SMEM, spec(LENGTH, 32), block_at((1, 16, 128), (4, 16, 0))],
        [spec(LENGTH, 128), spec(512, 128)],
        [shape_of(LENGTH, 128), shape_of(512, 128)],
        300_000_000,
        1_500_000,
    )(index, spectrum.reshape(LENGTH, 32), quarter)
    box = [even, odd]
    tie((parts, (0, 1, 2, 3)), (own, (0, 1, 2, 3)), (box, (0, 1)))
    even, odd = box
    unknowns = []
    work = sides
    pencil = slab
    for panel in range(1, 4):
        partial, unknown, *pair = call(
            functools.partial(step_kernel, panel),
            f"step{panel}",
            [SMEM, side_spec(1 if panel == 1 else 0)]
            + [panel_spec] * 4
            + [factor_spec(panel, panel - 1)]
            + inverse_specs(panel)
            + [panel_spec] * (panel == 3),
            [panel_spec] * 2 + [spec(32, LENGTH)] * (panel != 2),
            [panel_shape] * 2 + [shape_of(32, LENGTH)] * (panel != 2),
            40_000_000,
            1_500_000,
            inverse_scratch,
        )(index, work, *parts, factor_rows(panel), *[own[at] for at in inverses], *unknowns[1:2] * (panel == 3))
        unknowns.append(unknown)
        parts = share(partial)
        if panel == 1:
            early = lax.all_gather(pair[0], "z")
        later = panel < 3
        box = list(
            call(
                functools.partial(wait_kernel, panel),
                f"wait{panel}",
                obs_specs(panel - 1)
                + [spec(64, 16, 128) if panel == 1 else pencil_spec]
                + [panel_spec] * panel
                + [side_spec(panel + 1)] * later
                + [factor_spec(panel + 1, j) for j in range(panel)] * later,
                [pencil_spec] + [spec(1, COLS, 128)] * later,
                [shape_of(LENGTH, 128)] + [shape_of(1, COLS, 128)] * later,
                2 * 2 * 128 * LENGTH * LENGTH,
                1_500_000,
            )(
                cell_x, waves, planes, pencil, *unknowns, *[sides] * later,
                *[factor_rows(panel + 1)] * (panel * later),
            )
        )
        tie((parts, (0, 1, 2, 3)), (box, (0, 1) if later else (0,)))
        pencil, work = box[0], box[-1]

    slots = call(
        filter_kernel,
        "filter",
        [spec(LENGTH, 128)]
        + obs_specs(3)
        + [panel_spec] * 4
        + [ANY] * 4
        + [spec(LENGTH, 128), spec(512, 128)],
        spec(64, 16, 128),
        shape_of(64, 16, 128),
        8 * 2 * 128 * LENGTH * LENGTH,
        11_000_000,
        [TABLE] * 4 + [pltpu.SemaphoreType.DMA((4,))],
    )(pencil, cell_x, waves, planes, *parts, x_high, x_low, back_high, back_low, even, odd)
    late = (parts[0][:16] + parts[1][:16]) + (parts[2][:16] + parts[3][:16])
    late = lax.all_gather(jnp.concatenate([pair[0], late]), "z")
    slots = lax.all_to_all(slots, WIDE, 0, 0)
    solved = update(0, 1, index, right_side, factor, early)
    slots, solved = lax.optimization_barrier((slots, solved))
    correction = call(
        close_kernel,
        "close",
        [spec(64, 16, 128)] + [pl.BlockSpec((LENGTH, 256), lambda i: (0, i))] * 2,
        pl.BlockSpec((16, 4, 2, 256), lambda i: (0, 0, 0, i)),
        shape_of(16, 4, 2, LENGTH),
        3 * 2 * 128 * LENGTH * LENGTH,
        5_500_000,
        [pltpu.VMEM((256, LENGTH), BF16)],
        grid=4,
    )(slots, z_high, z_low)
    solved, correction = lax.optimization_barrier((solved, correction))
    solved = update(1, 3, index, solved, factor, late)
    return (solved, correction)


def solution(mesh):
    grid = Mesh(mesh.devices.reshape(8, 4, 2, 4), ("z", "x", "core", "y"))
    return jax.shard_map(
        per_device,
        mesh=grid,
        in_specs=(
            P(None, WIDE, None),
            P(None, None, WIDE, None),
            P(None, WIDE, "y"),
            P(),
            P(WIDE, None, "y", None),
            P(None, "y", WIDE),
        ),
        out_specs=(P(None, WIDE, "y"), P(WIDE, None, "y", None)),
        check_vma=False,
    )
```

```python
import functools
import math

import jax
import jax.numpy as jnp
import numpy as np
from jax import lax
from jax.experimental import pallas as pl
from jax.experimental.pallas import tpu as pltpu
from jax.sharding import Mesh, PartitionSpec as P

F32 = jnp.float32
BF16 = jnp.bfloat16
WIDE = ("z", "x", "core")
LENGTH = 1024
COLS = 24
NN = (((1,), (0,)), ((), ()))
NT = (((1,), (1,)), ((), ()))
LIMIT = pltpu.CompilerParams(vmem_limit_bytes=56 * 1024 * 1024)


def halves(table):
    high = table.astype(np.float32).astype(jnp.bfloat16)
    low = (table - high.astype(np.float64)).astype(np.float32).astype(jnp.bfloat16)
    return (np.asarray(high), np.asarray(low))


def z_frequencies(owner, xp):
    step = xp.arange(16) % 8
    part = xp.arange(16) // 8
    freq = 16 * owner + step + xp.where(owner >= 32, 1, 0)
    lone = (owner == 0) & (step == 0) & (part == 1)
    return (xp.where(lone, 512, freq), xp.where(lone, 0, 256 * part))


def z_table():
    rows = []
    cells = np.arange(LENGTH)
    for owner in range(64):
        freq, phase = z_frequencies(np.int64(owner), np)
        turn = (freq[:, None] * cells[None, :] + phase[:, None]) % LENGTH
        rows.append(np.cos(2.0 * np.pi * turn / LENGTH))
    return np.concatenate(rows)


def x_table():
    cells = np.arange(LENGTH)
    freq = np.concatenate([np.arange(512), np.arange(512)])
    phase = np.repeat([0, 256], 512)
    freq[512], phase[512] = 512, 0
    turn = (freq[:, None] * cells[None, :] + phase[:, None]) % LENGTH
    return np.cos(2.0 * np.pi * turn / LENGTH)


def split(value):
    high = value.astype(BF16)
    low = (value - high.astype(F32)).astype(BF16)
    return (high, low)


def dot(left, right, dims):
    return lax.dot_general(left, right, dims, preferred_element_type=F32)


def dot_nt(left, right):
    left_high, left_low = split(left)
    right_high, right_low = split(right)
    rows = left.shape[0]
    both = dot(jnp.concatenate([left_high, left_low]), right_high, NT)
    return both[:rows] + both[rows:] + dot(left_high, right_low, NT)


def table_nn(high, low, value):
    value_high, value_low = split(value)
    cols = value.shape[1]
    both = dot(high, jnp.concatenate([value_high, value_low], axis=1), NN)
    return both[:, :cols] + both[:, cols:] + dot(low, value_high, NN)


def swap_groups(value):
    row = lax.broadcasted_iota(jnp.int32, value.shape, 0)
    lane = lax.broadcasted_iota(jnp.int32, value.shape, 1)
    for bit in range(4):
        step = 1 << bit
        row_bit = (row >> bit) & 1
        lane_bit = (lane >> (3 + bit)) & 1
        up = pltpu.roll(pltpu.roll(value, LENGTH - step, 0), 8 * step, 1)
        down = pltpu.roll(pltpu.roll(value, step, 0), 128 - 8 * step, 1)
        value = jnp.where(row_bit == lane_bit, value, jnp.where(lane_bit == 1, up, down))
    return value


def columns_kernel(inverse_ref, right_ref, out_ref, side_ref):
    side_ref[...] = right_ref[...].reshape(64, 128)
    lane = lax.broadcasted_iota(jnp.int32, (64, 128), 1) // 16
    for r in range(8):
        total = jnp.zeros((64, 128), F32)
        for z in range(8):
            piece = inverse_ref[:, 128 * z : 128 * z + 128]
            piece = pltpu.roll(piece, (16 * (z - r)) % 128, 1) if z != r else piece
            total = jnp.where(lane == z, piece, total)
        out_ref[r] = total


def noise_kernel(noise_ref, high_ref, low_ref, out_ref):
    noise_high, noise_low = split(noise_ref[...])
    both = dot(high_ref[...], jnp.concatenate([noise_high, noise_low]), NT)
    slots = both[:, :128] + both[:, 128:] + dot(low_ref[...], noise_high, NT)
    out_ref[...] = slots.reshape(16, 16, 128)


def lower_kernel(one_ref, two_ref, three_ref, near_ref, far_ref):
    near_ref[0:16] = one_ref[0]
    near_ref[16:32] = two_ref[0, :, 0:LENGTH]
    far_ref[0:16] = two_ref[0, :, LENGTH : 2 * LENGTH]
    for j in range(3):
        far_ref[16 * j + 16 : 16 * j + 32] = three_ref[0, :, LENGTH * j : LENGTH * (j + 1)]


def bundle_kernel(index_ref, columns_ref, *refs):
    side_refs, extra_ref, out_ref = refs[:4], refs[4], refs[5]
    lane = lax.broadcasted_iota(jnp.int32, (64, 128), 1)
    weights = jnp.zeros((64, 128), F32)
    for step, ref in enumerate(side_refs):
        y = lax.rem(index_ref[1] + 4 - step, 4)
        weights = jnp.where(lane == y + 16, ref[:, 0:1], weights)
    side = side_refs[0][...]
    quarter = columns_ref[pl.ds(2 * index_ref[1], 2)]
    second = quarter[:, 16:32].reshape(32, 128)
    others = quarter[:, 32:64].reshape(64, 128)
    whole = columns_ref[:, 0:16, :].reshape(128, 128)
    for z in range(8):
        own = pltpu.roll(side, (128 - 16 * z) % 128, 1) if z else side
        rows = jnp.where(lane < 16, own, weights)
        out_ref[z, 0:128] = whole
        out_ref[z, 128:160] = second
        out_ref[z, 160:224] = others
        out_ref[z, 224:256] = jnp.transpose(jnp.concatenate([rows, rows]))[:32]
        out_ref[z, 256:272] = extra_ref[...]


def product(work, rows_high, rows_low):
    high, low = split(work)
    wide = dot(jnp.concatenate([high, low]), rows_high, NT)
    return wide[:COLS] + wide[COLS:] + dot(high, rows_low, NT)


def spread(work, index_ref, inverse_refs, out_ref, high_ref, low_ref):
    for number, ref in enumerate(inverse_refs):
        y = lax.rem(index_ref[1] + 4 - number // 2, 4)
        start = pl.multiple_of(32 * y + 16 * (number % 2), 16)
        rows_high, rows_low = split(ref[...])
        high_ref[:, pl.ds(start, 16), :] = rows_high
        low_ref[:, pl.ds(start, 16), :] = rows_low
    rows_high = high_ref[...].reshape(LENGTH, 128)
    out_ref[...] = product(work, rows_high, low_ref[...].reshape(LENGTH, 128))


def first_kernel(slab_ref, inverse_ref, out_ref, side_ref):
    lane = lax.broadcasted_iota(jnp.int32, (COLS, 128), 1) // 16
    for k in range(4):
        rows = jnp.zeros((COLS, 128), F32)
        for z in range(8):
            piece = slab_ref[z, 0:COLS]
            turn = (16 * (z - k)) % 128
            piece = pltpu.roll(piece, turn, 1) if turn else piece
            rows = jnp.where(lane == z, piece, rows)
        side_ref[k] = rows
    out_ref[...] = product(side_ref[0], *split(inverse_ref[...].reshape(LENGTH, 128)))


def step_kernel(panel, index_ref, start_ref, a_ref, b_ref, c_ref, d_ref, factor_ref, *refs):
    inverse_refs, refs = refs[:8], refs[8:]
    unknown = (a_ref[...] + b_ref[...]) + (c_ref[...] + d_ref[...])
    if panel == 1:
        refs[2][0:16] = unknown[0:16]
        refs[2][16:32] = jnp.zeros((16, LENGTH), F32)
    if panel == 3:
        older_ref, refs = refs[0], refs[1:]
        refs[2][0:16] = older_ref[0:16]
        refs[2][16:32] = unknown[0:16]
    out_ref, unknown_ref, high_ref, low_ref = refs[0], refs[1], refs[-2], refs[-1]
    unknown_ref[...] = unknown
    work = start_ref[0] - dot_nt(unknown, factor_ref[...].reshape(128, LENGTH))
    spread(work, index_ref, inverse_refs, out_ref, high_ref, low_ref)


def spectrum_kernel(index_ref, spectrum_ref, extra_ref, even_ref, odd_ref):
    owner = index_ref[0]
    row = lax.broadcasted_iota(jnp.int32, (32, 128), 0)
    lane = lax.broadcasted_iota(jnp.int32, (32, 128), 1)
    lone = (owner == 0) & (lane // 8 == 8)
    same_y = row // 16 == lane % 2
    same_z = row % 16 == (lane // 8) % 8 + jnp.where(owner >= 32, 1, 0)
    pick = jnp.where(same_y & same_z & jnp.logical_not(lone), 1.0, 0.0).astype(BF16)
    extra_pick = jnp.where(lone & (row == lane % 2), 1.0, 0.0)[:8].astype(BF16)

    def exact(value, choose):
        high = value.astype(BF16)
        rest = value - high.astype(F32)
        middle = rest.astype(BF16)
        low = (rest - middle.astype(F32)).astype(BF16)
        return choose(high) + (choose(middle) + choose(low))

    wanted = exact(spectrum_ref[...], lambda part: dot(part, pick, NN))
    extra = [
        jnp.concatenate([extra_ref[0, 8 * y + t : 8 * y + t + 1] for t in range(8)], axis=1)
        for y in range(2)
    ]
    extra = jnp.concatenate(extra + [jnp.zeros((6, LENGTH), F32)])
    wanted = wanted + exact(jnp.transpose(extra), lambda part: dot(part, extra_pick, NN))
    at_row = lax.broadcasted_iota(jnp.int32, (512, 512), 0)
    at_col = lax.broadcasted_iota(jnp.int32, (512, 512), 1)
    mirror = jnp.where(at_row + at_col == 512, 1.0, 0.0).astype(BF16)
    plus = wanted[:512]
    upper = wanted[512:]
    minus = exact(upper, lambda part: dot(mirror, part, NN))
    first = lax.broadcasted_iota(jnp.int32, (512, 128), 0) == 0
    minus = jnp.where(first, plus, minus)
    lanes = lax.broadcasted_iota(jnp.int32, (512, 128), 1)
    alone = (owner == 0) & ((lanes // 8) % 8 == 0)
    scale = jnp.where(first, 1.0, 2.0) * jnp.where(alone, 1.0, 2.0) / (LENGTH * LENGTH)
    even = (plus + minus) * (0.5 * scale)
    even_ref[0:512] = even
    even_ref[512:1024] = jnp.where(first, upper * scale, even)
    odd = (plus - minus) * (0.5 * scale)
    odd_ref[...] = jnp.where(lanes < 64, -odd, odd)


def add_weights(pencil, cell_ref, wave_ref, plane_ref, weights):
    doubled = jnp.concatenate(
        [weights[g : g + 1] * plane_ref[y : y + 1] for g in range(4) for y in range(2)]
    )
    waves = (wave_ref[...][:, None, :] * doubled[None]).reshape(128, LENGTH)
    cells = lax.broadcasted_iota(jnp.int32, (LENGTH, LENGTH), 0)
    chosen = jnp.where(cells == cell_ref[...], 1.0, 0.0).astype(BF16)
    high, low = split(waves)
    both = dot(chosen, jnp.concatenate([high, low]), NT)
    return pencil + both[:, :128] + both[:, 128:]


def wait_kernel(panel, *refs):
    cell_ref, wave_ref, plane_ref, pencil_ref = refs[:4]
    unknown_refs, refs = refs[4 : 4 + panel], refs[4 + panel :]
    weights = unknown_refs[-1][16:20]
    pencil = pencil_ref[...].reshape(LENGTH, 128)
    pencil = swap_groups(pencil) if panel == 1 else pencil
    pencil = add_weights(pencil, cell_ref, wave_ref, plane_ref, weights)
    if panel == 3:
        refs[0][...] = pencil
        return
    side_ref, factor_refs, (out_ref, work_ref) = refs[0], refs[1:-2], refs[-2:]
    out_ref[...] = pencil
    work = side_ref[0]
    for ref, factor_ref in zip(unknown_refs, factor_refs):
        work = work - dot_nt(ref[...], factor_ref[...].reshape(128, LENGTH))
    work_ref[0] = work


def filter_kernel(
    pencil_ref, cell_ref, wave_ref, plane_ref, a_ref, b_ref, c_ref, d_ref,
    high_hbm, low_hbm, back_high_hbm, back_low_hbm, even_ref, odd_ref, out_ref,
    high_ref, low_ref, back_high_ref, back_low_ref, sems,
):
    sources = (high_hbm, low_hbm, back_high_hbm, back_low_hbm)
    places = (high_ref, low_ref, back_high_ref, back_low_ref)
    copies = [
        pltpu.make_async_copy(source, place, sems.at[number])
        for number, (source, place) in enumerate(zip(sources, places))
    ]
    for copy in copies:
        copy.start()
    weights = (a_ref[16:20] + b_ref[16:20]) + (c_ref[16:20] + d_ref[16:20])
    pencil = add_weights(pencil_ref[...], cell_ref, wave_ref, plane_ref, weights)
    copies[0].wait()
    copies[1].wait()
    freq = table_nn(high_ref[...], low_ref[...], pencil)
    real, imag = freq[:512], freq[512:]
    odd = odd_ref[...]
    real_out = even_ref[0:512] * real + odd * pltpu.roll(imag, 64, 1)
    imag_out = even_ref[512:1024] * imag - odd * pltpu.roll(real, 64, 1)
    copies[2].wait()
    copies[3].wait()
    back = table_nn(
        back_high_ref[...], back_low_ref[...], jnp.concatenate([real_out, imag_out])
    )
    out_ref[...] = swap_groups(back).reshape(64, 16, 128)


def close_kernel(slots_ref, high_ref, low_ref, out_ref, rows_ref):
    @pl.when(pl.program_id(0) == 0)
    def _():
        rows = jnp.transpose(slots_ref[...].reshape(LENGTH, 128))
        rows_high, rows_low = split(rows)
        rows_ref[0:128] = rows_high
        rows_ref[128:256] = rows_low

    both = dot(rows_ref[...], high_ref[...], NN)
    total = both[:128] + both[128:] + dot(rows_ref[0:128], low_ref[...], NN)
    out_ref[...] = total.reshape(out_ref.shape)


def update_kernel(
    first_panel, panels, index_ref, base_ref, unknown_ref, *refs
):
    factor_refs, (out_ref, high_ref, low_ref) = refs[:panels], refs[panels:]
    block = pl.program_id(0)

    @pl.when(block == 0)
    def _():
        for k in range(panels):
            high, low = split(unknown_ref[:, 16 * k : 16 * k + 16, :].reshape(128, LENGTH))
            high_ref[k] = high
            low_ref[k] = low

    def subtract(base, first):
        for step in range(panels):
            panel = first_panel + step
            rows = factor_refs[step][...].reshape(128, LENGTH)
            if first:
                own = index_ref[0] * 16
                row = lax.broadcasted_iota(jnp.int32, (64, LENGTH), 0)
                col = lax.broadcasted_iota(jnp.int32, (64, LENGTH), 1)
                mine = (row // 16 == panel) & (col == own + row % 16)
                rows = jnp.concatenate([jnp.where(mine, -1.0, 0.0), rows[64:]])
            rows_high, rows_low = split(rows)
            wide = dot(jnp.concatenate([rows_high, rows_low]), high_ref[step], NT)
            base = base - (wide[:128] + wide[128:] + dot(rows_high, low_ref[step], NT))
        out_ref[...] = base.reshape(8, 16, 128)

    base = base_ref[...].reshape(128, 128)

    @pl.when(block == 0)
    def _():
        if first_panel == 0:
            subtract(jnp.concatenate([jnp.zeros((64, 128), F32), base[64:]]), True)
        else:
            subtract(base, True)

    @pl.when(block > 0)
    def _():
        subtract(base, False)


def spec(*shape):
    return pl.BlockSpec(shape, lambda *_: (0,) * len(shape))


def block_at(shape, place):
    return pl.BlockSpec(shape, lambda *_: place)


def cost(flops, moved):
    return pl.CostEstimate(flops=flops, bytes_accessed=moved, transcendentals=0)


def shape_of(*shape):
    return jax.ShapeDtypeStruct(shape, F32)


def call(body, name, in_specs, out_specs, out_shape, flops, moved, scratch=(), grid=1):
    return pl.pallas_call(
        body,
        grid=(grid,),
        in_specs=in_specs,
        out_specs=out_specs,
        out_shape=out_shape,
        scratch_shapes=scratch,
        compiler_params=LIMIT,
        cost_estimate=cost(flops, moved),
        name=name,
    )


def ring(size, step):
    return [(place, (place + step) % size) for place in range(size)]


def share(partial):
    total = partial + lax.ppermute(partial, "core", ring(2, 1))
    return [total] + [lax.ppermute(total, "x", ring(4, step)) for step in (1, 2, 3)]


def tie(*groups):
    flat = lax.optimization_barrier(tuple(group[at] for group, ats in groups for at in ats))
    flat = list(flat)
    for group, ats in groups:
        for at in ats:
            group[at] = flat.pop(0)


def update(first_panel, panels, index, base, factor, unknowns):
    return call(
        functools.partial(update_kernel, first_panel, panels),
        "update",
        [
            SMEM,
            pl.BlockSpec((8, 16, 128), lambda i: (i, 0, 0)),
            spec(8, 16 * panels, LENGTH),
        ]
        + [
            pl.BlockSpec((8, 16, LENGTH), lambda i, place=first_panel + k: (i, 0, place))
            for k in range(panels)
        ],
        pl.BlockSpec((8, 16, 128), lambda i: (i, 0, 0)),
        shape_of(32, 16, 128),
        3 * 2 * 512 * panels * LENGTH * 128,
        2_700_000 * panels,
        [pltpu.VMEM((panels, 128, LENGTH), BF16)] * 2,
        grid=4,
    )(index, base, unknowns, *[factor] * panels)


SMEM = pl.BlockSpec(memory_space=pltpu.SMEM)
ANY = pl.BlockSpec(memory_space=pl.ANY)
TABLE = pltpu.VMEM((LENGTH, LENGTH), BF16)


def per_device(factor, inverses, right_side, obs_cells, noise, spectrum):
    z_high, z_low = (jnp.asarray(t) for t in halves(z_table()))
    x_high, x_low = (jnp.asarray(t) for t in halves(x_table()))
    back_high, back_low = (jnp.asarray(t) for t in halves(x_table().T))
    wide = lax.axis_index(WIDE).astype(jnp.int32)
    index = jnp.stack([wide, lax.axis_index("y").astype(jnp.int32)])

    columns, side = call(
        columns_kernel,
        "columns",
        [spec(64, LENGTH), spec(4, 16, 128)],
        [spec(8, 64, 128), spec(64, 128)],
        [shape_of(8, 64, 128), shape_of(64, 128)],
        0,
        500_000,
    )(inverses.reshape(64, LENGTH), right_side)
    box = [columns, side, factor]
    tie((box, (0, 1, 2)))
    columns, side, factor = box
    columns = lax.all_to_all(columns, ("x", "core"), 0, 0)
    extra = spectrum[:, :, 0].T.reshape(16, 128)

    lower, lower_far = call(
        lower_kernel,
        "lower",
        [block_at((1, 16, LENGTH * k), (k, 0, 0)) for k in range(1, 4)],
        [spec(32, LENGTH), spec(64, LENGTH)],
        [shape_of(32, LENGTH), shape_of(64, LENGTH)],
        0,
        800_000,
    )(factor, factor, factor)
    lower = lax.all_gather(lower, "z")

    sides = [side] + [lax.ppermute(side, "y", ring(4, step)) for step in (1, 2, 3)]
    quarter = call(
        bundle_kernel,
        "bundle",
        [SMEM, spec(8, 64, 128)] + [spec(64, 128)] * 4 + [spec(16, 128)],
        spec(8, 272, 128),
        shape_of(8, 272, 128),
        0,
        1_500_000,
    )(index, columns, *sides, extra)
    box = [quarter, noise, spectrum, obs_cells, lower_far]
    tie((box, (0, 1, 2, 3, 4)))
    quarter, noise, spectrum, obs_cells, lower_far = box
    lower_far = lax.all_gather(lower_far, "z")
    quarter = lax.all_to_all(quarter, "z", 0, 0)

    slab = call(
        noise_kernel,
        "noise",
        [spec(128, LENGTH)] + [pl.BlockSpec((256, LENGTH), lambda i: (i, 0))] * 2,
        pl.BlockSpec((16, 16, 128), lambda i: (i, 0, 0)),
        shape_of(64, 16, 128),
        3 * 2 * 128 * LENGTH * LENGTH,
        5_000_000,
        grid=4,
    )(noise.reshape(128, LENGTH), z_high, z_low)

    cell_x = (obs_cells // (8 * LENGTH)).reshape(1, 4096)
    plane = obs_cells // LENGTH % 8 - 2 * lax.axis_index("y")
    planes = jnp.stack([plane == 0, plane == 1]).astype(F32)
    freq, phase = z_frequencies(wide, jnp)
    turn = (freq[:, None] * (obs_cells % LENGTH)[None, :] + phase[:, None]) % LENGTH
    waves = jnp.cos(turn.astype(F32) * (2.0 * math.pi / LENGTH))
    box = [quarter, slab, spectrum, cell_x, planes, waves]
    tie((box, tuple(range(6))))
    quarter, slab, spectrum, cell_x, planes, waves = box
    own = quarter[:, 128:224]
    own = [own] + [lax.ppermute(own, "y", ring(4, step)) for step in (1, 2, 3)]
    slab = lax.all_to_all(slab, WIDE, 0, 0)

    obs_specs = lambda k: [
        block_at((1, LENGTH), (0, k)),
        block_at((16, LENGTH), (0, k)),
        block_at((2, LENGTH), (0, k)),
    ]
    side_spec = lambda k: block_at((1, COLS, 128), (k, 0, 0))
    factor_at = {(1, 0): 0, (2, 0): 1, (2, 1): 0, (3, 0): 1, (3, 1): 2, (3, 2): 3}
    factor_spec = lambda k, j: block_at((8, 16, LENGTH), (0, factor_at[k, j], 0))
    factor_rows = lambda k, j: lower_far if k + j > 2 else lower
    inverse_specs = lambda k: [
        block_at((8, 16, 128), (0, a if k == 1 else k + 2 * a, 0)) for a in range(2)
    ] * 4
    inverses = [one for one in range(4) for _ in range(2)]
    inverse_scratch = [pltpu.VMEM((8, 128, 128), BF16)] * 2
    panel_spec = spec(COLS, LENGTH)
    panel_shape = shape_of(COLS, LENGTH)
    pencil_spec = spec(LENGTH, 128)

    partial, sides = call(
        first_kernel,
        "first",
        [block_at((8, 32, 128), (0, 7, 0)), block_at((8, 128, 128), (0, 0, 0))],
        [panel_spec, spec(4, COLS, 128)],
        [panel_shape, shape_of(4, COLS, 128)],
        20_000_000,
        1_200_000,
    )(quarter, quarter)
    box = [partial, spectrum]
    tie((box, (0, 1)))
    partial, spectrum = box
    parts = share(partial)
    even, odd = call(
        spectrum_kernel,
        "spectrum",
        [SMEM, spec(LENGTH, 32), block_at((1, 16, 128), (4, 16, 0))],
        [spec(LENGTH, 128), spec(512, 128)],
        [shape_of(LENGTH, 128), shape_of(512, 128)],
        300_000_000,
        1_500_000,
    )(index, spectrum.reshape(LENGTH, 32), quarter)
    box = [even, odd, slab]
    tie((parts, (0, 1, 2, 3)), (own, (0, 1, 2, 3)), (box, (0, 1, 2)))
    even, odd, slab = box
    unknowns = []
    work = sides
    pencil = slab
    for panel in range(1, 4):
        partial, unknown, *pair = call(
            functools.partial(step_kernel, panel),
            f"step{panel}",
            [SMEM, side_spec(1 if panel == 1 else 0)]
            + [panel_spec] * 4
            + [factor_spec(panel, panel - 1)]
            + inverse_specs(panel)
            + [panel_spec] * (panel == 3),
            [panel_spec] * 2 + [spec(32, LENGTH)] * (panel != 2),
            [panel_shape] * 2 + [shape_of(32, LENGTH)] * (panel != 2),
            40_000_000,
            1_500_000,
            inverse_scratch,
        )(index, work, *parts, factor_rows(panel, panel - 1), *[own[at] for at in inverses], *unknowns[1:2] * (panel == 3))
        unknowns.append(unknown)
        parts = share(partial)
        if panel == 1:
            early = lax.all_gather(pair[0], "z")
        later = panel < 3
        box = list(
            call(
                functools.partial(wait_kernel, panel),
                f"wait{panel}",
                obs_specs(panel - 1)
                + [spec(64, 16, 128) if panel == 1 else pencil_spec]
                + [panel_spec] * panel
                + [side_spec(panel + 1)] * later
                + [factor_spec(panel + 1, j) for j in range(panel * later)],
                [pencil_spec] + [spec(1, COLS, 128)] * later,
                [shape_of(LENGTH, 128)] + [shape_of(1, COLS, 128)] * later,
                2 * 2 * 128 * LENGTH * LENGTH,
                1_500_000,
            )(
                cell_x, waves, planes, pencil, *unknowns, *[sides] * later,
                *[factor_rows(panel + 1, j) for j in range(panel * later)],
            )
        )
        tie((parts, (0, 1, 2, 3)), (box, (0, 1) if later else (0,)))
        pencil, work = box[0], box[-1]

    slots = call(
        filter_kernel,
        "filter",
        [spec(LENGTH, 128)]
        + obs_specs(3)
        + [panel_spec] * 4
        + [ANY] * 4
        + [spec(LENGTH, 128), spec(512, 128)],
        spec(64, 16, 128),
        shape_of(64, 16, 128),
        8 * 2 * 128 * LENGTH * LENGTH,
        11_000_000,
        [TABLE] * 4 + [pltpu.SemaphoreType.DMA((4,))],
    )(pencil, cell_x, waves, planes, *parts, x_high, x_low, back_high, back_low, even, odd)
    late = (parts[0][:16] + parts[1][:16]) + (parts[2][:16] + parts[3][:16])
    late = lax.all_gather(jnp.concatenate([pair[0], late]), "z")
    slots = lax.all_to_all(slots, WIDE, 0, 0)
    solved = update(0, 1, index, right_side, factor, early)
    slots, solved = lax.optimization_barrier((slots, solved))
    correction = call(
        close_kernel,
        "close",
        [spec(64, 16, 128)] + [pl.BlockSpec((LENGTH, 256), lambda i: (0, i))] * 2,
        pl.BlockSpec((16, 4, 2, 256), lambda i: (0, 0, 0, i)),
        shape_of(16, 4, 2, LENGTH),
        3 * 2 * 128 * LENGTH * LENGTH,
        5_500_000,
        [pltpu.VMEM((256, LENGTH), BF16)],
        grid=4,
    )(slots, z_high, z_low)
    solved, correction = lax.optimization_barrier((solved, correction))
    solved = update(1, 3, index, solved, factor, late)
    return (solved, correction)


def solution(mesh):
    grid = Mesh(mesh.devices.reshape(8, 4, 2, 4), ("z", "x", "core", "y"))
    return jax.shard_map(
        per_device,
        mesh=grid,
        in_specs=(
            P(None, WIDE, None),
            P(None, None, WIDE, None),
            P(None, WIDE, "y"),
            P(),
            P(WIDE, None, "y", None),
            P(None, "y", WIDE),
        ),
        out_specs=(P(None, WIDE, "y"), P(WIDE, None, "y", None)),
        check_vma=False,
    )
```

```python
import functools
import math

import jax
import jax.numpy as jnp
import numpy as np
from jax import lax
from jax.experimental import pallas as pl
from jax.experimental.pallas import tpu as pltpu
from jax.sharding import Mesh, PartitionSpec as P

F32 = jnp.float32
BF16 = jnp.bfloat16
WIDE = ("z", "x", "core")
LENGTH = 1024
COLS = 24
NN = (((1,), (0,)), ((), ()))
NT = (((1,), (1,)), ((), ()))
LIMIT = pltpu.CompilerParams(vmem_limit_bytes=40 * 1024 * 1024)


def halves(table):
    high = table.astype(np.float32).astype(jnp.bfloat16)
    low = (table - high.astype(np.float64)).astype(np.float32).astype(jnp.bfloat16)
    return (np.asarray(high), np.asarray(low))


def z_frequencies(owner, xp):
    step = xp.arange(16) % 8
    part = xp.arange(16) // 8
    freq = 16 * owner + step + xp.where(owner >= 32, 1, 0)
    lone = (owner == 0) & (step == 0) & (part == 1)
    return (xp.where(lone, 512, freq), xp.where(lone, 0, 256 * part))


def z_table():
    rows = []
    cells = np.arange(LENGTH)
    for owner in range(64):
        freq, phase = z_frequencies(np.int64(owner), np)
        turn = (freq[:, None] * cells[None, :] + phase[:, None]) % LENGTH
        rows.append(np.cos(2.0 * np.pi * turn / LENGTH))
    return np.concatenate(rows)


def x_table():
    cells = np.arange(LENGTH)
    freq = np.concatenate([np.arange(512), np.arange(512)])
    phase = np.repeat([0, 256], 512)
    freq[512], phase[512] = 512, 0
    turn = (freq[:, None] * cells[None, :] + phase[:, None]) % LENGTH
    return np.cos(2.0 * np.pi * turn / LENGTH)


def split(value):
    high = value.astype(BF16)
    low = (value - high.astype(F32)).astype(BF16)
    return (high, low)


def dot(left, right, dims):
    return lax.dot_general(left, right, dims, preferred_element_type=F32)


def dot_nt(left, right):
    left_high, left_low = split(left)
    right_high, right_low = split(right)
    rows = left.shape[0]
    both = dot(jnp.concatenate([left_high, left_low]), right_high, NT)
    return both[:rows] + both[rows:] + dot(left_high, right_low, NT)


def table_nn(high, low, value):
    value_high, value_low = split(value)
    cols = value.shape[1]
    both = dot(high, jnp.concatenate([value_high, value_low], axis=1), NN)
    return both[:, :cols] + both[:, cols:] + dot(low, value_high, NN)


def swap_groups(value):
    row = lax.broadcasted_iota(jnp.int32, value.shape, 0)
    lane = lax.broadcasted_iota(jnp.int32, value.shape, 1)
    for bit in range(4):
        step = 1 << bit
        row_bit = (row >> bit) & 1
        lane_bit = (lane >> (3 + bit)) & 1
        up = pltpu.roll(pltpu.roll(value, LENGTH - step, 0), 8 * step, 1)
        down = pltpu.roll(pltpu.roll(value, step, 0), 128 - 8 * step, 1)
        value = jnp.where(row_bit == lane_bit, value, jnp.where(lane_bit == 1, up, down))
    return value


def columns_kernel(inverse_ref, right_ref, out_ref, side_ref):
    side_ref[...] = right_ref[...].reshape(64, 128)
    lane = lax.broadcasted_iota(jnp.int32, (64, 128), 1) // 16
    for r in range(8):
        total = jnp.zeros((64, 128), F32)
        for z in range(8):
            piece = inverse_ref[:, 128 * z : 128 * z + 128]
            piece = pltpu.roll(piece, (16 * (z - r)) % 128, 1) if z != r else piece
            total = jnp.where(lane == z, piece, total)
        out_ref[r] = total


def noise_kernel(noise_ref, high_ref, low_ref, out_ref):
    noise_high, noise_low = split(noise_ref[...])
    both = dot(high_ref[...], jnp.concatenate([noise_high, noise_low]), NT)
    slots = both[:, :128] + both[:, 128:] + dot(low_ref[...], noise_high, NT)
    out_ref[...] = slots.reshape(16, 16, 128)


def lower_kernel(one_ref, two_ref, three_ref, near_ref, far_ref):
    near_ref[0:16] = one_ref[0]
    near_ref[16:32] = two_ref[0, :, 0:LENGTH]
    far_ref[0:16] = two_ref[0, :, LENGTH : 2 * LENGTH]
    for j in range(3):
        far_ref[16 * j + 16 : 16 * j + 32] = three_ref[0, :, LENGTH * j : LENGTH * (j + 1)]


def bundle_kernel(index_ref, columns_ref, *refs):
    side_refs, extra_ref, out_ref = refs[:4], refs[4], refs[5]
    lane = lax.broadcasted_iota(jnp.int32, (64, 128), 1)
    weights = jnp.zeros((64, 128), F32)
    for step, ref in enumerate(side_refs):
        y = lax.rem(index_ref[1] + 4 - step, 4)
        weights = jnp.where(lane == y + 16, ref[:, 0:1], weights)
    side = side_refs[0][...]
    quarter = columns_ref[pl.ds(2 * index_ref[1], 2)]
    second = quarter[:, 16:32].reshape(32, 128)
    others = quarter[:, 32:64].reshape(64, 128)
    whole = columns_ref[:, 0:16, :].reshape(128, 128)
    for z in range(8):
        own = pltpu.roll(side, (128 - 16 * z) % 128, 1) if z else side
        rows = jnp.where(lane < 16, own, weights)
        out_ref[z, 0:128] = whole
        out_ref[z, 128:160] = second
        out_ref[z, 160:224] = others
        out_ref[z, 224:256] = jnp.transpose(jnp.concatenate([rows, rows]))[:32]
        out_ref[z, 256:272] = extra_ref[...]


def product(work, rows_high, rows_low):
    high, low = split(work)
    wide = dot(jnp.concatenate([high, low]), rows_high, NT)
    return wide[:COLS] + wide[COLS:] + dot(high, rows_low, NT)


def spread(work, index_ref, inverse_refs, out_ref, high_ref, low_ref):
    for number, ref in enumerate(inverse_refs):
        y = lax.rem(index_ref[1] + 4 - number // 2, 4)
        start = pl.multiple_of(32 * y + 16 * (number % 2), 16)
        rows_high, rows_low = split(ref[...])
        high_ref[:, pl.ds(start, 16), :] = rows_high
        low_ref[:, pl.ds(start, 16), :] = rows_low
    rows_high = high_ref[...].reshape(LENGTH, 128)
    out_ref[...] = product(work, rows_high, low_ref[...].reshape(LENGTH, 128))


def first_kernel(slab_ref, inverse_ref, out_ref, side_ref):
    lane = lax.broadcasted_iota(jnp.int32, (COLS, 128), 1) // 16
    for k in range(4):
        rows = jnp.zeros((COLS, 128), F32)
        for z in range(8):
            piece = slab_ref[z, 0:COLS]
            turn = (16 * (z - k)) % 128
            piece = pltpu.roll(piece, turn, 1) if turn else piece
            rows = jnp.where(lane == z, piece, rows)
        side_ref[k] = rows
    out_ref[...] = product(side_ref[0], *split(inverse_ref[...].reshape(LENGTH, 128)))


def step_kernel(panel, index_ref, start_ref, a_ref, b_ref, c_ref, d_ref, factor_ref, *refs):
    inverse_refs, refs = refs[:8], refs[8:]
    unknown = (a_ref[...] + b_ref[...]) + (c_ref[...] + d_ref[...])
    if panel == 3:
        older_refs, refs = refs[:2], refs[2:]
        refs[2][0:16] = older_refs[0][0:16]
        refs[2][16:32] = older_refs[1][0:16]
        refs[2][32:48] = unknown[0:16]
    out_ref, unknown_ref, high_ref, low_ref = refs[0], refs[1], refs[-2], refs[-1]
    unknown_ref[...] = unknown
    work = start_ref[0] - dot_nt(unknown, factor_ref[...].reshape(128, LENGTH))
    spread(work, index_ref, inverse_refs, out_ref, high_ref, low_ref)


def spectrum_kernel(index_ref, spectrum_ref, extra_ref, even_ref, odd_ref):
    owner = index_ref[0]
    row = lax.broadcasted_iota(jnp.int32, (32, 128), 0)
    lane = lax.broadcasted_iota(jnp.int32, (32, 128), 1)
    lone = (owner == 0) & (lane // 8 == 8)
    same_y = row // 16 == lane % 2
    same_z = row % 16 == (lane // 8) % 8 + jnp.where(owner >= 32, 1, 0)
    pick = jnp.where(same_y & same_z & jnp.logical_not(lone), 1.0, 0.0).astype(BF16)
    extra_pick = jnp.where(lone & (row == lane % 2), 1.0, 0.0)[:8].astype(BF16)

    def exact(value, choose):
        high = value.astype(BF16)
        rest = value - high.astype(F32)
        middle = rest.astype(BF16)
        low = (rest - middle.astype(F32)).astype(BF16)
        return choose(high) + (choose(middle) + choose(low))

    wanted = exact(spectrum_ref[...], lambda part: dot(part, pick, NN))
    extra = [
        jnp.concatenate([extra_ref[0, 8 * y + t : 8 * y + t + 1] for t in range(8)], axis=1)
        for y in range(2)
    ]
    extra = jnp.concatenate(extra + [jnp.zeros((6, LENGTH), F32)])
    wanted = wanted + exact(jnp.transpose(extra), lambda part: dot(part, extra_pick, NN))
    at_row = lax.broadcasted_iota(jnp.int32, (512, 512), 0)
    at_col = lax.broadcasted_iota(jnp.int32, (512, 512), 1)
    mirror = jnp.where(at_row + at_col == 512, 1.0, 0.0).astype(BF16)
    plus = wanted[:512]
    upper = wanted[512:]
    minus = exact(upper, lambda part: dot(mirror, part, NN))
    first = lax.broadcasted_iota(jnp.int32, (512, 128), 0) == 0
    minus = jnp.where(first, plus, minus)
    lanes = lax.broadcasted_iota(jnp.int32, (512, 128), 1)
    alone = (owner == 0) & ((lanes // 8) % 8 == 0)
    scale = jnp.where(first, 1.0, 2.0) * jnp.where(alone, 1.0, 2.0) / (LENGTH * LENGTH)
    even = (plus + minus) * (0.5 * scale)
    even_ref[0:512] = even
    even_ref[512:1024] = jnp.where(first, upper * scale, even)
    odd = (plus - minus) * (0.5 * scale)
    odd_ref[...] = jnp.where(lanes < 64, -odd, odd)


def add_weights(pencil, cell_ref, wave_ref, plane_ref, weights):
    doubled = jnp.concatenate(
        [weights[g : g + 1] * plane_ref[y : y + 1] for g in range(4) for y in range(2)]
    )
    waves = (wave_ref[...][:, None, :] * doubled[None]).reshape(128, LENGTH)
    cells = lax.broadcasted_iota(jnp.int32, (LENGTH, LENGTH), 0)
    chosen = jnp.where(cells == cell_ref[...], 1.0, 0.0).astype(BF16)
    high, low = split(waves)
    both = dot(chosen, jnp.concatenate([high, low]), NT)
    return pencil + both[:, :128] + both[:, 128:]


def wait_kernel(panel, *refs):
    cell_ref, wave_ref, plane_ref, pencil_ref = refs[:4]
    unknown_refs, refs = refs[4 : 4 + panel], refs[4 + panel :]
    weights = unknown_refs[-1][16:20]
    pencil = pencil_ref[...].reshape(LENGTH, 128)
    pencil = swap_groups(pencil) if panel == 1 else pencil
    pencil = add_weights(pencil, cell_ref, wave_ref, plane_ref, weights)
    if panel == 3:
        refs[0][...] = pencil
        return
    side_ref, factor_refs, (out_ref, work_ref) = refs[0], refs[1:-2], refs[-2:]
    out_ref[...] = pencil
    work = side_ref[0]
    for ref, factor_ref in zip(unknown_refs, factor_refs):
        work = work - dot_nt(ref[...], factor_ref[...].reshape(128, LENGTH))
    work_ref[0] = work


def filter_kernel(
    pencil_ref, cell_ref, wave_ref, plane_ref, a_ref, b_ref, c_ref, d_ref,
    high_hbm, low_hbm, back_high_hbm, back_low_hbm, even_ref, odd_ref, out_ref,
    high_ref, low_ref, back_high_ref, back_low_ref, sems,
):
    sources = (high_hbm, low_hbm, back_high_hbm, back_low_hbm)
    places = (high_ref, low_ref, back_high_ref, back_low_ref)
    copies = [
        pltpu.make_async_copy(source, place, sems.at[number])
        for number, (source, place) in enumerate(zip(sources, places))
    ]
    for copy in copies:
        copy.start()
    weights = (a_ref[16:20] + b_ref[16:20]) + (c_ref[16:20] + d_ref[16:20])
    pencil = add_weights(pencil_ref[...], cell_ref, wave_ref, plane_ref, weights)
    copies[0].wait()
    copies[1].wait()
    freq = table_nn(high_ref[...], low_ref[...], pencil)
    real, imag = freq[:512], freq[512:]
    odd = odd_ref[...]
    real_out = even_ref[0:512] * real + odd * pltpu.roll(imag, 64, 1)
    imag_out = even_ref[512:1024] * imag - odd * pltpu.roll(real, 64, 1)
    copies[2].wait()
    copies[3].wait()
    back = table_nn(
        back_high_ref[...], back_low_ref[...], jnp.concatenate([real_out, imag_out])
    )
    out_ref[...] = swap_groups(back).reshape(64, 16, 128)


def close_kernel(slots_ref, high_ref, low_ref, out_ref, rows_ref):
    @pl.when(pl.program_id(0) == 0)
    def _():
        rows = jnp.transpose(slots_ref[...].reshape(LENGTH, 128))
        rows_high, rows_low = split(rows)
        rows_ref[0:128] = rows_high
        rows_ref[128:256] = rows_low

    both = dot(rows_ref[...], high_ref[...], NN)
    total = both[:128] + both[128:] + dot(rows_ref[0:128], low_ref[...], NN)
    out_ref[...] = total.reshape(out_ref.shape)


def update_kernel(index_ref, base_ref, unknown_ref, *refs):
    factor_refs, (out_ref, both_ref) = refs[:4], refs[4:]
    block = pl.program_id(0)

    def subtract(base, first):
        for panel in range(4):
            rows = factor_refs[panel][...].reshape(128, LENGTH)
            if first:
                own = index_ref[0] * 16
                row = lax.broadcasted_iota(jnp.int32, (64, LENGTH), 0)
                col = lax.broadcasted_iota(jnp.int32, (64, LENGTH), 1)
                mine = (row // 16 == panel) & (col == own + row % 16)
                rows = jnp.concatenate([jnp.where(mine, -1.0, 0.0), rows[64:]])
            rows_high, rows_low = split(rows)
            wide = dot(rows_high, both_ref[panel], NT)
            base = base - (wide[:, :128] + wide[:, 128:])
            base = base - dot(rows_low, both_ref[panel, 0:128], NT)
        out_ref[...] = base.reshape(8, 16, 128)

    base = base_ref[...].reshape(128, 128)

    @pl.when(block == 0)
    def _():
        for panel in range(4):
            rows = unknown_ref[:, 16 * panel : 16 * panel + 16, :].reshape(128, LENGTH)
            high, low = split(rows)
            both_ref[panel, 0:128] = high
            both_ref[panel, 128:256] = low
        subtract(jnp.concatenate([jnp.zeros((64, 128), F32), base[64:]]), True)

    @pl.when(block > 0)
    def _():
        subtract(base, False)


def spec(*shape):
    return pl.BlockSpec(shape, lambda *_: (0,) * len(shape))


def block_at(shape, place):
    return pl.BlockSpec(shape, lambda *_: place)


def cost(flops, moved):
    return pl.CostEstimate(flops=flops, bytes_accessed=moved, transcendentals=0)


def shape_of(*shape):
    return jax.ShapeDtypeStruct(shape, F32)


def call(body, name, in_specs, out_specs, out_shape, flops, moved, scratch=(), grid=1):
    return pl.pallas_call(
        body,
        grid=(grid,),
        in_specs=in_specs,
        out_specs=out_specs,
        out_shape=out_shape,
        scratch_shapes=scratch,
        compiler_params=LIMIT,
        cost_estimate=cost(flops, moved),
        name=name,
    )


def ring(size, step):
    return [(place, (place + step) % size) for place in range(size)]


def share(partial):
    total = partial + lax.ppermute(partial, "core", ring(2, 1))
    return [total] + [lax.ppermute(total, "x", ring(4, step)) for step in (1, 2, 3)]


def tie(*groups):
    flat = lax.optimization_barrier(tuple(group[at] for group, ats in groups for at in ats))
    flat = list(flat)
    for group, ats in groups:
        for at in ats:
            group[at] = flat.pop(0)


def update(index, base, factor, unknowns):
    return call(
        update_kernel,
        "update",
        [
            SMEM,
            pl.BlockSpec((8, 16, 128), lambda i: (i, 0, 0)),
            spec(8, 64, LENGTH),
        ]
        + [
            pl.BlockSpec((8, 16, LENGTH), lambda i, place=k: (i, 0, place))
            for k in range(4)
        ],
        pl.BlockSpec((8, 16, 128), lambda i: (i, 0, 0)),
        shape_of(32, 16, 128),
        3 * 2 * 512 * 4 * LENGTH * 128,
        11_000_000,
        [pltpu.VMEM((4, 256, LENGTH), BF16)],
        grid=4,
    )(index, base, unknowns, *[factor] * 4)


SMEM = pl.BlockSpec(memory_space=pltpu.SMEM)
ANY = pl.BlockSpec(memory_space=pl.ANY)
NEAR = pl.BlockSpec(memory_space=pltpu.VMEM)
TABLE = pltpu.VMEM((LENGTH, LENGTH), BF16)


def per_device(factor, inverses, right_side, obs_cells, noise, spectrum):
    z_high, z_low = (jnp.asarray(t) for t in halves(z_table()))
    x_high, x_low = (jnp.asarray(t) for t in halves(x_table()))
    back_high, back_low = (jnp.asarray(t) for t in halves(x_table().T))
    wide = lax.axis_index(WIDE).astype(jnp.int32)
    index = jnp.stack([wide, lax.axis_index("y").astype(jnp.int32)])

    columns, side = call(
        columns_kernel,
        "columns",
        [spec(64, LENGTH), spec(4, 16, 128)],
        [spec(8, 64, 128), spec(64, 128)],
        [shape_of(8, 64, 128), shape_of(64, 128)],
        0,
        500_000,
    )(inverses.reshape(64, LENGTH), right_side)
    box = [columns, side, factor]
    tie((box, (0, 1, 2)))
    columns, side, factor = box
    columns = lax.all_to_all(columns, ("x", "core"), 0, 0)
    extra = spectrum[:, :, 0].T.reshape(16, 128)

    lower, lower_far = call(
        lower_kernel,
        "lower",
        [block_at((1, 16, LENGTH * k), (k, 0, 0)) for k in range(1, 4)],
        [spec(32, LENGTH), spec(64, LENGTH)],
        [shape_of(32, LENGTH), shape_of(64, LENGTH)],
        0,
        800_000,
    )(factor, factor, factor)
    lower = lax.all_gather(lower, "z")

    sides = [side] + [lax.ppermute(side, "y", ring(4, step)) for step in (1, 2, 3)]
    quarter = call(
        bundle_kernel,
        "bundle",
        [SMEM, spec(8, 64, 128)] + [spec(64, 128)] * 4 + [spec(16, 128)],
        spec(8, 272, 128),
        shape_of(8, 272, 128),
        0,
        1_500_000,
    )(index, columns, *sides, extra)
    box = [quarter, noise, spectrum, obs_cells, lower_far]
    tie((box, (0, 1, 2, 3, 4)))
    quarter, noise, spectrum, obs_cells, lower_far = box
    lower_far = lax.all_gather(lower_far, "z")
    quarter = lax.all_to_all(quarter, "z", 0, 0)

    slab = call(
        noise_kernel,
        "noise",
        [spec(128, LENGTH)] + [pl.BlockSpec((256, LENGTH), lambda i: (i, 0))] * 2,
        pl.BlockSpec((16, 16, 128), lambda i: (i, 0, 0)),
        shape_of(64, 16, 128),
        3 * 2 * 128 * LENGTH * LENGTH,
        5_000_000,
        grid=4,
    )(noise.reshape(128, LENGTH), z_high, z_low)

    cell_x = (obs_cells // (8 * LENGTH)).reshape(1, 4096)
    plane = obs_cells // LENGTH % 8 - 2 * lax.axis_index("y")
    planes = jnp.stack([plane == 0, plane == 1]).astype(F32)
    freq, phase = z_frequencies(wide, jnp)
    turn = (freq[:, None] * (obs_cells % LENGTH)[None, :] + phase[:, None]) % LENGTH
    waves = jnp.cos(turn.astype(F32) * (2.0 * math.pi / LENGTH))
    box = [quarter, slab, spectrum, cell_x, planes, waves]
    tie((box, tuple(range(6))))
    quarter, slab, spectrum, cell_x, planes, waves = box
    own = quarter[:, 128:224]
    own = [own] + [lax.ppermute(own, "y", ring(4, step)) for step in (1, 2, 3)]
    slab = lax.all_to_all(slab, WIDE, 0, 0)

    obs_specs = lambda k: [
        block_at((1, LENGTH), (0, k)),
        block_at((16, LENGTH), (0, k)),
        block_at((2, LENGTH), (0, k)),
    ]
    side_spec = lambda k: block_at((1, COLS, 128), (k, 0, 0))
    factor_at = {(1, 0): 0, (2, 0): 1, (2, 1): 0, (3, 0): 1, (3, 1): 2, (3, 2): 3}
    factor_spec = lambda k, j: block_at((8, 16, LENGTH), (0, factor_at[k, j], 0))
    factor_rows = lambda k, j: lower_far if k + j > 2 else lower
    inverse_specs = lambda k: [
        block_at((8, 16, 128), (0, a if k == 1 else k + 2 * a, 0)) for a in range(2)
    ] * 4
    inverses = [one for one in range(4) for _ in range(2)]
    inverse_scratch = [pltpu.VMEM((8, 128, 128), BF16)] * 2
    panel_spec = NEAR
    panel_shape = shape_of(COLS, LENGTH)
    pencil_spec = spec(LENGTH, 128)

    partial, sides = call(
        first_kernel,
        "first",
        [block_at((8, 32, 128), (0, 7, 0)), block_at((8, 128, 128), (0, 0, 0))],
        [panel_spec, spec(4, COLS, 128)],
        [panel_shape, shape_of(4, COLS, 128)],
        20_000_000,
        1_200_000,
    )(quarter, quarter)
    box = [partial, spectrum]
    tie((box, (0, 1)))
    partial, spectrum = box
    parts = share(partial)
    even, odd = call(
        spectrum_kernel,
        "spectrum",
        [SMEM, spec(LENGTH, 32), block_at((1, 16, 128), (4, 16, 0))],
        [spec(LENGTH, 128), spec(512, 128)],
        [shape_of(LENGTH, 128), shape_of(512, 128)],
        300_000_000,
        1_500_000,
    )(index, spectrum.reshape(LENGTH, 32), quarter)
    box = [even, odd, slab]
    tie((parts, (0, 1, 2, 3)), (own, (0, 1, 2, 3)), (box, (0, 1, 2)))
    even, odd, slab = box
    unknowns = []
    work = sides
    pencil = slab
    for panel in range(1, 4):
        partial, unknown, *solved_rows = call(
            functools.partial(step_kernel, panel),
            f"step{panel}",
            [SMEM, side_spec(1 if panel == 1 else 0)]
            + [panel_spec] * 4
            + [factor_spec(panel, panel - 1)]
            + inverse_specs(panel)
            + [panel_spec] * 2 * (panel == 3),
            [panel_spec] * 2 + [spec(48, LENGTH)] * (panel == 3),
            [panel_shape] * 2 + [shape_of(48, LENGTH)] * (panel == 3),
            40_000_000,
            1_500_000,
            inverse_scratch,
        )(index, work, *parts, factor_rows(panel, panel - 1), *[own[at] for at in inverses], *unknowns * (panel == 3))
        unknowns.append(unknown)
        parts = share(partial)
        later = panel < 3
        box = list(
            call(
                functools.partial(wait_kernel, panel),
                f"wait{panel}",
                obs_specs(panel - 1)
                + [spec(64, 16, 128) if panel == 1 else pencil_spec]
                + [panel_spec] * panel
                + [side_spec(panel + 1)] * later
                + [factor_spec(panel + 1, j) for j in range(panel * later)],
                [pencil_spec] + [spec(1, COLS, 128)] * later,
                [shape_of(LENGTH, 128)] + [shape_of(1, COLS, 128)] * later,
                2 * 2 * 128 * LENGTH * LENGTH,
                1_500_000,
            )(
                cell_x, waves, planes, pencil, *unknowns, *[sides] * later,
                *[factor_rows(panel + 1, j) for j in range(panel * later)],
            )
        )
        tie((parts, (0, 1, 2, 3)), (box, (0, 1) if later else (0,)))
        pencil, work = box[0], box[-1]

    slots = call(
        filter_kernel,
        "filter",
        [spec(LENGTH, 128)]
        + obs_specs(3)
        + [panel_spec] * 4
        + [ANY] * 4
        + [spec(LENGTH, 128), spec(512, 128)],
        spec(64, 16, 128),
        shape_of(64, 16, 128),
        8 * 2 * 128 * LENGTH * LENGTH,
        11_000_000,
        [TABLE] * 4 + [pltpu.SemaphoreType.DMA((4,))],
    )(pencil, cell_x, waves, planes, *parts, x_high, x_low, back_high, back_low, even, odd)
    late = (parts[0][:16] + parts[1][:16]) + (parts[2][:16] + parts[3][:16])
    late = lax.all_gather(jnp.concatenate([solved_rows[0], late]), "z")
    slots = lax.all_to_all(slots, WIDE, 0, 0)
    correction = call(
        close_kernel,
        "close",
        [spec(64, 16, 128)] + [pl.BlockSpec((LENGTH, 256), lambda i: (0, i))] * 2,
        pl.BlockSpec((16, 4, 2, 256), lambda i: (0, 0, 0, i)),
        shape_of(16, 4, 2, LENGTH),
        3 * 2 * 128 * LENGTH * LENGTH,
        5_500_000,
        [pltpu.VMEM((256, LENGTH), BF16)],
        grid=4,
    )(slots, z_high, z_low)
    base, correction = lax.optimization_barrier((right_side, correction))
    solved = update(index, base, factor, late)
    return (solved, correction)


def solution(mesh):
    grid = Mesh(mesh.devices.reshape(8, 4, 2, 4), ("z", "x", "core", "y"))
    return jax.shard_map(
        per_device,
        mesh=grid,
        in_specs=(
            P(None, WIDE, None),
            P(None, None, WIDE, None),
            P(None, WIDE, "y"),
            P(),
            P(WIDE, None, "y", None),
            P(None, "y", WIDE),
        ),
        out_specs=(P(None, WIDE, "y"), P(WIDE, None, "y", None)),
        check_vma=False,
    )
```

```python
import functools
import math

import jax
import jax.numpy as jnp
import numpy as np
from jax import lax
from jax.experimental import pallas as pl
from jax.experimental.pallas import tpu as pltpu
from jax.sharding import Mesh, PartitionSpec as P

F32 = jnp.float32
BF16 = jnp.bfloat16
WIDE = ("z", "x", "core")
LENGTH = 1024
COLS = 24
NN = (((1,), (0,)), ((), ()))
NT = (((1,), (1,)), ((), ()))


def halves(table):
    high = table.astype(np.float32).astype(jnp.bfloat16)
    low = (table - high.astype(np.float64)).astype(np.float32).astype(jnp.bfloat16)
    return (np.asarray(high), np.asarray(low))


def z_frequencies(owner, xp):
    step = xp.arange(16) % 8
    part = xp.arange(16) // 8
    freq = 16 * owner + step + xp.where(owner >= 32, 1, 0)
    lone = (owner == 0) & (step == 0) & (part == 1)
    return (xp.where(lone, 512, freq), xp.where(lone, 0, 256 * part))


def z_table():
    rows = []
    cells = np.arange(LENGTH)
    for owner in range(64):
        freq, phase = z_frequencies(np.int64(owner), np)
        turn = (freq[:, None] * cells[None, :] + phase[:, None]) % LENGTH
        rows.append(np.cos(2.0 * np.pi * turn / LENGTH))
    return np.concatenate(rows)


def x_table():
    cells = np.arange(LENGTH)
    freq = np.concatenate([np.arange(512), np.arange(512)])
    phase = np.repeat([0, 256], 512)
    freq[512], phase[512] = 512, 0
    turn = (freq[:, None] * cells[None, :] + phase[:, None]) % LENGTH
    return np.cos(2.0 * np.pi * turn / LENGTH)


def split(value):
    high = value.astype(BF16)
    low = (value - high.astype(F32)).astype(BF16)
    return (high, low)


def dot(left, right, dims):
    return lax.dot_general(left, right, dims, preferred_element_type=F32)


def dot_nt(left, right):
    left_high, left_low = split(left)
    right_high, right_low = split(right)
    rows = left.shape[0]
    both = dot(jnp.concatenate([left_high, left_low]), right_high, NT)
    return both[:rows] + both[rows:] + dot(left_high, right_low, NT)


def table_nn(high, low, value):
    value_high, value_low = split(value)
    cols = value.shape[1]
    both = dot(high, jnp.concatenate([value_high, value_low], axis=1), NN)
    return both[:, :cols] + both[:, cols:] + dot(low, value_high, NN)


def swap_groups(value):
    row = lax.broadcasted_iota(jnp.int32, value.shape, 0)
    lane = lax.broadcasted_iota(jnp.int32, value.shape, 1)
    for bit in range(4):
        step = 1 << bit
        row_bit = (row >> bit) & 1
        lane_bit = (lane >> (3 + bit)) & 1
        up = pltpu.roll(pltpu.roll(value, LENGTH - step, 0), 8 * step, 1)
        down = pltpu.roll(pltpu.roll(value, step, 0), 128 - 8 * step, 1)
        value = jnp.where(row_bit == lane_bit, value, jnp.where(lane_bit == 1, up, down))
    return value


def columns_kernel(inverse_ref, right_ref, out_ref, side_ref):
    side_ref[...] = right_ref[...].reshape(64, 128)
    lane = lax.broadcasted_iota(jnp.int32, (64, 128), 1) // 16
    for r in range(8):
        total = jnp.zeros((64, 128), F32)
        for z in range(8):
            piece = inverse_ref[:, 128 * z : 128 * z + 128]
            piece = pltpu.roll(piece, (16 * (z - r)) % 128, 1) if z != r else piece
            total = jnp.where(lane == z, piece, total)
        out_ref[r] = total


def noise_kernel(noise_ref, high_ref, low_ref, out_ref):
    noise_high, noise_low = split(noise_ref[...])
    both = dot(high_ref[...], jnp.concatenate([noise_high, noise_low]), NT)
    slots = both[:, :128] + both[:, 128:] + dot(low_ref[...], noise_high, NT)
    out_ref[...] = slots.reshape(16, 16, 128)


def lower_kernel(one_ref, two_ref, three_ref, near_ref, far_ref):
    near_ref[0:16] = one_ref[0]
    near_ref[16:32] = two_ref[0, :, 0:LENGTH]
    far_ref[0:16] = two_ref[0, :, LENGTH : 2 * LENGTH]
    for j in range(3):
        far_ref[16 * j + 16 : 16 * j + 32] = three_ref[0, :, LENGTH * j : LENGTH * (j + 1)]


def bundle_kernel(index_ref, columns_ref, *refs):
    side_refs, extra_ref, out_ref = refs[:4], refs[4], refs[5]
    lane = lax.broadcasted_iota(jnp.int32, (64, 128), 1)
    weights = jnp.zeros((64, 128), F32)
    for step, ref in enumerate(side_refs):
        y = lax.rem(index_ref[1] + 4 - step, 4)
        weights = jnp.where(lane == y + 16, ref[:, 0:1], weights)
    side = side_refs[0][...]
    quarter = columns_ref[pl.ds(2 * index_ref[1], 2)]
    second = quarter[:, 16:32].reshape(32, 128)
    others = quarter[:, 32:64].reshape(64, 128)
    whole = columns_ref[:, 0:16, :].reshape(128, 128)
    for z in range(8):
        own = pltpu.roll(side, (128 - 16 * z) % 128, 1) if z else side
        rows = jnp.where(lane < 16, own, weights)
        out_ref[z, 0:128] = whole
        out_ref[z, 128:160] = second
        out_ref[z, 160:224] = others
        out_ref[z, 224:256] = jnp.transpose(jnp.concatenate([rows, rows]))[:32]
        out_ref[z, 256:272] = extra_ref[...]


def product(work, rows_high, rows_low):
    high, low = split(work)
    wide = dot(jnp.concatenate([high, low]), rows_high, NT)
    return wide[:COLS] + wide[COLS:] + dot(high, rows_low, NT)


def spread(work, index_ref, inverse_refs, out_ref, high_ref, low_ref):
    for number, ref in enumerate(inverse_refs):
        y = lax.rem(index_ref[1] + 4 - number // 2, 4)
        start = pl.multiple_of(32 * y + 16 * (number % 2), 16)
        rows_high, rows_low = split(ref[...])
        high_ref[:, pl.ds(start, 16), :] = rows_high
        low_ref[:, pl.ds(start, 16), :] = rows_low
    rows_high = high_ref[...].reshape(LENGTH, 128)
    out_ref[...] = product(work, rows_high, low_ref[...].reshape(LENGTH, 128))


def first_kernel(slab_ref, inverse_ref, out_ref, side_ref):
    lane = lax.broadcasted_iota(jnp.int32, (COLS, 128), 1) // 16
    for k in range(4):
        rows = jnp.zeros((COLS, 128), F32)
        for z in range(8):
            piece = slab_ref[z, 0:COLS]
            turn = (16 * (z - k)) % 128
            piece = pltpu.roll(piece, turn, 1) if turn else piece
            rows = jnp.where(lane == z, piece, rows)
        side_ref[k] = rows
    out_ref[...] = product(side_ref[0], *split(inverse_ref[...].reshape(LENGTH, 128)))


def step_kernel(panel, index_ref, start_ref, a_ref, b_ref, c_ref, d_ref, factor_ref, *refs):
    inverse_refs, refs = refs[:8], refs[8:]
    unknown = (a_ref[...] + b_ref[...]) + (c_ref[...] + d_ref[...])
    if panel == 3:
        older_refs, refs = refs[:2], refs[2:]
        refs[2][0:16] = older_refs[0][0:16]
        refs[2][16:32] = older_refs[1][0:16]
        refs[2][32:48] = unknown[0:16]
    out_ref, unknown_ref, high_ref, low_ref = refs[0], refs[1], refs[-2], refs[-1]
    unknown_ref[...] = unknown
    work = start_ref[0] - dot_nt(unknown, factor_ref[...].reshape(128, LENGTH))
    spread(work, index_ref, inverse_refs, out_ref, high_ref, low_ref)


def spectrum_kernel(index_ref, spectrum_ref, extra_ref, even_ref, odd_ref):
    owner = index_ref[0]
    row = lax.broadcasted_iota(jnp.int32, (32, 128), 0)
    lane = lax.broadcasted_iota(jnp.int32, (32, 128), 1)
    lone = (owner == 0) & (lane // 8 == 8)
    same_y = row // 16 == lane % 2
    same_z = row % 16 == (lane // 8) % 8 + jnp.where(owner >= 32, 1, 0)
    pick = jnp.where(same_y & same_z & jnp.logical_not(lone), 1.0, 0.0).astype(BF16)
    extra_pick = jnp.where(lone & (row == lane % 2), 1.0, 0.0)[:8].astype(BF16)

    def exact(value, choose):
        high = value.astype(BF16)
        rest = value - high.astype(F32)
        middle = rest.astype(BF16)
        low = (rest - middle.astype(F32)).astype(BF16)
        return choose(high) + (choose(middle) + choose(low))

    wanted = exact(spectrum_ref[...], lambda part: dot(part, pick, NN))
    extra = [
        jnp.concatenate([extra_ref[0, 8 * y + t : 8 * y + t + 1] for t in range(8)], axis=1)
        for y in range(2)
    ]
    extra = jnp.concatenate(extra + [jnp.zeros((6, LENGTH), F32)])
    wanted = wanted + exact(jnp.transpose(extra), lambda part: dot(part, extra_pick, NN))
    at_row = lax.broadcasted_iota(jnp.int32, (512, 512), 0)
    at_col = lax.broadcasted_iota(jnp.int32, (512, 512), 1)
    mirror = jnp.where(at_row + at_col == 512, 1.0, 0.0).astype(BF16)
    plus = wanted[:512]
    upper = wanted[512:]
    minus = exact(upper, lambda part: dot(mirror, part, NN))
    first = lax.broadcasted_iota(jnp.int32, (512, 128), 0) == 0
    minus = jnp.where(first, plus, minus)
    lanes = lax.broadcasted_iota(jnp.int32, (512, 128), 1)
    alone = (owner == 0) & ((lanes // 8) % 8 == 0)
    scale = jnp.where(first, 1.0, 2.0) * jnp.where(alone, 1.0, 2.0) / (LENGTH * LENGTH)
    even = (plus + minus) * (0.5 * scale)
    even_ref[0:512] = even
    even_ref[512:1024] = jnp.where(first, upper * scale, even)
    odd = (plus - minus) * (0.5 * scale)
    odd_ref[...] = jnp.where(lanes < 64, -odd, odd)


def add_weights(pencil, cell_ref, wave_ref, plane_ref, weights):
    doubled = jnp.concatenate(
        [weights[g : g + 1] * plane_ref[y : y + 1] for g in range(4) for y in range(2)]
    )
    waves = (wave_ref[...][:, None, :] * doubled[None]).reshape(128, LENGTH)
    cells = lax.broadcasted_iota(jnp.int32, (LENGTH, LENGTH), 0)
    chosen = jnp.where(cells == cell_ref[...], 1.0, 0.0).astype(BF16)
    high, low = split(waves)
    both = dot(chosen, jnp.concatenate([high, low]), NT)
    return pencil + both[:, :128] + both[:, 128:]


def wait_kernel(panel, *refs):
    cell_ref, wave_ref, plane_ref, pencil_ref = refs[:4]
    unknown_refs, refs = refs[4 : 4 + panel], refs[4 + panel :]
    weights = unknown_refs[-1][16:20]
    pencil = pencil_ref[...].reshape(LENGTH, 128)
    pencil = swap_groups(pencil) if panel == 1 else pencil
    pencil = add_weights(pencil, cell_ref, wave_ref, plane_ref, weights)
    if panel == 3:
        refs[0][...] = pencil
        return
    side_ref, factor_refs, (out_ref, work_ref) = refs[0], refs[1:-2], refs[-2:]
    out_ref[...] = pencil
    work = side_ref[0]
    for ref, factor_ref in zip(unknown_refs, factor_refs):
        work = work - dot_nt(ref[...], factor_ref[...].reshape(128, LENGTH))
    work_ref[0] = work


def filter_kernel(
    pencil_ref, cell_ref, wave_ref, plane_ref, a_ref, b_ref, c_ref, d_ref,
    high_hbm, low_hbm, back_high_hbm, back_low_hbm, even_ref, odd_ref, out_ref,
    high_ref, low_ref, back_high_ref, back_low_ref, sems,
):
    sources = (high_hbm, low_hbm, back_high_hbm, back_low_hbm)
    places = (high_ref, low_ref, back_high_ref, back_low_ref)
    copies = [
        pltpu.make_async_copy(source, place, sems.at[number])
        for number, (source, place) in enumerate(zip(sources, places))
    ]
    for copy in copies:
        copy.start()
    weights = (a_ref[16:20] + b_ref[16:20]) + (c_ref[16:20] + d_ref[16:20])
    pencil = add_weights(pencil_ref[...], cell_ref, wave_ref, plane_ref, weights)
    copies[0].wait()
    copies[1].wait()
    freq = table_nn(high_ref[...], low_ref[...], pencil)
    real, imag = freq[:512], freq[512:]
    odd = odd_ref[...]
    real_out = even_ref[0:512] * real + odd * pltpu.roll(imag, 64, 1)
    imag_out = even_ref[512:1024] * imag - odd * pltpu.roll(real, 64, 1)
    copies[2].wait()
    copies[3].wait()
    back = table_nn(
        back_high_ref[...], back_low_ref[...], jnp.concatenate([real_out, imag_out])
    )
    out_ref[...] = swap_groups(back).reshape(64, 16, 128)


def close_kernel(slots_ref, high_ref, low_ref, out_ref, rows_ref):
    @pl.when(pl.program_id(0) == 0)
    def _():
        rows = jnp.transpose(slots_ref[...].reshape(LENGTH, 128))
        rows_high, rows_low = split(rows)
        rows_ref[0:128] = rows_high
        rows_ref[128:256] = rows_low

    both = dot(rows_ref[...], high_ref[...], NN)
    total = both[:128] + both[128:] + dot(rows_ref[0:128], low_ref[...], NN)
    out_ref[...] = total.reshape(out_ref.shape)


def update_kernel(index_ref, base_ref, unknown_ref, *refs):
    factor_refs, (out_ref, both_ref) = refs[:4], refs[4:]
    block = pl.program_id(0)

    def subtract(base, first):
        for panel in range(4):
            rows = factor_refs[panel][...].reshape(128, LENGTH)
            if first:
                own = index_ref[0] * 16
                row = lax.broadcasted_iota(jnp.int32, (64, LENGTH), 0)
                col = lax.broadcasted_iota(jnp.int32, (64, LENGTH), 1)
                mine = (row // 16 == panel) & (col == own + row % 16)
                rows = jnp.concatenate([jnp.where(mine, -1.0, 0.0), rows[64:]])
            rows_high, rows_low = split(rows)
            wide = dot(rows_high, both_ref[panel], NT)
            base = base - (wide[:, :128] + wide[:, 128:])
            base = base - dot(rows_low, both_ref[panel, 0:128], NT)
        out_ref[...] = base.reshape(8, 16, 128)

    base = base_ref[...].reshape(128, 128)

    @pl.when(block == 0)
    def _():
        for panel in range(4):
            rows = unknown_ref[:, 16 * panel : 16 * panel + 16, :].reshape(128, LENGTH)
            high, low = split(rows)
            both_ref[panel, 0:128] = high
            both_ref[panel, 128:256] = low
        subtract(jnp.concatenate([jnp.zeros((64, 128), F32), base[64:]]), True)

    @pl.when(block > 0)
    def _():
        subtract(base, False)


def spec(*shape):
    return pl.BlockSpec(shape, lambda *_: (0,) * len(shape))


def block_at(shape, place):
    return pl.BlockSpec(shape, lambda *_: place)


def cost(flops, moved):
    return pl.CostEstimate(flops=flops, bytes_accessed=moved, transcendentals=0)


def shape_of(*shape):
    return jax.ShapeDtypeStruct(shape, F32)


def call(
    body, name, in_specs, out_specs, out_shape, flops, moved, scratch=(), grid=1, room=40
):
    return pl.pallas_call(
        body,
        grid=(grid,),
        in_specs=in_specs,
        out_specs=out_specs,
        out_shape=out_shape,
        scratch_shapes=scratch,
        compiler_params=pltpu.CompilerParams(vmem_limit_bytes=room * 1024 * 1024),
        cost_estimate=cost(flops, moved),
        name=name,
    )


def ring(size, step):
    return [(place, (place + step) % size) for place in range(size)]


def share(partial):
    total = partial + lax.ppermute(partial, "core", ring(2, 1))
    return [total] + [lax.ppermute(total, "x", ring(4, step)) for step in (1, 2, 3)]


def tie(*groups):
    flat = lax.optimization_barrier(tuple(group[at] for group, ats in groups for at in ats))
    flat = list(flat)
    for group, ats in groups:
        for at in ats:
            group[at] = flat.pop(0)


def update(index, base, factor, unknowns):
    return call(
        update_kernel,
        "update",
        [
            SMEM,
            pl.BlockSpec((8, 16, 128), lambda i: (i, 0, 0)),
            spec(8, 64, LENGTH),
        ]
        + [
            pl.BlockSpec((8, 16, LENGTH), lambda i, place=k: (i, 0, place))
            for k in range(4)
        ],
        pl.BlockSpec((8, 16, 128), lambda i: (i, 0, 0)),
        shape_of(32, 16, 128),
        3 * 2 * 512 * 4 * LENGTH * 128,
        11_000_000,
        [pltpu.VMEM((4, 256, LENGTH), BF16)],
        grid=4,
        room=56,
    )(index, base, unknowns, *[factor] * 4)


SMEM = pl.BlockSpec(memory_space=pltpu.SMEM)
ANY = pl.BlockSpec(memory_space=pl.ANY)
NEAR = pl.BlockSpec(memory_space=pltpu.VMEM)
TABLE = pltpu.VMEM((LENGTH, LENGTH), BF16)


def per_device(factor, inverses, right_side, obs_cells, noise, spectrum):
    z_high, z_low = (jnp.asarray(t) for t in halves(z_table()))
    x_high, x_low = (jnp.asarray(t) for t in halves(x_table()))
    back_high, back_low = (jnp.asarray(t) for t in halves(x_table().T))
    wide = lax.axis_index(WIDE).astype(jnp.int32)
    index = jnp.stack([wide, lax.axis_index("y").astype(jnp.int32)])

    columns, side = call(
        columns_kernel,
        "columns",
        [spec(64, LENGTH), spec(4, 16, 128)],
        [spec(8, 64, 128), spec(64, 128)],
        [shape_of(8, 64, 128), shape_of(64, 128)],
        0,
        500_000,
    )(inverses.reshape(64, LENGTH), right_side)
    box = [columns, side, factor]
    tie((box, (0, 1, 2)))
    columns, side, factor = box
    columns = lax.all_to_all(columns, ("x", "core"), 0, 0)
    extra = spectrum[:, :, 0].T.reshape(16, 128)

    lower, lower_far = call(
        lower_kernel,
        "lower",
        [block_at((1, 16, LENGTH * k), (k, 0, 0)) for k in range(1, 4)],
        [spec(32, LENGTH), spec(64, LENGTH)],
        [shape_of(32, LENGTH), shape_of(64, LENGTH)],
        0,
        800_000,
    )(factor, factor, factor)
    lower = lax.all_gather(lower, "z")

    sides = [side] + [lax.ppermute(side, "y", ring(4, step)) for step in (1, 2, 3)]
    quarter = call(
        bundle_kernel,
        "bundle",
        [SMEM, spec(8, 64, 128)] + [spec(64, 128)] * 4 + [spec(16, 128)],
        spec(8, 272, 128),
        shape_of(8, 272, 128),
        0,
        1_500_000,
    )(index, columns, *sides, extra)
    box = [quarter, noise, spectrum, obs_cells, lower_far]
    tie((box, (0, 1, 2, 3, 4)))
    quarter, noise, spectrum, obs_cells, lower_far = box
    lower_far = lax.all_gather(lower_far, "z")
    quarter = lax.all_to_all(quarter, "z", 0, 0)

    slab = call(
        noise_kernel,
        "noise",
        [spec(128, LENGTH)] + [pl.BlockSpec((256, LENGTH), lambda i: (i, 0))] * 2,
        pl.BlockSpec((16, 16, 128), lambda i: (i, 0, 0)),
        shape_of(64, 16, 128),
        3 * 2 * 128 * LENGTH * LENGTH,
        5_000_000,
        grid=4,
    )(noise.reshape(128, LENGTH), z_high, z_low)

    cell_x = (obs_cells // (8 * LENGTH)).reshape(1, 4096)
    plane = obs_cells // LENGTH % 8 - 2 * lax.axis_index("y")
    planes = jnp.stack([plane == 0, plane == 1]).astype(F32)
    freq, phase = z_frequencies(wide, jnp)
    turn = (freq[:, None] * (obs_cells % LENGTH)[None, :] + phase[:, None]) % LENGTH
    waves = jnp.cos(turn.astype(F32) * (2.0 * math.pi / LENGTH))
    box = [quarter, slab, spectrum, cell_x, planes, waves]
    tie((box, tuple(range(6))))
    quarter, slab, spectrum, cell_x, planes, waves = box
    own = quarter[:, 128:224]
    own = [own] + [lax.ppermute(own, "y", ring(4, step)) for step in (1, 2, 3)]
    slab = lax.all_to_all(slab, WIDE, 0, 0)

    obs_specs = lambda k: [
        block_at((1, LENGTH), (0, k)),
        block_at((16, LENGTH), (0, k)),
        block_at((2, LENGTH), (0, k)),
    ]
    side_spec = lambda k: block_at((1, COLS, 128), (k, 0, 0))
    factor_at = {(1, 0): 0, (2, 0): 1, (2, 1): 0, (3, 0): 1, (3, 1): 2, (3, 2): 3}
    factor_spec = lambda k, j: block_at((8, 16, LENGTH), (0, factor_at[k, j], 0))
    factor_rows = lambda k, j: lower_far if k + j > 2 else lower
    inverse_specs = lambda k: [
        block_at((8, 16, 128), (0, a if k == 1 else k + 2 * a, 0)) for a in range(2)
    ] * 4
    inverses = [one for one in range(4) for _ in range(2)]
    inverse_scratch = [pltpu.VMEM((8, 128, 128), BF16)] * 2
    panel_spec = NEAR
    panel_shape = shape_of(COLS, LENGTH)
    pencil_spec = spec(LENGTH, 128)

    partial, sides = call(
        first_kernel,
        "first",
        [block_at((8, 32, 128), (0, 7, 0)), block_at((8, 128, 128), (0, 0, 0))],
        [panel_spec, spec(4, COLS, 128)],
        [panel_shape, shape_of(4, COLS, 128)],
        20_000_000,
        1_200_000,
    )(quarter, quarter)
    box = [partial, spectrum]
    tie((box, (0, 1)))
    partial, spectrum = box
    parts = share(partial)
    even, odd = call(
        spectrum_kernel,
        "spectrum",
        [SMEM, spec(LENGTH, 32), block_at((1, 16, 128), (4, 16, 0))],
        [spec(LENGTH, 128), spec(512, 128)],
        [shape_of(LENGTH, 128), shape_of(512, 128)],
        300_000_000,
        1_500_000,
    )(index, spectrum.reshape(LENGTH, 32), quarter)
    box = [even, odd, slab]
    tie((parts, (0, 1, 2, 3)), (own, (0, 1, 2, 3)), (box, (0, 1, 2)))
    even, odd, slab = box
    unknowns = []
    work = sides
    pencil = slab
    for panel in range(1, 4):
        partial, unknown, *solved_rows = call(
            functools.partial(step_kernel, panel),
            f"step{panel}",
            [SMEM, side_spec(1 if panel == 1 else 0)]
            + [panel_spec] * 4
            + [factor_spec(panel, panel - 1)]
            + inverse_specs(panel)
            + [panel_spec] * 2 * (panel == 3),
            [panel_spec] * 2 + [spec(48, LENGTH)] * (panel == 3),
            [panel_shape] * 2 + [shape_of(48, LENGTH)] * (panel == 3),
            40_000_000,
            1_500_000,
            inverse_scratch,
            room=56 if panel == 1 else 40,
        )(index, work, *parts, factor_rows(panel, panel - 1), *[own[at] for at in inverses], *unknowns * (panel == 3))
        unknowns.append(unknown)
        parts = share(partial)
        later = panel < 3
        box = list(
            call(
                functools.partial(wait_kernel, panel),
                f"wait{panel}",
                obs_specs(panel - 1)
                + [spec(64, 16, 128) if panel == 1 else pencil_spec]
                + [panel_spec] * panel
                + [side_spec(panel + 1)] * later
                + [factor_spec(panel + 1, j) for j in range(panel * later)],
                [pencil_spec] + [spec(1, COLS, 128)] * later,
                [shape_of(LENGTH, 128)] + [shape_of(1, COLS, 128)] * later,
                2 * 2 * 128 * LENGTH * LENGTH,
                1_500_000,
            )(
                cell_x, waves, planes, pencil, *unknowns, *[sides] * later,
                *[factor_rows(panel + 1, j) for j in range(panel * later)],
            )
        )
        tie((parts, (0, 1, 2, 3)), (box, (0, 1) if later else (0,)))
        pencil, work = box[0], box[-1]

    slots = call(
        filter_kernel,
        "filter",
        [spec(LENGTH, 128)]
        + obs_specs(3)
        + [panel_spec] * 4
        + [ANY] * 4
        + [spec(LENGTH, 128), spec(512, 128)],
        spec(64, 16, 128),
        shape_of(64, 16, 128),
        8 * 2 * 128 * LENGTH * LENGTH,
        11_000_000,
        [TABLE] * 4 + [pltpu.SemaphoreType.DMA((4,))],
        room=56,
    )(pencil, cell_x, waves, planes, *parts, x_high, x_low, back_high, back_low, even, odd)
    late = (parts[0][:16] + parts[1][:16]) + (parts[2][:16] + parts[3][:16])
    late = lax.all_gather(jnp.concatenate([solved_rows[0], late]), "z")
    slots = lax.all_to_all(slots, WIDE, 0, 0)
    correction = call(
        close_kernel,
        "close",
        [spec(64, 16, 128)] + [pl.BlockSpec((LENGTH, 256), lambda i: (0, i))] * 2,
        pl.BlockSpec((16, 4, 2, 256), lambda i: (0, 0, 0, i)),
        shape_of(16, 4, 2, LENGTH),
        3 * 2 * 128 * LENGTH * LENGTH,
        5_500_000,
        [pltpu.VMEM((256, LENGTH), BF16)],
        grid=4,
    )(slots, z_high, z_low)
    base, correction = lax.optimization_barrier((right_side, correction))
    solved = update(index, base, factor, late)
    return (solved, correction)


def solution(mesh):
    grid = Mesh(mesh.devices.reshape(8, 4, 2, 4), ("z", "x", "core", "y"))
    return jax.shard_map(
        per_device,
        mesh=grid,
        in_specs=(
            P(None, WIDE, None),
            P(None, None, WIDE, None),
            P(None, WIDE, "y"),
            P(),
            P(WIDE, None, "y", None),
            P(None, "y", WIDE),
        ),
        out_specs=(P(None, WIDE, "y"), P(WIDE, None, "y", None)),
        check_vma=False,
    )
```

```python
import functools
import math

import jax
import jax.numpy as jnp
import numpy as np
from jax import lax
from jax.experimental import pallas as pl
from jax.experimental.pallas import tpu as pltpu
from jax.sharding import Mesh, PartitionSpec as P

F32 = jnp.float32
BF16 = jnp.bfloat16
WIDE = ("z", "x", "core")
LENGTH = 1024
COLS = 24
NN = (((1,), (0,)), ((), ()))
NT = (((1,), (1,)), ((), ()))


def halves(table):
    high = table.astype(np.float32).astype(jnp.bfloat16)
    low = (table - high.astype(np.float64)).astype(np.float32).astype(jnp.bfloat16)
    return (np.asarray(high), np.asarray(low))


def z_frequencies(owner, xp):
    step = xp.arange(16) % 8
    part = xp.arange(16) // 8
    freq = 16 * owner + step + xp.where(owner >= 32, 1, 0)
    lone = (owner == 0) & (step == 0) & (part == 1)
    return (xp.where(lone, 512, freq), xp.where(lone, 0, 256 * part))


def z_table():
    rows = []
    cells = np.arange(LENGTH)
    for owner in range(64):
        freq, phase = z_frequencies(np.int64(owner), np)
        turn = (freq[:, None] * cells[None, :] + phase[:, None]) % LENGTH
        rows.append(np.cos(2.0 * np.pi * turn / LENGTH))
    return np.concatenate(rows)


def x_table():
    cells = np.arange(LENGTH)
    freq = np.concatenate([np.arange(512), np.arange(512)])
    phase = np.repeat([0, 256], 512)
    freq[512], phase[512] = 512, 0
    turn = (freq[:, None] * cells[None, :] + phase[:, None]) % LENGTH
    return np.cos(2.0 * np.pi * turn / LENGTH)


def split(value):
    high = value.astype(BF16)
    low = (value - high.astype(F32)).astype(BF16)
    return (high, low)


def dot(left, right, dims):
    return lax.dot_general(left, right, dims, preferred_element_type=F32)


def dot_nt(left, right):
    left_high, left_low = split(left)
    right_high, right_low = split(right)
    rows = left.shape[0]
    both = dot(jnp.concatenate([left_high, left_low]), right_high, NT)
    return both[:rows] + both[rows:] + dot(left_high, right_low, NT)


def table_nn(high, low, value):
    value_high, value_low = split(value)
    cols = value.shape[1]
    both = dot(high, jnp.concatenate([value_high, value_low], axis=1), NN)
    return both[:, :cols] + both[:, cols:] + dot(low, value_high, NN)


def swap_groups(value):
    row = lax.broadcasted_iota(jnp.int32, value.shape, 0)
    lane = lax.broadcasted_iota(jnp.int32, value.shape, 1)
    for bit in range(4):
        step = 1 << bit
        row_bit = (row >> bit) & 1
        lane_bit = (lane >> (3 + bit)) & 1
        up = pltpu.roll(pltpu.roll(value, LENGTH - step, 0), 8 * step, 1)
        down = pltpu.roll(pltpu.roll(value, step, 0), 128 - 8 * step, 1)
        value = jnp.where(row_bit == lane_bit, value, jnp.where(lane_bit == 1, up, down))
    return value


def columns_kernel(inverse_ref, right_ref, out_ref, side_ref):
    side_ref[...] = right_ref[...].reshape(64, 128)
    lane = lax.broadcasted_iota(jnp.int32, (64, 128), 1) // 16
    for r in range(8):
        total = jnp.zeros((64, 128), F32)
        for z in range(8):
            piece = inverse_ref[:, 128 * z : 128 * z + 128]
            piece = pltpu.roll(piece, (16 * (z - r)) % 128, 1) if z != r else piece
            total = jnp.where(lane == z, piece, total)
        out_ref[r] = total


def noise_kernel(noise_ref, high_ref, low_ref, out_ref):
    noise_high, noise_low = split(noise_ref[...])
    both = dot(high_ref[...], jnp.concatenate([noise_high, noise_low]), NT)
    slots = both[:, :128] + both[:, 128:] + dot(low_ref[...], noise_high, NT)
    out_ref[...] = slots.reshape(16, 16, 128)


def lower_kernel(one_ref, two_ref, three_ref, near_ref, far_ref):
    near_ref[0:16] = one_ref[0]
    near_ref[16:32] = two_ref[0, :, 0:LENGTH]
    far_ref[0:16] = two_ref[0, :, LENGTH : 2 * LENGTH]
    for j in range(3):
        far_ref[16 * j + 16 : 16 * j + 32] = three_ref[0, :, LENGTH * j : LENGTH * (j + 1)]


def bundle_kernel(index_ref, columns_ref, *refs):
    side_refs, extra_ref, out_ref = refs[:4], refs[4], refs[5]
    lane = lax.broadcasted_iota(jnp.int32, (64, 128), 1)
    weights = jnp.zeros((64, 128), F32)
    for step, ref in enumerate(side_refs):
        y = lax.rem(index_ref[1] + 4 - step, 4)
        weights = jnp.where(lane == y + 16, ref[:, 0:1], weights)
    side = side_refs[0][...]
    quarter = columns_ref[pl.ds(2 * index_ref[1], 2)]
    second = quarter[:, 16:32].reshape(32, 128)
    others = quarter[:, 32:64].reshape(64, 128)
    whole = columns_ref[:, 0:16, :].reshape(128, 128)
    for z in range(8):
        own = pltpu.roll(side, (128 - 16 * z) % 128, 1) if z else side
        rows = jnp.where(lane < 16, own, weights)
        out_ref[z, 0:128] = whole
        out_ref[z, 128:160] = second
        out_ref[z, 160:224] = others
        out_ref[z, 224:256] = jnp.transpose(jnp.concatenate([rows, rows]))[:32]
        out_ref[z, 256:272] = extra_ref[...]


def product(work, rows_high, rows_low):
    high, low = split(work)
    wide = dot(jnp.concatenate([high, low]), rows_high, NT)
    return wide[:COLS] + wide[COLS:] + dot(high, rows_low, NT)


def spread(work, index_ref, inverse_refs, out_ref, high_ref, low_ref):
    for number, ref in enumerate(inverse_refs):
        y = lax.rem(index_ref[1] + 4 - number // 2, 4)
        start = pl.multiple_of(32 * y + 16 * (number % 2), 16)
        rows_high, rows_low = split(ref[...])
        high_ref[:, pl.ds(start, 16), :] = rows_high
        low_ref[:, pl.ds(start, 16), :] = rows_low
    rows_high = high_ref[...].reshape(LENGTH, 128)
    out_ref[...] = product(work, rows_high, low_ref[...].reshape(LENGTH, 128))


def first_kernel(slab_ref, inverse_ref, out_ref, side_ref):
    lane = lax.broadcasted_iota(jnp.int32, (COLS, 128), 1) // 16
    for k in range(4):
        rows = jnp.zeros((COLS, 128), F32)
        for z in range(8):
            piece = slab_ref[z, 0:COLS]
            turn = (16 * (z - k)) % 128
            piece = pltpu.roll(piece, turn, 1) if turn else piece
            rows = jnp.where(lane == z, piece, rows)
        side_ref[k] = rows
    out_ref[...] = product(side_ref[0], *split(inverse_ref[...].reshape(LENGTH, 128)))


def step_kernel(panel, index_ref, start_ref, a_ref, b_ref, c_ref, d_ref, factor_ref, *refs):
    inverse_refs, refs = refs[:8], refs[8:]
    unknown = (a_ref[...] + b_ref[...]) + (c_ref[...] + d_ref[...])
    if panel == 3:
        older_refs, refs = refs[:2], refs[2:]
        refs[2][0:16] = older_refs[0][0:16]
        refs[2][16:32] = older_refs[1][0:16]
        refs[2][32:48] = unknown[0:16]
    out_ref, unknown_ref, high_ref, low_ref = refs[0], refs[1], refs[-2], refs[-1]
    unknown_ref[...] = unknown
    work = start_ref[0] - dot_nt(unknown, factor_ref[...].reshape(128, LENGTH))
    spread(work, index_ref, inverse_refs, out_ref, high_ref, low_ref)


def spectrum_kernel(index_ref, spectrum_ref, extra_ref, even_ref, odd_ref):
    owner = index_ref[0]
    row = lax.broadcasted_iota(jnp.int32, (32, 128), 0)
    lane = lax.broadcasted_iota(jnp.int32, (32, 128), 1)
    lone = (owner == 0) & (lane // 8 == 8)
    same_y = row // 16 == lane % 2
    same_z = row % 16 == (lane // 8) % 8 + jnp.where(owner >= 32, 1, 0)
    pick = jnp.where(same_y & same_z & jnp.logical_not(lone), 1.0, 0.0).astype(BF16)
    extra_pick = jnp.where(lone & (row == lane % 2), 1.0, 0.0)[:8].astype(BF16)

    def exact(value, choose):
        high = value.astype(BF16)
        rest = value - high.astype(F32)
        middle = rest.astype(BF16)
        low = (rest - middle.astype(F32)).astype(BF16)
        return choose(high) + (choose(middle) + choose(low))

    wanted = exact(spectrum_ref[...], lambda part: dot(part, pick, NN))
    extra = [
        jnp.concatenate([extra_ref[0, 8 * y + t : 8 * y + t + 1] for t in range(8)], axis=1)
        for y in range(2)
    ]
    extra = jnp.concatenate(extra + [jnp.zeros((6, LENGTH), F32)])
    wanted = wanted + exact(jnp.transpose(extra), lambda part: dot(part, extra_pick, NN))
    at_row = lax.broadcasted_iota(jnp.int32, (512, 512), 0)
    at_col = lax.broadcasted_iota(jnp.int32, (512, 512), 1)
    mirror = jnp.where(at_row + at_col == 512, 1.0, 0.0).astype(BF16)
    plus = wanted[:512]
    upper = wanted[512:]
    minus = exact(upper, lambda part: dot(mirror, part, NN))
    first = lax.broadcasted_iota(jnp.int32, (512, 128), 0) == 0
    minus = jnp.where(first, plus, minus)
    lanes = lax.broadcasted_iota(jnp.int32, (512, 128), 1)
    alone = (owner == 0) & ((lanes // 8) % 8 == 0)
    scale = jnp.where(first, 1.0, 2.0) * jnp.where(alone, 1.0, 2.0) / (LENGTH * LENGTH)
    even = (plus + minus) * (0.5 * scale)
    even_ref[0:512] = even
    even_ref[512:1024] = jnp.where(first, upper * scale, even)
    odd = (plus - minus) * (0.5 * scale)
    odd_ref[...] = jnp.where(lanes < 64, -odd, odd)


def add_weights(pencil, cell_ref, wave_ref, plane_ref, weights):
    doubled = jnp.concatenate(
        [weights[g : g + 1] * plane_ref[y : y + 1] for g in range(4) for y in range(2)]
    )
    waves = (wave_ref[...][:, None, :] * doubled[None]).reshape(128, LENGTH)
    cells = lax.broadcasted_iota(jnp.int32, (LENGTH, LENGTH), 0)
    chosen = jnp.where(cells == cell_ref[...], 1.0, 0.0).astype(BF16)
    high, low = split(waves)
    both = dot(chosen, jnp.concatenate([high, low]), NT)
    return pencil + both[:, :128] + both[:, 128:]


def wait_kernel(panel, *refs):
    cell_ref, wave_ref, plane_ref, pencil_ref = refs[:4]
    unknown_refs, refs = refs[4 : 4 + panel], refs[4 + panel :]
    weights = unknown_refs[-1][16:20]
    pencil = pencil_ref[...].reshape(LENGTH, 128)
    pencil = swap_groups(pencil) if panel == 1 else pencil
    pencil = add_weights(pencil, cell_ref, wave_ref, plane_ref, weights)
    if panel == 3:
        refs[0][...] = pencil
        return
    side_ref, factor_refs, (out_ref, work_ref) = refs[0], refs[1:-2], refs[-2:]
    out_ref[...] = pencil
    work = side_ref[0]
    for ref, factor_ref in zip(unknown_refs, factor_refs):
        work = work - dot_nt(ref[...], factor_ref[...].reshape(128, LENGTH))
    work_ref[0] = work


def filter_kernel(
    pencil_ref, cell_ref, wave_ref, plane_ref, a_ref, b_ref, c_ref, d_ref,
    high_hbm, low_hbm, back_high_hbm, back_low_hbm, even_ref, odd_ref, out_ref,
    high_ref, low_ref, back_high_ref, back_low_ref, sems,
):
    sources = (high_hbm, low_hbm, back_high_hbm, back_low_hbm)
    places = (high_ref, low_ref, back_high_ref, back_low_ref)
    copies = [
        pltpu.make_async_copy(source, place, sems.at[number])
        for number, (source, place) in enumerate(zip(sources, places))
    ]
    for copy in copies:
        copy.start()
    weights = (a_ref[16:20] + b_ref[16:20]) + (c_ref[16:20] + d_ref[16:20])
    pencil = add_weights(pencil_ref[...], cell_ref, wave_ref, plane_ref, weights)
    copies[0].wait()
    copies[1].wait()
    freq = table_nn(high_ref[...], low_ref[...], pencil)
    real, imag = freq[:512], freq[512:]
    odd = odd_ref[...]
    real_out = even_ref[0:512] * real + odd * pltpu.roll(imag, 64, 1)
    imag_out = even_ref[512:1024] * imag - odd * pltpu.roll(real, 64, 1)
    copies[2].wait()
    copies[3].wait()
    back = table_nn(
        back_high_ref[...], back_low_ref[...], jnp.concatenate([real_out, imag_out])
    )
    out_ref[...] = swap_groups(back).reshape(64, 16, 128)


def close_kernel(slots_ref, high_ref, low_ref, out_ref, rows_ref):
    @pl.when(pl.program_id(0) == 0)
    def _():
        rows = jnp.transpose(slots_ref[...].reshape(LENGTH, 128))
        rows_high, rows_low = split(rows)
        rows_ref[0:128] = rows_high
        rows_ref[128:256] = rows_low

    both = dot(rows_ref[...], high_ref[...], NN)
    total = both[:128] + both[128:] + dot(rows_ref[0:128], low_ref[...], NN)
    out_ref[...] = total.reshape(out_ref.shape)


def update_kernel(index_ref, base_ref, unknown_ref, *refs):
    factor_refs, (out_ref, both_ref) = refs[:4], refs[4:]
    block = pl.program_id(0)

    def subtract(base, first):
        for panel in range(4):
            rows = factor_refs[panel][...].reshape(128, LENGTH)
            if first:
                own = index_ref[0] * 16
                row = lax.broadcasted_iota(jnp.int32, (64, LENGTH), 0)
                col = lax.broadcasted_iota(jnp.int32, (64, LENGTH), 1)
                mine = (row // 16 == panel) & (col == own + row % 16)
                rows = jnp.concatenate([jnp.where(mine, -1.0, 0.0), rows[64:]])
            rows_high, rows_low = split(rows)
            wide = dot(rows_high, both_ref[panel], NT)
            base = base - (wide[:, :128] + wide[:, 128:])
            base = base - dot(rows_low, both_ref[panel, 0:128], NT)
        out_ref[...] = base.reshape(8, 16, 128)

    base = base_ref[...].reshape(128, 128)

    @pl.when(block == 0)
    def _():
        for panel in range(4):
            rows = unknown_ref[:, 16 * panel : 16 * panel + 16, :].reshape(128, LENGTH)
            high, low = split(rows)
            both_ref[panel, 0:128] = high
            both_ref[panel, 128:256] = low
        subtract(jnp.concatenate([jnp.zeros((64, 128), F32), base[64:]]), True)

    @pl.when(block > 0)
    def _():
        subtract(base, False)


def spec(*shape):
    return pl.BlockSpec(shape, lambda *_: (0,) * len(shape))


def block_at(shape, place):
    return pl.BlockSpec(shape, lambda *_: place)


def cost(flops, moved):
    return pl.CostEstimate(flops=flops, bytes_accessed=moved, transcendentals=0)


def shape_of(*shape):
    return jax.ShapeDtypeStruct(shape, F32)


def call(
    body, name, in_specs, out_specs, out_shape, flops, moved, scratch=(), grid=1, room=40
):
    return pl.pallas_call(
        body,
        grid=(grid,),
        in_specs=in_specs,
        out_specs=out_specs,
        out_shape=out_shape,
        scratch_shapes=scratch,
        compiler_params=pltpu.CompilerParams(vmem_limit_bytes=room * 1024 * 1024),
        cost_estimate=cost(flops, moved),
        name=name,
    )


def ring(size, step):
    return [(place, (place + step) % size) for place in range(size)]


def share(partial):
    total = partial + lax.ppermute(partial, "core", ring(2, 1))
    return [total] + [lax.ppermute(total, "x", ring(4, step)) for step in (1, 2, 3)]


def tie(*groups):
    flat = lax.optimization_barrier(tuple(group[at] for group, ats in groups for at in ats))
    flat = list(flat)
    for group, ats in groups:
        for at in ats:
            group[at] = flat.pop(0)


def update(index, base, factor, unknowns):
    return call(
        update_kernel,
        "update",
        [
            SMEM,
            pl.BlockSpec((8, 16, 128), lambda i: (i, 0, 0)),
            spec(8, 64, LENGTH),
        ]
        + [
            pl.BlockSpec((8, 16, LENGTH), lambda i, place=k: (i, 0, place))
            for k in range(4)
        ],
        pl.BlockSpec((8, 16, 128), lambda i: (i, 0, 0)),
        shape_of(32, 16, 128),
        3 * 2 * 512 * 4 * LENGTH * 128,
        11_000_000,
        [pltpu.VMEM((4, 256, LENGTH), BF16)],
        grid=4,
        room=56,
    )(index, base, unknowns, *[factor] * 4)


SMEM = pl.BlockSpec(memory_space=pltpu.SMEM)
ANY = pl.BlockSpec(memory_space=pl.ANY)
NEAR = pl.BlockSpec(memory_space=pltpu.VMEM)
TABLE = pltpu.VMEM((LENGTH, LENGTH), BF16)


def per_device(factor, inverses, right_side, obs_cells, noise, spectrum):
    z_high, z_low = (jnp.asarray(t) for t in halves(z_table()))
    x_high, x_low = (jnp.asarray(t) for t in halves(x_table()))
    back_high, back_low = (jnp.asarray(t) for t in halves(x_table().T))
    wide = lax.axis_index(WIDE).astype(jnp.int32)
    index = jnp.stack([wide, lax.axis_index("y").astype(jnp.int32)])

    columns, side = call(
        columns_kernel,
        "columns",
        [spec(64, LENGTH), spec(4, 16, 128)],
        [spec(8, 64, 128), spec(64, 128)],
        [shape_of(8, 64, 128), shape_of(64, 128)],
        0,
        500_000,
    )(inverses.reshape(64, LENGTH), right_side)
    box = [columns, side, factor]
    tie((box, (0, 1, 2)))
    columns, side, factor = box
    columns = lax.all_to_all(columns, ("x", "core"), 0, 0)
    extra = spectrum[:, :, 0].T.reshape(16, 128)

    lower, lower_far = call(
        lower_kernel,
        "lower",
        [block_at((1, 16, LENGTH * k), (k, 0, 0)) for k in range(1, 4)],
        [spec(32, LENGTH), spec(64, LENGTH)],
        [shape_of(32, LENGTH), shape_of(64, LENGTH)],
        0,
        800_000,
    )(factor, factor, factor)
    lower = lax.all_gather(lower, "z")

    sides = [side] + [lax.ppermute(side, "y", ring(4, step)) for step in (1, 2, 3)]
    quarter = call(
        bundle_kernel,
        "bundle",
        [SMEM, spec(8, 64, 128)] + [spec(64, 128)] * 4 + [spec(16, 128)],
        spec(8, 272, 128),
        shape_of(8, 272, 128),
        0,
        1_500_000,
    )(index, columns, *sides, extra)
    box = [quarter, noise, spectrum, obs_cells, lower_far]
    tie((box, (0, 1, 2, 3, 4)))
    quarter, noise, spectrum, obs_cells, lower_far = box
    lower_far = lax.all_gather(lower_far, "z")
    quarter = lax.all_to_all(quarter, "z", 0, 0)

    slab = call(
        noise_kernel,
        "noise",
        [spec(128, LENGTH)] + [pl.BlockSpec((256, LENGTH), lambda i: (i, 0))] * 2,
        pl.BlockSpec((16, 16, 128), lambda i: (i, 0, 0)),
        shape_of(64, 16, 128),
        3 * 2 * 128 * LENGTH * LENGTH,
        5_000_000,
        grid=4,
    )(noise.reshape(128, LENGTH), z_high, z_low)

    cell_x = (obs_cells // (8 * LENGTH)).reshape(1, 4096)
    plane = obs_cells // LENGTH % 8 - 2 * lax.axis_index("y")
    planes = jnp.stack([plane == 0, plane == 1]).astype(F32)
    freq, phase = z_frequencies(wide, jnp)
    turn = (freq[:, None] * (obs_cells % LENGTH)[None, :] + phase[:, None]) % LENGTH
    waves = jnp.cos(turn.astype(F32) * (2.0 * math.pi / LENGTH))
    box = [quarter, slab, spectrum, cell_x, planes, waves]
    tie((box, tuple(range(6))))
    quarter, slab, spectrum, cell_x, planes, waves = box
    own = quarter[:, 128:224]
    own = [own] + [lax.ppermute(own, "y", ring(4, step)) for step in (1, 2, 3)]
    slab = lax.all_to_all(slab, WIDE, 0, 0)

    obs_specs = lambda k: [
        block_at((1, LENGTH), (0, k)),
        block_at((16, LENGTH), (0, k)),
        block_at((2, LENGTH), (0, k)),
    ]
    side_spec = lambda k: block_at((1, COLS, 128), (k, 0, 0))
    factor_at = {(1, 0): 0, (2, 0): 1, (2, 1): 0, (3, 0): 1, (3, 1): 2, (3, 2): 3}
    factor_spec = lambda k, j: block_at((8, 16, LENGTH), (0, factor_at[k, j], 0))
    factor_rows = lambda k, j: lower_far if k + j > 2 else lower
    inverse_specs = lambda k: [
        block_at((8, 16, 128), (0, a if k == 1 else k + 2 * a, 0)) for a in range(2)
    ] * 4
    inverses = [one for one in range(4) for _ in range(2)]
    inverse_scratch = [pltpu.VMEM((8, 128, 128), BF16)] * 2
    panel_spec = NEAR
    panel_shape = shape_of(COLS, LENGTH)
    pencil_spec = spec(LENGTH, 128)

    partial, sides = call(
        first_kernel,
        "first",
        [block_at((8, 32, 128), (0, 7, 0)), block_at((8, 128, 128), (0, 0, 0))],
        [panel_spec, spec(4, COLS, 128)],
        [panel_shape, shape_of(4, COLS, 128)],
        20_000_000,
        1_200_000,
    )(quarter, quarter)
    box = [partial, spectrum]
    tie((box, (0, 1)))
    partial, spectrum = box
    parts = share(partial)
    even, odd = call(
        spectrum_kernel,
        "spectrum",
        [SMEM, spec(LENGTH, 32), block_at((1, 16, 128), (4, 16, 0))],
        [spec(LENGTH, 128), spec(512, 128)],
        [shape_of(LENGTH, 128), shape_of(512, 128)],
        300_000_000,
        1_500_000,
    )(index, spectrum.reshape(LENGTH, 32), quarter)
    box = [even, odd]
    tie((parts, (0, 1, 2, 3)), (own, (0, 1, 2, 3)), (box, (0, 1)))
    even, odd = box
    unknowns = []
    work = sides
    pencil = slab
    for panel in range(1, 4):
        partial, unknown, *solved_rows = call(
            functools.partial(step_kernel, panel),
            f"step{panel}",
            [SMEM, side_spec(1 if panel == 1 else 0)]
            + [panel_spec] * 4
            + [factor_spec(panel, panel - 1)]
            + inverse_specs(panel)
            + [panel_spec] * 2 * (panel == 3),
            [panel_spec] * 2 + [spec(48, LENGTH)] * (panel == 3),
            [panel_shape] * 2 + [shape_of(48, LENGTH)] * (panel == 3),
            40_000_000,
            1_500_000,
            inverse_scratch,
            room=56 if panel == 1 else 40,
        )(index, work, *parts, factor_rows(panel, panel - 1), *[own[at] for at in inverses], *unknowns * (panel == 3))
        if panel == 1:
            box = [partial, pencil]
            tie((box, (0, 1)))
            partial, pencil = box
        unknowns.append(unknown)
        parts = share(partial)
        later = panel < 3
        box = list(
            call(
                functools.partial(wait_kernel, panel),
                f"wait{panel}",
                obs_specs(panel - 1)
                + [spec(64, 16, 128) if panel == 1 else pencil_spec]
                + [panel_spec] * panel
                + [side_spec(panel + 1)] * later
                + [factor_spec(panel + 1, j) for j in range(panel * later)],
                [pencil_spec] + [spec(1, COLS, 128)] * later,
                [shape_of(LENGTH, 128)] + [shape_of(1, COLS, 128)] * later,
                2 * 2 * 128 * LENGTH * LENGTH,
                1_500_000,
            )(
                cell_x, waves, planes, pencil, *unknowns, *[sides] * later,
                *[factor_rows(panel + 1, j) for j in range(panel * later)],
            )
        )
        tie((parts, (0, 1, 2, 3)), (box, (0, 1) if later else (0,)))
        pencil, work = box[0], box[-1]

    slots = call(
        filter_kernel,
        "filter",
        [spec(LENGTH, 128)]
        + obs_specs(3)
        + [panel_spec] * 4
        + [ANY] * 4
        + [spec(LENGTH, 128), spec(512, 128)],
        spec(64, 16, 128),
        shape_of(64, 16, 128),
        8 * 2 * 128 * LENGTH * LENGTH,
        11_000_000,
        [TABLE] * 4 + [pltpu.SemaphoreType.DMA((4,))],
        room=56,
    )(pencil, cell_x, waves, planes, *parts, x_high, x_low, back_high, back_low, even, odd)
    late = (parts[0][:16] + parts[1][:16]) + (parts[2][:16] + parts[3][:16])
    late = lax.all_gather(jnp.concatenate([solved_rows[0], late]), "z")
    slots = lax.all_to_all(slots, WIDE, 0, 0)
    correction = call(
        close_kernel,
        "close",
        [spec(64, 16, 128)] + [pl.BlockSpec((LENGTH, 256), lambda i: (0, i))] * 2,
        pl.BlockSpec((16, 4, 2, 256), lambda i: (0, 0, 0, i)),
        shape_of(16, 4, 2, LENGTH),
        3 * 2 * 128 * LENGTH * LENGTH,
        5_500_000,
        [pltpu.VMEM((256, LENGTH), BF16)],
        grid=4,
    )(slots, z_high, z_low)
    base, correction = lax.optimization_barrier((right_side, correction))
    solved = update(index, base, factor, late)
    return (solved, correction)


def solution(mesh):
    grid = Mesh(mesh.devices.reshape(8, 4, 2, 4), ("z", "x", "core", "y"))
    return jax.shard_map(
        per_device,
        mesh=grid,
        in_specs=(
            P(None, WIDE, None),
            P(None, None, WIDE, None),
            P(None, WIDE, "y"),
            P(),
            P(WIDE, None, "y", None),
            P(None, "y", WIDE),
        ),
        out_specs=(P(None, WIDE, "y"), P(WIDE, None, "y", None)),
        check_vma=False,
    )
```
